32 devices in a mesh: segment: 2 (over x), dp: 4 (over z), tensor: 4 (over y, core).
Axes of the slice: x: 2, y: 2, z: 4, core: 2. Of those that a mesh axis runs over, the one named last changes fastest.
Arguments:
- hidden_in: bfloat16 [2, 2, 1024, 8192], P('segment', None, ('dp', 'tensor')), may hold values from -600 to 600
- norm_gain: float32 [2, 8192], P('segment'), may hold values from 0.5 to 1.5
- kv_cot: bfloat16 [2, 2, 1024, 1024], P('segment', None, 'dp', 'tensor'), may hold values from -6 to 6
- master_kv: float32 [2, 8192, 1024], P('segment', 'dp', 'tensor'), may hold values from -0.0625 to 0.0625
- moment_m: float32 [2, 8192, 1024], P('segment', 'dp', 'tensor'), may hold values from -128 to 128
- moment_v: float32 [2, 8192, 1024], P('segment', 'dp', 'tensor'), may hold values from 102.4 to 2048
Outputs:
- kv_own: bfloat16 [2, 2, 1024, 1024], P('segment', None, 'dp', 'tensor')
- grad_in: bfloat16 [2, 2, 1024, 8192], P('segment', None, ('dp', 'tensor'))
- master_new: float32 [2, 8192, 1024], P('segment', 'dp', 'tensor')
- kv_next: bfloat16 [2, 2, 1024, 1024], P('segment', None, 'dp', 'tensor')
The draws below stay inside these ranges and needn't reach their ends.
All inputs are finite; a program needn't handle non-finite values.
Results may differ from the reference program's by a relative error of at most 0.012.
Values may be sent and summed in bfloat16 or wider, within the bound.
No kernel may reach another device: no remote copies, remote signals or barrier semaphores. Data moves between devices by JAX's collectives and lax.ppermute only.
A program may use at most 128 MiB of HBM per device.

```python
import math
import jax
import jax.numpy as jnp
from jax import lax

D = 8192
MICRO = 2
KVW = 1024
TOKENS = 1024
SEGMENTS = 2
N_TENSOR = 4


def draw_hidden_in(key, part):
    key = jax.random.fold_in(key, 7)
    key_base, key_rows, key_cols = jax.random.split(key, 3)
    shape = (SEGMENTS, MICRO, TOKENS, D)
    row_scale = jnp.exp(jax.random.uniform(key_rows, (SEGMENTS, MICRO, TOKENS, 1), jnp.float32, 0.0, math.log(10.0)))
    col_scale = jnp.exp(jax.random.uniform(key_cols, (SEGMENTS, 1, 1, D), jnp.float32, 0.0, math.log(10.0)))
    base = jnp.clip(jax.random.normal(key_base, shape, jnp.float32), -6.0, 6.0)
    return (base * row_scale * col_scale).astype(jnp.bfloat16)


def shard_levels(rng, extent, cuts, smallest, high):
    level, own = 1.0, jax.random.fold_in(rng, 6)
    for position, shards_of in cuts:
        draws = jnp.exp(jax.random.uniform(jax.random.fold_in(own, position), (shards_of,), jnp.float32, smallest / len(cuts), high / len(cuts)))
        level = level * jnp.repeat(draws, extent[position] // shards_of).reshape([-1 if axis == position else 1 for axis in range(len(extent))])
    return level


def normal_values(stream_key, shape, scale, limit, cuts=(), dtype=jnp.bfloat16):
    factor_of = shard_levels(stream_key, shape, cuts, -0.22, 0.18) if cuts else 1.0
    result = jax.random.normal(stream_key, shape, jnp.float32) * scale * factor_of
    return jnp.minimum(jnp.maximum(result, -limit), limit).astype(dtype)


def setup_inputs(seed: int = 0) -> dict:
    key_of = jax.random.split(jax.random.key(seed), 7)
    return {
        "hidden_in": draw_hidden_in(jax.random.fold_in(key_of[6], 71), 0),
        "norm_gain": jnp.clip(1.0 + 0.1 * jax.random.normal(key_of[1], (SEGMENTS, D), jnp.float32), 0.5, 1.5),
        "kv_cot": normal_values(key_of[2], (SEGMENTS, MICRO, TOKENS, KVW), 1.0, 6.0, ((0, 2), (2, 4), (3, 4))),
        "master_kv": normal_values(key_of[3], (SEGMENTS, D, KVW), D ** -0.5, 0.0625, ((0, 2), (1, 4), (2, 4)), jnp.float32),
        "moment_m": normal_values(key_of[4], (SEGMENTS, D, KVW), (0.5 * (MICRO * TOKENS) ** 0.5), 128.0, ((0, 2), (1, 4), (2, 4)), jnp.float32),
        "moment_v": jnp.clip(jnp.exp(math.log(2048.0) - 2.9957323 * jax.random.uniform(key_of[5], (SEGMENTS, D, KVW), jnp.float32) ** shard_levels(key_of[5], (SEGMENTS, D, KVW), ((0, 2), (1, 4), (2, 4)), -0.2, 0.2)), 102.4, 2048.0),
    }


beta_first = 0.9
beta_second = 0.95
learn_rate = 0.03
weight_decay = 0.1
adam_eps = 1e-08
norm_eps = 1e-05
step_count = 20.0

def normalize(hidden, gain):
    widened = hidden.astype(jnp.float32)
    scaling = lax.rsqrt(lax.optimization_barrier(jnp.mean(widened * widened, axis=-1, keepdims=True)) + norm_eps)
    return ((widened * scaling * gain).astype(jnp.bfloat16), scaling)

def one_segment(inputs):
    hidden, gain, cotangent, master, first_moment, second_moment = inputs
    normed, scaling = normalize(hidden, gain)
    weights_bf = master.astype(jnp.bfloat16)
    normed_wide = normed.astype(jnp.float32)
    weights_wide = weights_bf.astype(jnp.float32)
    cot_wide = cotangent.astype(jnp.float32)
    keys_values = jnp.einsum('mrd,dc->mrc', normed_wide, weights_wide).astype(jnp.bfloat16)
    grad_w = jnp.einsum('mrd,mrc->dc', normed_wide, cot_wide)
    block = KVW // N_TENSOR
    d_normed = jnp.zeros(normed.shape, jnp.float32)
    for index in range(N_TENSOR):
        partial_value = jnp.einsum('mrc,dc->mrd', cot_wide[:, :, index * block:(index + 1) * block], weights_wide[:, index * block:(index + 1) * block])
        rounded = lax.optimization_barrier(partial_value.astype(jnp.bfloat16))
        d_normed = d_normed + rounded.astype(jnp.float32)
    widened = hidden.astype(jnp.float32)
    upper = d_normed * gain
    grad_in = (scaling * upper - widened * scaling ** 3 * lax.optimization_barrier(jnp.mean(upper * widened, axis=-1, keepdims=True))).astype(jnp.bfloat16)
    m_new = beta_first * first_moment + (1.0 - beta_first) * grad_w
    v_new = beta_second * second_moment + (1.0 - beta_second) * grad_w * grad_w
    m_hat = m_new / (1.0 - beta_first ** step_count)
    v_hat = v_new / (1.0 - beta_second ** step_count)
    master_new = master - learn_rate * (m_hat / (jnp.sqrt(v_hat) + adam_eps) + weight_decay * master)
    return (keys_values, grad_in, master_new, normed)

def successor_keys(inputs):
    normed, master = inputs
    return jnp.einsum('mrd,dc->mrc', normed.astype(jnp.float32), master.astype(jnp.bfloat16).astype(jnp.float32)).astype(jnp.bfloat16)

def reference(hidden_in, norm_gain, kv_cot, master_kv, moment_m, moment_v):
    kv_own, grad_in, master_new, normed = lax.map(one_segment, (hidden_in, norm_gain, kv_cot, master_kv, moment_m, moment_v))
    next_normed = jnp.roll(normed, -1, axis=0)
    next_master = jnp.roll(master_new, -1, axis=0)
    kv_next = lax.map(successor_keys, (next_normed, next_master))
    return (kv_own, grad_in, master_new, kv_next)
```

```python
import jax
import jax.numpy as jnp
from jax import lax
from jax.sharding import PartitionSpec as P

beta_first = 0.9
beta_second = 0.95
learn_rate = 0.03
weight_decay = 0.1
adam_eps = 1e-08
norm_eps = 1e-05
step_count = 20.0

f32 = jnp.float32
bf16 = jnp.bfloat16


def swap(x, axis, bits):
    peers = lax.axis_size(axis)
    return lax.ppermute(x, axis, [(i, i ^ bits) for i in range(peers)])


def from_behind(x, axis, by):
    peers = lax.axis_size(axis)
    return lax.ppermute(x, axis, [(i, (i + by) % peers) for i in range(peers)])


def dot(a, b, contract):
    return lax.dot_general(a, b, (contract, ((), ())), preferred_element_type=f32)


def reorder(blocks, me):
    bit = 1
    while bit < len(blocks):
        flip = (me & bit) != 0
        blocks = [jnp.where(flip, blocks[i ^ bit], blocks[i]) for i in range(len(blocks))]
        bit *= 2
    return blocks


def scatter_sum(parts):
    r1 = swap(parts[1], "dp", 1)
    r3 = swap(parts[3], "dp", 1)
    mine = parts[0].astype(f32) + r1.astype(f32)
    other = (parts[2].astype(f32) + r3.astype(f32)).astype(bf16)
    return mine + swap(other, "dp", 2).astype(f32)


def shards(hidden_in, norm_gain, kv_cot, master_kv, moment_m, moment_v):
    dp, tensor = lax.axis_size("dp"), lax.axis_size("tensor")
    z, t = lax.axis_index("dp"), lax.axis_index("tensor")
    gain_row = norm_gain[0]
    widened = hidden_in[0].astype(f32)
    micro, rows, width = widened.shape
    depth = width // dp
    cols = kv_cot.shape[-1]
    scaling = lax.rsqrt(jnp.mean(widened * widened, axis=-1, keepdims=True) + norm_eps)
    normed = (widened * scaling * gain_row).astype(bf16)

    def feature_block(x, k):
        return lax.dynamic_slice_in_dim(x, (z ^ k) * depth, depth, x.ndim - 1)

    own = [feature_block(normed, k).reshape(micro * rows, depth) for k in range(dp)]
    pieces = [own[0]] + [swap(own[k], "dp", k) for k in range(1, dp)]
    cot = kv_cot[0].reshape(micro, tensor, rows, cols)
    cot = jnp.stack(
        [
            lax.dynamic_slice_in_dim(cot, t ^ j, 1, 1).reshape(micro * rows, cols)
            for j in range(tensor)
        ]
    )
    cot2 = swap(cot, "dp", 2)
    cots = [cot, swap(cot, "dp", 1), cot2, swap(cot2, "dp", 1)]
    weights = master_kv[0].astype(bf16)
    w2 = swap(weights, "tensor", 2)
    whole_w = jnp.concatenate([weights, swap(weights, "tensor", 1), w2, swap(w2, "tensor", 1)], 1)
    gathered = []
    for piece in pieces:
        across = swap(piece, "tensor", 2)
        gathered += [piece, swap(piece, "tensor", 1), across, swap(across, "tensor", 1)]
    tokens = jnp.concatenate(gathered)
    cot_all = jnp.concatenate(cots).reshape(-1, cols)
    block = tensor * micro * rows

    def by_replica(x):
        return [x[k * block : (k + 1) * block] for k in range(dp)]

    def place(x):
        x = x.reshape(tensor, micro, rows, cols)
        return jnp.stack(reorder([x[j] for j in range(tensor)], t), 1).reshape(
            1, micro, tensor * rows, cols
        )

    kv_part = dot(tokens, weights, ((1,), (0,))).astype(bf16)
    kv_own = place(scatter_sum(by_replica(kv_part)).astype(bf16))

    mine_cot = []
    for j in range(tensor):
        rows_j = jnp.concatenate([c[j] for c in cots])
        mine_cot.append(rows_j if j == 0 else swap(rows_j, "tensor", j))
    d_part = dot(jnp.concatenate(mine_cot, 1), whole_w, ((1,), (1,))).astype(bf16)
    d_part = d_part.reshape(dp, micro, rows, depth)
    d_blocks = [d_part[0]] + [swap(d_part[k], "dp", k) for k in range(1, dp)]
    d_normed = jnp.concatenate(reorder(d_blocks, z), -1).astype(f32)
    upper = d_normed * gain_row
    grad_in = (
        scaling * upper - widened * scaling**3 * jnp.mean(upper * widened, axis=-1, keepdims=True)
    ).astype(bf16)

    grad_w = dot(tokens, cot_all, ((0,), (0,)))
    master = master_kv[0]
    m_new = beta_first * moment_m[0] + (1.0 - beta_first) * grad_w
    v_new = beta_second * moment_v[0] + (1.0 - beta_second) * grad_w * grad_w
    m_hat = m_new / (1.0 - beta_first**step_count)
    v_hat = v_new / (1.0 - beta_second**step_count)
    master_new = master - learn_rate * (
        m_hat / (jnp.sqrt(v_hat) + adam_eps) + weight_decay * master
    )
    updated = master_new.astype(bf16)
    next_part = dot(tokens, updated, ((1,), (0,))).astype(bf16)
    mine = place(scatter_sum(by_replica(next_part)).astype(bf16))
    kv_next = from_behind(mine, "segment", -1)
    return (kv_own, grad_in[None], master_new[None], kv_next)


def solution(mesh):
    in_specs = (
        P("segment", None, ("dp", "tensor"), None),
        P("segment", None),
        P("segment", None, "dp", "tensor"),
        P("segment", "dp", "tensor"),
        P("segment", "dp", "tensor"),
        P("segment", "dp", "tensor"),
    )
    out_specs = (
        P("segment", None, "dp", "tensor"),
        P("segment", None, ("dp", "tensor"), None),
        P("segment", "dp", "tensor"),
        P("segment", None, "dp", "tensor"),
    )
    return jax.shard_map(shards, mesh=mesh, in_specs=in_specs, out_specs=out_specs, check_vma=False)
```

```python
import jax
import jax.numpy as jnp
from jax import lax
from jax.experimental import pallas as pl
from jax.sharding import PartitionSpec as P

beta_first = 0.9
beta_second = 0.95
learn_rate = 0.03
weight_decay = 0.1
adam_eps = 1e-08
norm_eps = 1e-05
step_count = 20.0

f32 = jnp.float32
bf16 = jnp.bfloat16


def swap(x, axis, bits):
    peers = lax.axis_size(axis)
    return lax.ppermute(x, axis, [(i, i ^ bits) for i in range(peers)])


def after(x, *earlier):
    hbm = pl.BlockSpec(memory_space=pl.ANY)
    return pl.pallas_call(
        lambda *refs: None,
        out_shape=jax.ShapeDtypeStruct(x.shape, x.dtype),
        in_specs=[hbm] * (1 + len(earlier)),
        out_specs=hbm,
        input_output_aliases={0: 0},
        name="after",
    )(x, *earlier)


def from_behind(x, axis, by):
    peers = lax.axis_size(axis)
    return lax.ppermute(x, axis, [(i, (i + by) % peers) for i in range(peers)])


def dot(a, b, contract):
    return lax.dot_general(a, b, (contract, ((), ())), preferred_element_type=f32)


def reorder(blocks, me):
    bit = 1
    while bit < len(blocks):
        flip = (me & bit) != 0
        blocks = [jnp.where(flip, blocks[i ^ bit], blocks[i]) for i in range(len(blocks))]
        bit *= 2
    return blocks


def scatter_sum(parts):
    r1 = swap(parts[1], "dp", 1)
    r3 = swap(parts[3], "dp", 1)
    mine = parts[0].astype(f32) + r1.astype(f32)
    other = (parts[2].astype(f32) + r3.astype(f32)).astype(bf16)
    return mine + swap(other, "dp", 2).astype(f32)


def shards(hidden_in, norm_gain, kv_cot, master_kv, moment_m, moment_v):
    dp, tensor = lax.axis_size("dp"), lax.axis_size("tensor")
    z, t = lax.axis_index("dp"), lax.axis_index("tensor")
    gain_row = norm_gain[0]
    widened = hidden_in[0].astype(f32)
    micro, rows, width = widened.shape
    depth = width // dp
    cols = kv_cot.shape[-1]
    scaling = lax.rsqrt(jnp.mean(widened * widened, axis=-1, keepdims=True) + norm_eps)
    normed = (widened * scaling * gain_row).astype(bf16)

    def feature_block(x, k):
        return lax.dynamic_slice_in_dim(x, (z ^ k) * depth, depth, x.ndim - 1)

    weights = master_kv[0].astype(bf16)
    cot = kv_cot[0].reshape(micro, tensor, rows, cols)
    cot = jnp.stack(
        [
            lax.dynamic_slice_in_dim(cot, t ^ j, 1, 1).reshape(micro * rows, cols)
            for j in range(tensor)
        ]
    )
    w2 = swap(weights, "tensor", 2)
    cot2 = swap(cot, "dp", 2)
    own = [feature_block(normed, k).reshape(micro * rows, depth) for k in range(dp)]
    pieces = [own[0]] + [swap(own[k], "dp", k) for k in range(1, dp)]
    pair = swap(jnp.stack([cot, cot2]), "dp", 1)
    cots = [cot, pair[0], cot2, pair[1]]
    w13 = swap(jnp.concatenate([weights, w2], 1), "tensor", 1)
    whole_w = jnp.concatenate([weights, w2, w13], 1)
    cot_order = (0, 2, 1, 3)
    gathered = []
    for piece in pieces:
        near = jnp.concatenate([piece, swap(piece, "tensor", 2)])
        gathered += [near, swap(near, "tensor", 1)]
    tokens = jnp.concatenate(gathered)
    cot_all = jnp.concatenate([c[j] for c in cots for j in cot_order])
    block = tensor * micro * rows

    def by_replica(x):
        return [x[k * block : (k + 1) * block] for k in range(dp)]

    def place(x):
        x = x.reshape(tensor, micro, rows, cols)
        return jnp.stack(reorder([x[j] for j in (0, 2, 1, 3)], t), 1).reshape(
            1, micro, tensor * rows, cols
        )

    kv_part = dot(tokens, weights, ((1,), (0,))).astype(bf16)
    kv_own = place(scatter_sum(by_replica(kv_part)).astype(bf16))

    mine_cot = []
    for j in cot_order:
        rows_j = jnp.concatenate([c[j] for c in cots])
        mine_cot.append(rows_j if j == 0 else swap(rows_j, "tensor", j))
    d_part = dot(after(jnp.concatenate(mine_cot, 1), pieces[1], pieces[2], pieces[3]), whole_w, ((1,), (1,))).astype(bf16)
    d_part = d_part.reshape(dp, micro, rows, depth)
    d_blocks = [d_part[0]] + [swap(d_part[k], "dp", k) for k in range(1, dp)]
    d_normed = jnp.concatenate(reorder(d_blocks, z), -1).astype(f32)
    upper = d_normed * gain_row
    grad_in = (
        scaling * upper - widened * scaling**3 * jnp.mean(upper * widened, axis=-1, keepdims=True)
    ).astype(bf16)

    grad_w = dot(tokens, after(cot_all, d_part), ((0,), (0,)))
    master = master_kv[0]
    m_new = beta_first * moment_m[0] + (1.0 - beta_first) * grad_w
    v_new = beta_second * moment_v[0] + (1.0 - beta_second) * grad_w * grad_w
    m_hat = m_new / (1.0 - beta_first**step_count)
    v_hat = v_new / (1.0 - beta_second**step_count)
    master_new = master - learn_rate * (
        m_hat / (jnp.sqrt(v_hat) + adam_eps) + weight_decay * master
    )
    updated = master_new.astype(bf16)
    next_part = dot(tokens, updated, ((1,), (0,))).astype(bf16)
    mine = place(scatter_sum(by_replica(next_part)).astype(bf16))
    kv_next = from_behind(mine, "segment", -1)
    return (kv_own, grad_in[None], master_new[None], kv_next)


def solution(mesh):
    in_specs = (
        P("segment", None, ("dp", "tensor"), None),
        P("segment", None),
        P("segment", None, "dp", "tensor"),
        P("segment", "dp", "tensor"),
        P("segment", "dp", "tensor"),
        P("segment", "dp", "tensor"),
    )
    out_specs = (
        P("segment", None, "dp", "tensor"),
        P("segment", None, ("dp", "tensor"), None),
        P("segment", "dp", "tensor"),
        P("segment", None, "dp", "tensor"),
    )
    return jax.shard_map(shards, mesh=mesh, in_specs=in_specs, out_specs=out_specs, check_vma=False)
```

```python
import functools

import jax
import jax.numpy as jnp
from jax import lax
from jax.experimental import pallas as pl
from jax.experimental.pallas import tpu as pltpu
from jax.sharding import PartitionSpec as P

beta_first = 0.9
beta_second = 0.95
learn_rate = 0.03
weight_decay = 0.1
adam_eps = 1e-08
norm_eps = 1e-05
step_count = 20.0

f32 = jnp.float32
bf16 = jnp.bfloat16


def swap(x, axis, bits):
    peers = lax.axis_size(axis)
    return lax.ppermute(x, axis, [(i, i ^ bits) for i in range(peers)])


def mark(x):
    return x[tuple(slice(0, 1) for _ in x.shape[:-2])][..., :16, :128]


def after(values, *earlier):
    hbm = pl.BlockSpec(memory_space=pl.ANY)
    marks = [mark(e) for e in earlier]
    tied = pl.pallas_call(
        lambda *refs: None,
        out_shape=[jax.ShapeDtypeStruct(x.shape, x.dtype) for x in values],
        in_specs=[hbm] * (len(values) + len(marks)),
        out_specs=[hbm] * len(values),
        input_output_aliases={i: i for i in range(len(values))},
        name="after",
    )(*values, *marks)
    return list(tied)


def from_behind(x, axis, by):
    peers = lax.axis_size(axis)
    return lax.ppermute(x, axis, [(i, (i + by) % peers) for i in range(peers)])


def dot(a, b, contract):
    return lax.dot_general(a, b, (contract, ((), ())), preferred_element_type=f32)


def reorder(blocks, me):
    bit = 1
    while bit < len(blocks):
        flip = (me & bit) != 0
        blocks = [jnp.where(flip, blocks[i ^ bit], blocks[i]) for i in range(len(blocks))]
        bit *= 2
    return blocks


def scatter_sum(keep, send):
    got = swap(send, "dp", 1)
    mine = keep[0].astype(f32) + got[0].astype(f32)
    other = (keep[1].astype(f32) + got[1].astype(f32)).astype(bf16)
    return mine + swap(other, "dp", 2).astype(f32), other


def update_kernel(mark_ref, cot_ref, master_ref, m_ref, v_ref, *rest, layout, tile):
    count = len(layout)
    token_refs, (new_ref, keep_ref, send_ref, updated_ref) = rest[:count], rest[count:]
    starts = [sum(x.shape[0] for x in token_refs[:p]) for p in range(count)]

    @pl.loop(0, master_ref.shape[0] // tile)
    def _(i):
        at = pl.ds(pl.multiple_of(i * tile, tile), tile)
        grad = sum(
            dot(cot_ref[:, start : start + x.shape[0]], x[:, at], ((1,), (0,)))
            for start, x in zip(starts, token_refs)
        ).T
        m_new = beta_first * m_ref[at, :] + (1.0 - beta_first) * grad
        v_new = beta_second * v_ref[at, :] + (1.0 - beta_second) * grad * grad
        m_hat = m_new / (1.0 - beta_first**step_count)
        v_hat = v_new / (1.0 - beta_second**step_count)
        master = master_ref[at, :]
        master_new = master - learn_rate * (
            m_hat / (jnp.sqrt(v_hat) + adam_eps) + weight_decay * master
        )
        new_ref[at, :] = master_new
        updated_ref[at, :] = master_new.astype(bf16)

    project(layout, token_refs, updated_ref, keep_ref, send_ref)


def project(layout, token_refs, weights_ref, keep_ref, send_ref):
    for (first, side, replicas), token_ref in zip(layout, token_refs):
        height = token_ref.shape[0] // replicas
        for i in range(replicas):
            k = first + i
            part_ref = send_ref if k % 2 else keep_ref
            part_ref[k // 2, side * height : (side + 1) * height, :] = dot(
                token_ref[i * height : (i + 1) * height, :], weights_ref[...], ((1,), (0,))
            ).astype(bf16)


def project_kernel(mark_ref, weights_ref, *rest, layout):
    project(layout, rest[: len(layout)], weights_ref, *rest[len(layout) :])


vmem = pl.BlockSpec(memory_space=pltpu.VMEM)
anywhere = pl.BlockSpec(memory_space=pl.ANY)
params = pltpu.CompilerParams(vmem_limit_bytes=28 * 1024 * 1024)
light = pl.CostEstimate(flops=1000, bytes_accessed=1000, transcendentals=0)


def shards(hidden_in, norm_gain, kv_cot, master_kv, moment_m, moment_v):
    dp, tensor = lax.axis_size("dp"), lax.axis_size("tensor")
    z, t = lax.axis_index("dp"), lax.axis_index("tensor")
    gain_row = norm_gain[0]
    widened = hidden_in[0].astype(f32)
    micro, rows, width = widened.shape
    depth = width // dp
    cols = kv_cot.shape[-1]
    scaling = lax.rsqrt(jnp.mean(widened * widened, axis=-1, keepdims=True) + norm_eps)
    normed = (widened * scaling * gain_row).astype(bf16)

    def feature_block(x, k):
        return lax.dynamic_slice_in_dim(x, (z ^ k) * depth, depth, x.ndim - 1)

    weights = master_kv[0].astype(bf16)
    blocks = kv_cot[0].reshape(micro, tensor, rows, cols)
    blocks = [
        lax.dynamic_slice_in_dim(blocks, t ^ j, 1, 1).reshape(micro * rows, cols)
        for j in range(tensor)
    ]
    order = (0, 2, 1, 3)
    cot = jnp.concatenate([blocks[0]] + [swap(blocks[j], "tensor", j) for j in order[1:]], 1)
    w2 = swap(weights, "tensor", 2)
    cot2 = swap(cot, "dp", 2)
    own = [feature_block(normed, k).reshape(micro * rows, depth) for k in range(dp)]
    own[1], own[3] = after([own[1], own[3]], cot2)
    piece1, piece3 = swap(own[1], "dp", 1), swap(own[3], "dp", 3)
    pair = swap(jnp.stack([cot, cot2]), "dp", 1)
    cots = [cot, pair[0], cot2, pair[1]]
    own[0], w2 = after([own[0], w2], w2)
    across0 = swap(own[0], "tensor", 2)
    w13 = swap(jnp.concatenate([weights, w2], 1), "tensor", 1)
    theirs = [
        jnp.stack([c[:, order.index(j) * cols : (order.index(j) + 1) * cols] for c in cots[1:]])
        for j in range(tensor)
    ]
    whole_w = jnp.concatenate([weights, w2, w13], 1)
    d_part = dot(jnp.concatenate(cots), whole_w, ((1,), (1,))).astype(bf16)
    d_part = d_part.reshape(dp, micro * rows, depth)
    d_send = [d_part[k] for k in range(dp)]
    piece1, piece3, own[2], across0, far_cot = after(
        [piece1, piece3, own[2], across0, jnp.concatenate(theirs[2:])], d_send[1]
    )
    piece2 = swap(own[2], "dp", 2)
    across1, across3 = swap(piece1, "tensor", 2), swap(piece3, "tensor", 2)
    got = swap(far_cot, "tensor", 2)
    got2, got3 = got[: dp - 1], got[dp - 1 :]
    near_rows = swap(jnp.concatenate([theirs[1], got3]), "tensor", 1)
    got1, got3 = near_rows[: dp - 1], near_rows[dp - 1 :]
    rows_of = [jnp.concatenate([blocks[j][None], x]) for j, x in enumerate((theirs[0], got1, got2, got3))]
    near01 = jnp.concatenate([own[0], across0, piece1, across1])
    piece2, d_send[2] = after([piece2, d_send[2]], across1, across3)
    across2 = swap(piece2, "tensor", 2)
    d_recv = [d_send[0], None, swap(d_send[2], "dp", 2), None]
    far01 = swap(near01, "tensor", 1)
    near3 = jnp.concatenate([piece3, across3])
    far3 = swap(near3, "tensor", 1)
    across2, d_send[1], d_send[3] = after([across2, d_send[1], d_send[3]], d_recv[2])
    near2 = jnp.concatenate([piece2, across2])
    far2 = swap(near2, "tensor", 1)
    d_recv[1], d_recv[3] = swap(d_send[1], "dp", 1), swap(d_send[3], "dp", 3)
    tokens = [near01, far01, near2, far2, near3, far3]
    layout = ((0, 0, 2), (0, 1, 2), (2, 0, 1), (2, 1, 1), (3, 0, 1), (3, 1, 1))
    cot_all = jnp.concatenate(
        [
            rows_of[j + side][k]
            for first, side, replicas in layout
            for k in range(first, first + replicas)
            for j in (0, 2)
        ]
    ).T
    block = tensor * micro * rows

    def place(x):
        x = x.reshape(tensor, micro, rows, cols)
        return jnp.stack(reorder([x[j] for j in order], t), 1).reshape(
            1, micro, tensor * rows, cols
        )

    own_depth = master_kv.shape[1]
    part_shape = [jax.ShapeDtypeStruct((dp // 2, block, cols), bf16)] * 2
    count = len(tokens)
    master_new, keep, send = pl.pallas_call(
        functools.partial(update_kernel, layout=layout, tile=min(own_depth, 256)),
        out_shape=[jax.ShapeDtypeStruct((own_depth, cols), f32)] + part_shape,
        in_specs=[anywhere] + [vmem] * (4 + count),
        out_specs=[vmem] * 3,
        scratch_shapes=[pltpu.VMEM((own_depth, cols), bf16)],
        compiler_params=params,
        cost_estimate=light,
        name="update",
    )(mark(d_send[3]), cot_all, master_kv[0], moment_m[0], moment_v[0], *tokens)
    total, other = scatter_sum(keep, send)
    mine = place(total.astype(bf16))
    kv_next = from_behind(mine, "segment", -1)
    own_keep, own_send = pl.pallas_call(
        functools.partial(project_kernel, layout=layout),
        out_shape=part_shape,
        in_specs=[anywhere] + [vmem] * (1 + count),
        out_specs=[vmem] * 2,
        compiler_params=params,
        cost_estimate=light,
        name="project",
    )(mark(send), weights, *tokens)
    kv_own = place(scatter_sum(own_keep, own_send)[0].astype(bf16))

    d_recv[1], d_recv[3] = after([d_recv[1], d_recv[3]], own_send, other)
    d_normed = jnp.concatenate(reorder(d_recv, z), -1).astype(f32).reshape(widened.shape)
    upper = d_normed * gain_row
    grad_in = (
        scaling * upper - widened * scaling**3 * jnp.mean(upper * widened, axis=-1, keepdims=True)
    ).astype(bf16)

    return (kv_own, grad_in[None], master_new[None], kv_next)


def solution(mesh):
    in_specs = (
        P("segment", None, ("dp", "tensor"), None),
        P("segment", None),
        P("segment", None, "dp", "tensor"),
        P("segment", "dp", "tensor"),
        P("segment", "dp", "tensor"),
        P("segment", "dp", "tensor"),
    )
    out_specs = (
        P("segment", None, "dp", "tensor"),
        P("segment", None, ("dp", "tensor"), None),
        P("segment", "dp", "tensor"),
        P("segment", None, "dp", "tensor"),
    )
    return jax.shard_map(shards, mesh=mesh, in_specs=in_specs, out_specs=out_specs, check_vma=False)
```

```python
import functools

import jax
import jax.numpy as jnp
from jax import lax
from jax.experimental import pallas as pl
from jax.experimental.pallas import tpu as pltpu
from jax.sharding import PartitionSpec as P

beta_first = 0.9
beta_second = 0.95
learn_rate = 0.03
weight_decay = 0.1
adam_eps = 1e-08
norm_eps = 1e-05
step_count = 20.0

f32 = jnp.float32
bf16 = jnp.bfloat16


def swap(x, axis, bits):
    peers = lax.axis_size(axis)
    return lax.ppermute(x, axis, [(i, i ^ bits) for i in range(peers)])


def mark(x):
    return x[tuple(slice(0, 1) for _ in x.shape[:-2])][..., :16, :128]


def after(values, *earlier):
    hbm = pl.BlockSpec(memory_space=pl.ANY)
    marks = [mark(e) for e in earlier]
    tied = pl.pallas_call(
        lambda *refs: None,
        out_shape=[jax.ShapeDtypeStruct(x.shape, x.dtype) for x in values],
        in_specs=[hbm] * (len(values) + len(marks)),
        out_specs=[hbm] * len(values),
        input_output_aliases={i: i for i in range(len(values))},
        compiler_params=pltpu.CompilerParams(vmem_limit_bytes=256 * 1024),
        cost_estimate=light,
        name="after",
    )(*values, *marks)
    return list(tied)


def from_behind(x, axis, by):
    peers = lax.axis_size(axis)
    return lax.ppermute(x, axis, [(i, (i + by) % peers) for i in range(peers)])


def dot(a, b, contract):
    return lax.dot_general(a, b, (contract, ((), ())), preferred_element_type=f32)


def reorder(blocks, me):
    bit = 1
    while bit < len(blocks):
        flip = (me & bit) != 0
        blocks = [jnp.where(flip, blocks[i ^ bit], blocks[i]) for i in range(len(blocks))]
        bit *= 2
    return blocks


def scatter_sum(keep, send):
    got = swap(send, "dp", 1)
    mine = keep[0].astype(f32) + got[0].astype(f32)
    other = (keep[1].astype(f32) + got[1].astype(f32)).astype(bf16)
    return mine + swap(other, "dp", 2).astype(f32), other


def update_kernel(mark_ref, cot_ref, master_ref, m_ref, v_ref, *rest, layout, tile):
    count = len(layout)
    token_refs, (new_ref, keep_ref, send_ref, updated_ref) = rest[:count], rest[count:]
    starts = [sum(x.shape[0] for x in token_refs[:p]) for p in range(count)]

    @pl.loop(0, master_ref.shape[0] // tile)
    def _(i):
        at = pl.ds(pl.multiple_of(i * tile, tile), tile)
        grad = sum(
            dot(cot_ref[:, start : start + x.shape[0]], x[:, at], ((1,), (0,)))
            for start, x in zip(starts, token_refs)
        ).T
        m_new = beta_first * m_ref[at, :] + (1.0 - beta_first) * grad
        v_new = beta_second * v_ref[at, :] + (1.0 - beta_second) * grad * grad
        m_hat = m_new / (1.0 - beta_first**step_count)
        v_hat = v_new / (1.0 - beta_second**step_count)
        master = master_ref[at, :]
        master_new = master - learn_rate * (
            m_hat / (jnp.sqrt(v_hat) + adam_eps) + weight_decay * master
        )
        new_ref[at, :] = master_new
        updated_ref[at, :] = master_new.astype(bf16)

    project(layout, token_refs, updated_ref, keep_ref, send_ref)


def project(layout, token_refs, weights_ref, keep_ref, send_ref):
    for (first, side, replicas), token_ref in zip(layout, token_refs):
        height = token_ref.shape[0] // replicas
        for i in range(replicas):
            k = first + i
            part_ref = send_ref if k % 2 else keep_ref
            part_ref[k // 2, side * height : (side + 1) * height, :] = dot(
                token_ref[i * height : (i + 1) * height, :], weights_ref[...], ((1,), (0,))
            ).astype(bf16)


def project_kernel(mark_ref, weights_ref, *rest, layout):
    project(layout, rest[: len(layout)], weights_ref, *rest[len(layout) :])


vmem = pl.BlockSpec(memory_space=pltpu.VMEM)
anywhere = pl.BlockSpec(memory_space=pl.ANY)
params = pltpu.CompilerParams(vmem_limit_bytes=24 * 1024 * 1024)
light = pl.CostEstimate(flops=1000, bytes_accessed=1000, transcendentals=0)


def shards(hidden_in, norm_gain, kv_cot, master_kv, moment_m, moment_v):
    dp, tensor = lax.axis_size("dp"), lax.axis_size("tensor")
    z, t = lax.axis_index("dp"), lax.axis_index("tensor")
    gain_row = norm_gain[0]
    widened = hidden_in[0].astype(f32)
    micro, rows, width = widened.shape
    depth = width // dp
    cols = kv_cot.shape[-1]
    scaling = lax.rsqrt(jnp.mean(widened * widened, axis=-1, keepdims=True) + norm_eps)
    normed = (widened * scaling * gain_row).astype(bf16)

    def feature_block(x, k):
        return lax.dynamic_slice_in_dim(x, (z ^ k) * depth, depth, x.ndim - 1)

    weights = master_kv[0].astype(bf16)
    blocks = kv_cot[0].reshape(micro, tensor, rows, cols)
    blocks = [
        lax.dynamic_slice_in_dim(blocks, t ^ j, 1, 1).reshape(micro * rows, cols)
        for j in range(tensor)
    ]
    order = (0, 2, 1, 3)
    cot = jnp.concatenate([blocks[0]] + [swap(blocks[j], "tensor", j) for j in order[1:]], 1)
    w2 = swap(weights, "tensor", 2)
    cot2 = swap(cot, "dp", 2)
    own = [feature_block(normed, k).reshape(micro * rows, depth) for k in range(dp)]
    own[1], own[3] = after([own[1], own[3]], cot2)
    piece1, piece3 = swap(own[1], "dp", 1), swap(own[3], "dp", 3)
    pair = swap(jnp.stack([cot, cot2]), "dp", 1)
    cots = [cot, pair[0], cot2, pair[1]]
    own[0], w2 = after([own[0], w2], w2)
    across0 = swap(own[0], "tensor", 2)
    w13 = swap(jnp.concatenate([weights, w2], 1), "tensor", 1)
    theirs = [
        jnp.stack([c[:, order.index(j) * cols : (order.index(j) + 1) * cols] for c in cots[1:]])
        for j in range(tensor)
    ]
    whole_w = jnp.concatenate([weights, w2, w13], 1)
    d_part = dot(jnp.concatenate(cots), whole_w, ((1,), (1,))).astype(bf16)
    d_part = d_part.reshape(dp, micro * rows, depth)
    d_send = [d_part[k] for k in range(dp)]
    piece1, piece3, own[2], across0, far_cot = after(
        [piece1, piece3, own[2], across0, jnp.concatenate(theirs[2:])], d_send[1]
    )
    piece2 = swap(own[2], "dp", 2)
    across1, across3 = swap(piece1, "tensor", 2), swap(piece3, "tensor", 2)
    got = swap(far_cot, "tensor", 2)
    got2, got3 = got[: dp - 1], got[dp - 1 :]
    near_rows = swap(jnp.concatenate([theirs[1], got3]), "tensor", 1)
    got1, got3 = near_rows[: dp - 1], near_rows[dp - 1 :]
    rows_of = [jnp.concatenate([blocks[j][None], x]) for j, x in enumerate((theirs[0], got1, got2, got3))]
    near01 = jnp.concatenate([own[0], across0, piece1, across1])
    piece2, d_send[2] = after([piece2, d_send[2]], across1, across3)
    across2 = swap(piece2, "tensor", 2)
    d_recv = [d_send[0], None, swap(d_send[2], "dp", 2), None]
    far01 = swap(near01, "tensor", 1)
    near3 = jnp.concatenate([piece3, across3])
    far3 = swap(near3, "tensor", 1)
    across2, d_send[1], d_send[3] = after([across2, d_send[1], d_send[3]], d_recv[2])
    near2 = jnp.concatenate([piece2, across2])
    far2 = swap(near2, "tensor", 1)
    d_recv[1], d_recv[3] = swap(d_send[1], "dp", 1), swap(d_send[3], "dp", 3)
    tokens = [near01, far01, near2, far2, near3, far3]
    layout = ((0, 0, 2), (0, 1, 2), (2, 0, 1), (2, 1, 1), (3, 0, 1), (3, 1, 1))
    cot_all = jnp.concatenate(
        [
            rows_of[j + side][k]
            for first, side, replicas in layout
            for k in range(first, first + replicas)
            for j in (0, 2)
        ]
    ).T
    block = tensor * micro * rows

    def place(x):
        x = x.reshape(tensor, micro, rows, cols)
        return jnp.stack(reorder([x[j] for j in order], t), 1).reshape(
            1, micro, tensor * rows, cols
        )

    own_depth = master_kv.shape[1]
    part_shape = [jax.ShapeDtypeStruct((dp // 2, block, cols), bf16)] * 2
    count = len(tokens)
    master_new, keep, send = pl.pallas_call(
        functools.partial(update_kernel, layout=layout, tile=min(own_depth, 256)),
        out_shape=[jax.ShapeDtypeStruct((own_depth, cols), f32)] + part_shape,
        in_specs=[anywhere] + [vmem] * (4 + count),
        out_specs=[vmem] * 3,
        scratch_shapes=[pltpu.VMEM((own_depth, cols), bf16)],
        compiler_params=params,
        cost_estimate=light,
        name="update",
    )(mark(d_send[3]), cot_all, master_kv[0], moment_m[0], moment_v[0], *tokens)
    total, other = scatter_sum(keep, send)
    mine = place(total.astype(bf16))
    kv_next = from_behind(mine, "segment", -1)
    own_keep, own_send = pl.pallas_call(
        functools.partial(project_kernel, layout=layout),
        out_shape=part_shape,
        in_specs=[anywhere] + [vmem] * (1 + count),
        out_specs=[vmem] * 2,
        compiler_params=params,
        cost_estimate=light,
        name="project",
    )(mark(send), weights, *tokens)
    kv_own = place(scatter_sum(own_keep, own_send)[0].astype(bf16))

    d_recv[1], d_recv[3] = after([d_recv[1], d_recv[3]], own_send, other)
    d_normed = jnp.concatenate(reorder(d_recv, z), -1).astype(f32).reshape(widened.shape)
    upper = d_normed * gain_row
    grad_in = (
        scaling * upper - widened * scaling**3 * jnp.mean(upper * widened, axis=-1, keepdims=True)
    ).astype(bf16)

    return (kv_own, grad_in[None], master_new[None], kv_next)


def solution(mesh):
    in_specs = (
        P("segment", None, ("dp", "tensor"), None),
        P("segment", None),
        P("segment", None, "dp", "tensor"),
        P("segment", "dp", "tensor"),
        P("segment", "dp", "tensor"),
        P("segment", "dp", "tensor"),
    )
    out_specs = (
        P("segment", None, "dp", "tensor"),
        P("segment", None, ("dp", "tensor"), None),
        P("segment", "dp", "tensor"),
        P("segment", None, "dp", "tensor"),
    )
    return jax.shard_map(shards, mesh=mesh, in_specs=in_specs, out_specs=out_specs, check_vma=False)
```

```python
import functools

import jax
import jax.numpy as jnp
from jax import lax
from jax.experimental import pallas as pl
from jax.experimental.pallas import tpu as pltpu
from jax.sharding import PartitionSpec as P

beta_first = 0.9
beta_second = 0.95
learn_rate = 0.03
weight_decay = 0.1
adam_eps = 1e-08
norm_eps = 1e-05
step_count = 20.0

f32 = jnp.float32
bf16 = jnp.bfloat16

vmem = pl.BlockSpec(memory_space=pltpu.VMEM)
smem = pl.BlockSpec(memory_space=pltpu.SMEM)
anywhere = pl.BlockSpec(memory_space=pl.ANY)
light = pl.CostEstimate(flops=1000, bytes_accessed=1000, transcendentals=0)


def swap(x, axis, bits):
    peers = lax.axis_size(axis)
    return lax.ppermute(x, axis, [(i, i ^ bits) for i in range(peers)])


def from_behind(x, axis, by):
    peers = lax.axis_size(axis)
    return lax.ppermute(x, axis, [(i, (i + by) % peers) for i in range(peers)])


def dot(a, b, contract):
    return lax.dot_general(a, b, (contract, ((), ())), preferred_element_type=f32)


def like(*shape, dtype=bf16):
    return jax.ShapeDtypeStruct(shape, dtype)


def call(body, out_shape, in_specs, out_specs, mib, name, scratch=(), **more):
    return pl.pallas_call(
        body,
        out_shape=out_shape,
        in_specs=in_specs,
        out_specs=out_specs,
        scratch_shapes=list(scratch),
        compiler_params=pltpu.CompilerParams(vmem_limit_bytes=int(mib * 1024 * 1024)),
        cost_estimate=light,
        name=name,
        **more,
    )


def after(values, *earlier):
    tied = call(
        lambda *refs: None,
        [like(*x.shape, dtype=x.dtype) for x in values],
        [anywhere] * (len(values) + len(earlier)),
        [anywhere] * len(values),
        0.25,
        "after",
        input_output_aliases={i: i for i in range(len(values))},
    )(*values, *earlier)
    return list(tied)


def lanes(index, size):
    return pl.ds(pl.multiple_of(index * size, size), size)


def norm_kernel(where_ref, hidden_ref, gain_ref, *own_refs, tile):
    z = where_ref[0]
    rows, width = hidden_ref.shape
    depth = width // len(own_refs)

    @pl.loop(0, rows // tile)
    def _(i):
        at = pl.ds(pl.multiple_of(i * tile, tile), tile)
        total = jnp.zeros((tile, 1), f32)
        for k in range(len(own_refs)):
            part = hidden_ref[at, k * depth : (k + 1) * depth].astype(f32)
            total += jnp.sum(part * part, axis=-1, keepdims=True)
        scaling = lax.rsqrt(total * (1.0 / width) + norm_eps)
        for k, own_ref in enumerate(own_refs):
            cut = lanes(z ^ k, depth)
            own_ref[at, :] = (
                hidden_ref[at, cut].astype(f32) * scaling * gain_ref[:, cut]
            ).astype(bf16)


def grad_kernel(where_ref, hidden_ref, gain_ref, *rest, tile):
    d_refs, out_ref = rest[:-1], rest[-1]
    z = where_ref[0]
    rows, width = hidden_ref.shape
    depth = width // len(d_refs)

    @pl.loop(0, rows // tile)
    def _(i):
        at = pl.ds(pl.multiple_of(i * tile, tile), tile)
        squares = jnp.zeros((tile, 1), f32)
        cross = jnp.zeros((tile, 1), f32)
        for k, d_ref in enumerate(d_refs):
            cut = lanes(z ^ k, depth)
            hidden = hidden_ref[at, cut].astype(f32)
            squares += jnp.sum(hidden * hidden, axis=-1, keepdims=True)
            upper = d_ref[at, :].astype(f32) * gain_ref[:, cut]
            cross += jnp.sum(upper * hidden, axis=-1, keepdims=True)
        scaling = lax.rsqrt(squares * (1.0 / width) + norm_eps)
        factor = scaling * scaling * scaling * (cross * (1.0 / width))
        for k, d_ref in enumerate(d_refs):
            cut = lanes(z ^ k, depth)
            upper = d_ref[at, :].astype(f32) * gain_ref[:, cut]
            hidden = hidden_ref[at, cut].astype(f32)
            out_ref[at, cut] = (scaling * upper - hidden * factor).astype(bf16)


def arrange_kernel(where_ref, *refs, dp, layout):
    cots, (zero_ref, one_ref, far_ref, turned_ref) = refs[:dp], refs[dp:]
    t = where_ref[1]
    micro, rows, cols = cots[0].shape
    rows //= 4
    piece = micro * rows

    def block(k, j):
        at = pl.ds(pl.multiple_of((t ^ j) * rows, rows), rows)
        return jnp.concatenate([cots[k][m, at, :] for m in range(micro)])

    for k in range(dp):
        zero_ref[k * piece : (k + 1) * piece, :] = block(k, 0)
        one_ref[k * piece : (k + 1) * piece, :] = block(k, 1)
        far_ref[0, k * piece : (k + 1) * piece, :] = block(k, 2)
        far_ref[1, k * piece : (k + 1) * piece, :] = block(k, 3)
    for p, (k, j) in enumerate(layout):
        turned_ref[:, p * piece : (p + 1) * piece] = block(k, j).astype(f32).T.astype(bf16)


def d_kernel(c0_ref, c1_ref, c2_ref, c3_ref, w0_ref, w1_ref, w2_ref, w3_ref, *d_refs):
    rows = d_refs[0].shape[0]
    depth = d_refs[0].shape[1]
    tile = min(depth, 512)
    for k, d_ref in enumerate(d_refs):
        at = slice(k * rows, (k + 1) * rows)
        cot = jnp.concatenate(
            [c0_ref[at, :], c1_ref[at, :], c2_ref[0, at, :], c3_ref[at, :]], axis=1
        )
        for i in range(depth // tile):
            cut = slice(i * tile, (i + 1) * tile)
            whole = jnp.concatenate([w[cut, :] for w in (w0_ref, w1_ref, w2_ref, w3_ref)], axis=1)
            d_ref[:, cut] = dot(cot, whole, ((1,), (1,))).astype(bf16)


def pack_kernel(*refs):
    pieces, packed_ref, sem = refs[:-2], refs[-2], refs[-1]
    rows = pieces[0].shape[0]
    copies = [
        pltpu.make_async_copy(x, packed_ref.at[pl.ds(p * rows, rows), :], sem.at[p])
        for p, x in enumerate(pieces)
    ]
    for copy in copies:
        copy.start()
    for copy in copies:
        copy.wait()


def token_copies(token_refs, tokens_ref, sems, cut, first):
    copies, row = [], 0
    for p, x in enumerate(token_refs):
        rows = x.shape[0]
        copies.append(
            pltpu.make_async_copy(
                x.at[:, cut], tokens_ref.at[pl.ds(row, rows), cut], sems.at[first + p]
            )
        )
        row += rows
    return copies


def update_kernel(turned_ref, master_hbm, m_hbm, v_hbm, *rest, count, tile, layout):
    token_refs = rest[:count]
    new_hbm, keep_ref, send_ref = rest[count : count + 3]
    tokens, master, m, v, updated, new, sems, out_sems = rest[count + 3 :]
    depth = master.shape[0]
    tiles = depth // tile
    each = count + 3
    groups = []
    for i in range(tiles):
        cut = pl.ds(i * tile, tile)
        group = token_copies(token_refs, tokens, sems, cut, i * each)
        for p, (source, target) in enumerate(((master_hbm, master), (m_hbm, m), (v_hbm, v))):
            group.append(
                pltpu.make_async_copy(
                    source.at[cut, :], target.at[cut, :], sems.at[i * each + count + p]
                )
            )
        for copy in group:
            copy.start()
        groups.append(group)
    outs = []
    for i in range(tiles):
        cut = slice(i * tile, (i + 1) * tile)
        for copy in groups[i]:
            copy.wait()
        grad = dot(turned_ref[...], tokens[:, cut], ((1,), (0,))).T
        m_new = beta_first * m[cut, :] + (1.0 - beta_first) * grad
        v_new = beta_second * v[cut, :] + (1.0 - beta_second) * grad * grad
        m_hat = m_new / (1.0 - beta_first**step_count)
        v_hat = v_new / (1.0 - beta_second**step_count)
        old = master[cut, :]
        master_new = old - learn_rate * (
            m_hat / (jnp.sqrt(v_hat) + adam_eps) + weight_decay * old
        )
        new[cut, :] = master_new
        out = pltpu.make_async_copy(
            new.at[pl.ds(i * tile, tile), :], new_hbm.at[pl.ds(i * tile, tile), :], out_sems.at[i]
        )
        out.start()
        outs.append(out)
        updated[cut, :] = master_new.astype(bf16)
    project(tokens, updated, keep_ref, send_ref, layout)
    for out in outs:
        out.wait()


def project(tokens, weights, keep_ref, send_ref, layout):
    piece = tokens.shape[0] // len(layout)
    slot = {0: 0, 2: 1, 1: 2, 3: 3}
    p = 0
    while p < len(layout):
        k, j = layout[p]
        span = 2 if layout[p + 1 : p + 2] == ((k, j + 2),) else 1
        part_ref = send_ref if k % 2 else keep_ref
        part_ref[k // 2, slot[j] * piece : (slot[j] + span) * piece, :] = dot(
            tokens[p * piece : (p + span) * piece, :], weights[...], ((1,), (0,))
        ).astype(bf16)
        p += span


def project_kernel(mark_ref, weights_ref, *rest, count, layout):
    token_refs = rest[:count]
    keep_ref, send_ref, tokens, sems = rest[count:]
    copies = token_copies(token_refs, tokens, sems, slice(None), 0)
    for copy in copies:
        copy.start()
    for copy in copies:
        copy.wait()
    project(tokens, weights_ref, keep_ref, send_ref, layout)


def reorder(blocks, me):
    bit = 1
    while bit < len(blocks):
        flip = (me & bit) != 0
        blocks = [jnp.where(flip, blocks[i ^ bit], blocks[i]) for i in range(len(blocks))]
        bit *= 2
    return blocks


def scatter_sum(keep, send):
    got = swap(send, "dp", 1)
    mine = keep[0].astype(f32) + got[0].astype(f32)
    other = (keep[1].astype(f32) + got[1].astype(f32)).astype(bf16)
    return mine + swap(other, "dp", 2).astype(f32)


def shards(hidden_in, norm_gain, kv_cot, master_kv, moment_m, moment_v):
    dp, tensor = lax.axis_size("dp"), lax.axis_size("tensor")
    assert dp == 4 and tensor == 4
    z, t = lax.axis_index("dp"), lax.axis_index("tensor")
    where = jnp.stack([z, t]).astype(jnp.int32)
    _, micro, rows, width = hidden_in.shape
    piece = micro * rows
    hidden = hidden_in.reshape(piece, width)
    own_depth, cols = master_kv.shape[1:]
    depth = width // dp
    tile = min(piece, 16)

    weights = master_kv[0].astype(bf16)
    w2 = swap(weights, "tensor", 2)
    w1 = swap(weights, "tensor", 1)
    cot0 = kv_cot[0]
    cot2 = swap(cot0, "dp", 2)
    cot1 = swap(cot0, "dp", 1)
    cot3 = swap(cot2, "dp", 1)
    own = call(
        functools.partial(norm_kernel, tile=tile),
        [like(piece, depth)] * dp,
        [smem, vmem, vmem],
        [vmem] * dp,
        8,
        "norm",
    )(where, hidden, norm_gain)
    n1, n3 = swap(own[1], "dp", 1), swap(own[3], "dp", 3)
    a0 = swap(own[0], "tensor", 2)
    w3 = swap(w2, "tensor", 1)
    layout = (
        (0, 0), (0, 2), (1, 0), (1, 2), (0, 1), (0, 3), (1, 1), (1, 3),
        (3, 0), (3, 2), (3, 1), (3, 3), (2, 0), (2, 2), (2, 1), (2, 3),
    )
    zero, one, far, turned = call(
        functools.partial(arrange_kernel, dp=dp, layout=layout),
        [like(dp * piece, cols)] * 2
        + [like(2, dp * piece, cols), like(cols, dp * tensor * piece)],
        [smem] + [vmem] * dp,
        [vmem] * 4,
        8,
        "arrange",
    )(where, cot0, cot1, cot2, cot3)
    got1 = swap(one, "tensor", 1)
    got2 = swap(far, "tensor", 2)
    got3 = swap(got2[1], "tensor", 1)
    d = list(
        call(
            d_kernel,
            [like(piece, depth)] * dp,
            [vmem] * 8,
            [vmem] * dp,
            16,
            "d_normed",
        )(zero, got1, got2, got3, weights, w1, w2, w3)
    )
    n3, own2 = after([n3, own[2]], d[0])
    n2 = swap(own2, "dp", 2)
    a1, a3 = swap(n1, "tensor", 2), swap(n3, "tensor", 2)
    near = call(
        pack_kernel,
        like(4 * piece, depth),
        [anywhere] * 4,
        anywhere,
        0.25,
        "pack",
        scratch=[pltpu.SemaphoreType.DMA((4,))],
    )(own[0], a0, n1, a1)
    n2, d[2] = after([n2, d[2]], near)
    d2 = swap(d[2], "dp", 2)
    a2 = swap(n2, "tensor", 2)
    a2, d[1], d[3] = after([a2, d[1], d[3]], d2)
    d1, d3 = swap(d[1], "dp", 1), swap(d[3], "dp", 3)
    tokens = [near, swap(near, "tensor", 1)]
    tokens += [n3, a3, swap(n3, "tensor", 1), swap(a3, "tensor", 1)]
    tokens += [n2, a2, swap(n2, "tensor", 1), swap(a2, "tensor", 1)]
    count = len(tokens)
    block = tensor * piece
    part_shape = [like(dp // 2, block, cols)] * 2
    step = min(own_depth, 512)
    tiles = own_depth // step
    whole = pltpu.VMEM((own_depth, cols), f32)
    all_tokens = pltpu.VMEM((dp * block, depth), bf16)
    master_new, keep, send = call(
        functools.partial(update_kernel, count=count, tile=step, layout=layout),
        [like(own_depth, cols, dtype=f32)] + part_shape,
        [vmem] + [anywhere] * (3 + count),
        [anywhere, vmem, vmem],
        24,
        "update",
        scratch=[
            all_tokens,
            whole,
            whole,
            whole,
            pltpu.VMEM((own_depth, cols), bf16),
            whole,
            pltpu.SemaphoreType.DMA((tiles * (count + 3),)),
            pltpu.SemaphoreType.DMA((tiles,)),
        ],
    )(turned, master_kv[0], moment_m[0], moment_v[0], *tokens)

    def place(x):
        x = x.reshape(tensor, micro, rows, cols)
        return jnp.stack(reorder([x[j] for j in (0, 2, 1, 3)], t), 1).reshape(
            1, micro, tensor * rows, cols
        )

    mine = place(scatter_sum(keep, send).astype(bf16))
    kv_next = from_behind(mine, "segment", -1)
    own_keep, own_send = call(
        functools.partial(project_kernel, count=count, layout=layout),
        part_shape,
        [anywhere, vmem] + [anywhere] * count,
        [vmem] * 2,
        16,
        "project",
        scratch=[all_tokens, pltpu.SemaphoreType.DMA((count,))],
    )(send, weights, *tokens)
    kv_own = place(scatter_sum(own_keep, own_send).astype(bf16))
    d1, d3 = after([d1, d3], send)
    grad_in = call(
        functools.partial(grad_kernel, tile=tile),
        like(piece, width),
        [smem] + [vmem] * (2 + dp),
        vmem,
        12,
        "grad_in",
    )(where, hidden, norm_gain, d[0], d1, d2, d3)
    return (kv_own, grad_in.reshape(hidden_in.shape), master_new[None], kv_next)


def solution(mesh):
    in_specs = (
        P("segment", None, ("dp", "tensor"), None),
        P("segment", None),
        P("segment", None, "dp", "tensor"),
        P("segment", "dp", "tensor"),
        P("segment", "dp", "tensor"),
        P("segment", "dp", "tensor"),
    )
    out_specs = (
        P("segment", None, "dp", "tensor"),
        P("segment", None, ("dp", "tensor"), None),
        P("segment", "dp", "tensor"),
        P("segment", None, "dp", "tensor"),
    )
    return jax.shard_map(shards, mesh=mesh, in_specs=in_specs, out_specs=out_specs, check_vma=False)
```

```python
import functools

import jax
import jax.numpy as jnp
from jax import lax
from jax.experimental import pallas as pl
from jax.experimental.pallas import tpu as pltpu
from jax.sharding import PartitionSpec as P

beta_first = 0.9
beta_second = 0.95
learn_rate = 0.03
weight_decay = 0.1
adam_eps = 1e-08
norm_eps = 1e-05
step_count = 20.0

f32 = jnp.float32
bf16 = jnp.bfloat16

vmem = pl.BlockSpec(memory_space=pltpu.VMEM)
smem = pl.BlockSpec(memory_space=pltpu.SMEM)
anywhere = pl.BlockSpec(memory_space=pl.ANY)
light = pl.CostEstimate(flops=1000, bytes_accessed=1000, transcendentals=0)


def swap(x, axis, bits):
    peers = lax.axis_size(axis)
    return lax.ppermute(x, axis, [(i, i ^ bits) for i in range(peers)])


def from_behind(x, axis, by):
    peers = lax.axis_size(axis)
    return lax.ppermute(x, axis, [(i, (i + by) % peers) for i in range(peers)])


def dot(a, b, contract):
    return lax.dot_general(a, b, (contract, ((), ())), preferred_element_type=f32)


def like(*shape, dtype=bf16):
    return jax.ShapeDtypeStruct(shape, dtype)


def call(body, out_shape, in_specs, out_specs, mib, name, scratch=(), **more):
    return pl.pallas_call(
        body,
        out_shape=out_shape,
        in_specs=in_specs,
        out_specs=out_specs,
        scratch_shapes=list(scratch),
        compiler_params=pltpu.CompilerParams(vmem_limit_bytes=int(mib * 1024 * 1024)),
        cost_estimate=light,
        name=name,
        **more,
    )


def after(values, *earlier):
    tied = call(
        lambda *refs: None,
        [like(*x.shape, dtype=x.dtype) for x in values],
        [anywhere] * (len(values) + len(earlier)),
        [anywhere] * len(values),
        0.25,
        "after",
        input_output_aliases={i: i for i in range(len(values))},
    )(*values, *earlier)
    return list(tied)


def lanes(index, size):
    return pl.ds(pl.multiple_of(index * size, size), size)


def norm_kernel(mark_ref, other_ref, where_ref, hidden_ref, gain_ref, *own_refs, tile):
    z = where_ref[0]
    rows, width = hidden_ref.shape
    depth = width // len(own_refs)

    @pl.loop(0, rows // tile)
    def _(i):
        at = pl.ds(pl.multiple_of(i * tile, tile), tile)
        total = jnp.zeros((tile, 1), f32)
        for k in range(len(own_refs)):
            part = hidden_ref[at, k * depth : (k + 1) * depth].astype(f32)
            total += jnp.sum(part * part, axis=-1, keepdims=True)
        scaling = lax.rsqrt(total * (1.0 / width) + norm_eps)
        for k, own_ref in enumerate(own_refs):
            cut = lanes(z ^ k, depth)
            own_ref[at, :] = (
                hidden_ref[at, cut].astype(f32) * scaling * gain_ref[:, cut]
            ).astype(bf16)


def grad_kernel(where_ref, hidden_ref, gain_ref, *rest, tile):
    d0_ref, d1_ref, d23_ref, d3_ref, out_ref = rest
    d_refs = (d0_ref, d1_ref, d23_ref.at[0], d3_ref)
    z = where_ref[0]
    rows, width = hidden_ref.shape
    depth = width // len(d_refs)

    @pl.loop(0, rows // tile)
    def _(i):
        at = pl.ds(pl.multiple_of(i * tile, tile), tile)
        squares = jnp.zeros((tile, 1), f32)
        cross = jnp.zeros((tile, 1), f32)
        for k, d_ref in enumerate(d_refs):
            cut = lanes(z ^ k, depth)
            hidden = hidden_ref[at, cut].astype(f32)
            squares += jnp.sum(hidden * hidden, axis=-1, keepdims=True)
            upper = d_ref[at, :].astype(f32) * gain_ref[:, cut]
            cross += jnp.sum(upper * hidden, axis=-1, keepdims=True)
        scaling = lax.rsqrt(squares * (1.0 / width) + norm_eps)
        factor = scaling * scaling * scaling * (cross * (1.0 / width))
        for k, d_ref in enumerate(d_refs):
            cut = lanes(z ^ k, depth)
            upper = d_ref[at, :].astype(f32) * gain_ref[:, cut]
            hidden = hidden_ref[at, cut].astype(f32)
            out_ref[at, cut] = (scaling * upper - hidden * factor).astype(bf16)


def arrange_kernel(where_ref, *refs, dp, layout):
    cots, (send_ref, turned_ref) = refs[:dp], refs[dp:]
    t = where_ref[1]
    tensor = send_ref.shape[0]
    micro, rows, cols = cots[0].shape
    rows //= tensor
    piece = micro * rows
    for k in range(dp):
        for b in range(tensor):
            for m in range(micro):
                at = k * piece + m * rows
                send_ref[b, at : at + rows, :] = cots[k][m, b * rows : (b + 1) * rows, :]
    for p, (k, j) in enumerate(layout):
        at = pl.ds(pl.multiple_of((t ^ j) * rows, rows), rows)
        block = jnp.concatenate([cots[k][m, at, :] for m in range(micro)])
        turned_ref[:, p * piece : (p + 1) * piece] = block.astype(f32).T.astype(bf16)


def d_kernel(where_ref, cot_ref, *rest):
    w_refs, (d0_ref, d1_ref, d23_ref) = rest[:8], rest[8:]
    rows = d0_ref.shape[0]
    half = w_refs[0].shape[0]
    tile = min(half, 512)
    targets = (d0_ref, d1_ref, d23_ref.at[0], d23_ref.at[1])
    t = where_ref[1]
    cot = jnp.concatenate([cot_ref[t ^ j] for j in range(cot_ref.shape[0])], axis=1)
    for side in range(2):
        for i in range(half // tile):
            cut = slice(i * tile, (i + 1) * tile)
            whole = jnp.concatenate([w[cut, :] for w in w_refs[side::2]], axis=1)
            part = dot(cot, whole, ((1,), (1,))).astype(bf16)
            for k, target in enumerate(targets):
                target[:, side * half + i * tile : side * half + (i + 1) * tile] = part[
                    k * rows : (k + 1) * rows
                ]


def pack_kernel(*refs):
    pieces, packed_ref, sem = refs[:-2], refs[-2], refs[-1]
    rows = pieces[0].shape[0]
    copies = [
        pltpu.make_async_copy(x, packed_ref.at[pl.ds(p * rows, rows), :], sem.at[p])
        for p, x in enumerate(pieces)
    ]
    for copy in copies:
        copy.start()
    for copy in copies:
        copy.wait()


def token_copies(token_refs, tokens_ref, sems, cut, first):
    copies, row = [], 0
    for p, x in enumerate(token_refs):
        rows = x.shape[0]
        copies.append(
            pltpu.make_async_copy(
                x.at[:, cut], tokens_ref.at[pl.ds(row, rows), cut], sems.at[first + p]
            )
        )
        row += rows
    return copies


def update_kernel(turned_ref, master_hbm, m_hbm, v_hbm, *rest, count, tile, layout):
    token_refs = rest[:count]
    new_hbm, part_refs = rest[count], rest[count + 1 : -8]
    tokens, master, m, v, updated, new, sems, out_sems = rest[-8:]
    depth = master.shape[0]
    tiles = depth // tile
    each = count + 3
    groups = []
    for i in range(tiles):
        cut = pl.ds(i * tile, tile)
        group = token_copies(token_refs, tokens, sems, cut, i * each)
        for p, (source, target) in enumerate(((master_hbm, master), (m_hbm, m), (v_hbm, v))):
            group.append(
                pltpu.make_async_copy(
                    source.at[cut, :], target.at[cut, :], sems.at[i * each + count + p]
                )
            )
        for copy in group:
            copy.start()
        groups.append(group)
    outs = []
    for i in range(tiles):
        cut = slice(i * tile, (i + 1) * tile)
        for copy in groups[i]:
            copy.wait()
        grad = dot(turned_ref[...], tokens[:, cut], ((1,), (0,))).T
        m_new = beta_first * m[cut, :] + (1.0 - beta_first) * grad
        v_new = beta_second * v[cut, :] + (1.0 - beta_second) * grad * grad
        m_hat = m_new / (1.0 - beta_first**step_count)
        v_hat = v_new / (1.0 - beta_second**step_count)
        old = master[cut, :]
        master_new = old - learn_rate * (
            m_hat / (jnp.sqrt(v_hat) + adam_eps) + weight_decay * old
        )
        new[cut, :] = master_new
        out = pltpu.make_async_copy(
            new.at[pl.ds(i * tile, tile), :], new_hbm.at[pl.ds(i * tile, tile), :], out_sems.at[i]
        )
        out.start()
        outs.append(out)
        updated[cut, :] = master_new.astype(bf16)
    project(tokens, updated, part_refs, layout)
    for out in outs:
        out.wait()


def project(tokens, weights, part_refs, layout):
    piece = tokens.shape[0] // len(layout)
    slot = {0: 0, 2: 1, 1: 2, 3: 3}
    p = 0
    while p < len(layout):
        k, j = layout[p]
        span = 2 if layout[p + 1 : p + 2] == ((k, j + 2),) else 1
        part_refs[k][slot[j] * piece : (slot[j] + span) * piece, :] = dot(
            tokens[p * piece : (p + span) * piece, :], weights[...], ((1,), (0,))
        ).astype(bf16)
        p += span


def project_kernel(mark_ref, weights_ref, *rest, count, layout):
    token_refs = rest[:count]
    part_refs, (tokens, sems) = rest[count:-2], rest[-2:]
    copies = token_copies(token_refs, tokens, sems, slice(None), 0)
    for copy in copies:
        copy.start()
    for copy in copies:
        copy.wait()
    project(tokens, weights_ref, part_refs, layout)


def reorder(blocks, me):
    bit = 1
    while bit < len(blocks):
        flip = (me & bit) != 0
        blocks = [jnp.where(flip, blocks[i ^ bit], blocks[i]) for i in range(len(blocks))]
        bit *= 2
    return blocks


def scatter_sum(parts, *earlier):
    got1, got3 = swap(parts[1], "dp", 1), swap(parts[3], "dp", 1)
    if earlier:
        got1, got3 = after([got1, got3], *earlier)
    mine = parts[0].astype(f32) + got1.astype(f32)
    other = (parts[2].astype(f32) + got3.astype(f32)).astype(bf16)
    return mine + swap(other, "dp", 2).astype(f32)


def shards(hidden_in, norm_gain, kv_cot, master_kv, moment_m, moment_v):
    dp, tensor = lax.axis_size("dp"), lax.axis_size("tensor")
    assert dp == 4 and tensor == 4
    z, t = lax.axis_index("dp"), lax.axis_index("tensor")
    where = jnp.stack([z, t]).astype(jnp.int32)
    _, micro, rows, width = hidden_in.shape
    piece = micro * rows
    hidden = hidden_in.reshape(piece, width)
    own_depth, cols = master_kv.shape[1:]
    depth = width // dp
    tile = min(piece, 16)

    half = own_depth // 2
    w0 = [master_kv[0, :half].astype(bf16), master_kv[0, half:].astype(bf16)]
    w2 = [swap(w, "tensor", 2) for w in w0]
    w1 = [swap(w, "tensor", 1) for w in w0]
    cot0 = kv_cot[0]
    cot2 = swap(cot0, "dp", 2)
    cot1 = swap(cot0, "dp", 1)
    cot3 = swap(cot2, "dp", 1)
    own = call(
        functools.partial(norm_kernel, tile=tile),
        [like(piece, depth)] * dp,
        [anywhere, anywhere, smem, vmem, vmem],
        [vmem] * dp,
        8,
        "norm",
    )(cot2, cot1, where, hidden, norm_gain)
    n1, n3 = swap(own[1], "dp", 1), swap(own[3], "dp", 3)
    w3 = [swap(w, "tensor", 1) for w in w2]
    layout = tuple((k, j) for k in (0, 1, 3, 2) for j in (0, 2, 1, 3))
    send, turned = call(
        functools.partial(arrange_kernel, dp=dp, layout=layout),
        [like(tensor, dp * piece, cols), like(cols, dp * tensor * piece)],
        [smem] + [vmem] * dp,
        [vmem] * 2,
        8,
        "arrange",
    )(where, cot0, cot1, cot2, cot3)
    own2, n3 = after([own[2], n3])
    n2 = swap(own2, "dp", 2)
    (send,) = after([send], own2)
    mine_cot = lax.all_to_all(send, "tensor", 0, 0, tiled=True)
    d0, d1, d23 = call(
        d_kernel,
        [like(piece, depth)] * 2 + [like(2, piece, depth)],
        [smem] + [vmem] * 9,
        [vmem] * 3,
        20,
        "d_normed",
    )(where, mine_cot, *w0, *w1, *w2, *w3)
    def pack(*pieces):
        return call(
            pack_kernel,
            like(len(pieces) * piece, depth),
            [anywhere] * len(pieces),
            anywhere,
            0.25,
            "pack",
            scratch=[pltpu.SemaphoreType.DMA((len(pieces),))],
        )(*pieces)

    tokens = []
    for x in (own[0], n1, n3):
        near = pack(x, swap(x, "tensor", 2))
        tokens += [near, swap(near, "tensor", 1)]
    n2, d23 = after([n2, d23], tokens[1])
    d23 = swap(d23, "dp", 2)
    d1 = swap(d1, "dp", 1)

    across = swap(n2, "tensor", 2)
    tokens += [n2, across, swap(n2, "tensor", 1), swap(across, "tensor", 1)]
    count = len(tokens)
    block = tensor * piece
    part_shape = [like(block, cols)] * dp
    step = min(own_depth, 512)
    tiles = own_depth // step
    whole = pltpu.VMEM((own_depth, cols), f32)
    all_tokens = pltpu.VMEM((dp * block, depth), bf16)
    master_new, *parts = call(
        functools.partial(update_kernel, count=count, tile=step, layout=layout),
        [like(own_depth, cols, dtype=f32)] + part_shape,
        [vmem] + [anywhere] * (3 + count),
        [anywhere] + [vmem] * dp,
        24,
        "update",
        scratch=[
            all_tokens,
            whole,
            whole,
            whole,
            pltpu.VMEM((own_depth, cols), bf16),
            whole,
            pltpu.SemaphoreType.DMA((tiles * (count + 3),)),
            pltpu.SemaphoreType.DMA((tiles,)),
        ],
    )(turned, master_kv[0], moment_m[0], moment_v[0], *tokens)

    def place(x):
        x = x.reshape(tensor, micro, rows, cols)
        return jnp.stack(reorder([x[j] for j in (0, 2, 1, 3)], t), 1).reshape(
            1, micro, tensor * rows, cols
        )

    mine = place(scatter_sum(parts, d23).astype(bf16))
    kv_next = from_behind(mine, "segment", -1)
    own_parts = call(
        functools.partial(project_kernel, count=count, layout=layout),
        part_shape,
        [anywhere, vmem] + [anywhere] * count,
        [vmem] * dp,
        16,
        "project",
        scratch=[all_tokens, pltpu.SemaphoreType.DMA((count,))],
    )(parts[1], jnp.concatenate(w0), *tokens)
    kv_own = place(scatter_sum(own_parts).astype(bf16))
    d3 = swap(after([d23[1]], parts[1])[0], "dp", 1)
    d1, d3 = after([d1, d3], mine, kv_own)
    grad_in = call(
        functools.partial(grad_kernel, tile=tile),
        like(piece, width),
        [smem] + [vmem] * 6,
        vmem,
        12,
        "grad_in",
    )(where, hidden, norm_gain, d0, d1, d23, d3)
    return (kv_own, grad_in.reshape(hidden_in.shape), master_new[None], kv_next)


def solution(mesh):
    in_specs = (
        P("segment", None, ("dp", "tensor"), None),
        P("segment", None),
        P("segment", None, "dp", "tensor"),
        P("segment", "dp", "tensor"),
        P("segment", "dp", "tensor"),
        P("segment", "dp", "tensor"),
    )
    out_specs = (
        P("segment", None, "dp", "tensor"),
        P("segment", None, ("dp", "tensor"), None),
        P("segment", "dp", "tensor"),
        P("segment", None, "dp", "tensor"),
    )
    return jax.shard_map(shards, mesh=mesh, in_specs=in_specs, out_specs=out_specs, check_vma=False)
```

```python
import functools

import jax
import jax.numpy as jnp
from jax import lax
from jax.experimental import pallas as pl
from jax.experimental.pallas import tpu as pltpu
from jax.sharding import PartitionSpec as P

beta_first = 0.9
beta_second = 0.95
learn_rate = 0.03
weight_decay = 0.1
adam_eps = 1e-08
norm_eps = 1e-05
step_count = 20.0

f32 = jnp.float32
bf16 = jnp.bfloat16

vmem = pl.BlockSpec(memory_space=pltpu.VMEM)
smem = pl.BlockSpec(memory_space=pltpu.SMEM)
anywhere = pl.BlockSpec(memory_space=pl.ANY)
light = pl.CostEstimate(flops=1000, bytes_accessed=1000, transcendentals=0)


def swap(x, axis, bits):
    peers = lax.axis_size(axis)
    return lax.ppermute(x, axis, [(i, i ^ bits) for i in range(peers)])


def from_behind(x, axis, by):
    peers = lax.axis_size(axis)
    return lax.ppermute(x, axis, [(i, (i + by) % peers) for i in range(peers)])


def dot(a, b, contract):
    return lax.dot_general(a, b, (contract, ((), ())), preferred_element_type=f32)


def like(*shape, dtype=bf16):
    return jax.ShapeDtypeStruct(shape, dtype)


def call(body, out_shape, in_specs, out_specs, mib, name, scratch=(), **more):
    return pl.pallas_call(
        body,
        out_shape=out_shape,
        in_specs=in_specs,
        out_specs=out_specs,
        scratch_shapes=list(scratch),
        compiler_params=pltpu.CompilerParams(vmem_limit_bytes=int(mib * 1024 * 1024)),
        cost_estimate=light,
        name=name,
        **more,
    )


def after(values, *earlier):
    tied = call(
        lambda *refs: None,
        [like(*x.shape, dtype=x.dtype) for x in values],
        [anywhere] * (len(values) + len(earlier)),
        [anywhere] * len(values),
        0.25,
        "after",
        input_output_aliases={i: i for i in range(len(values))},
    )(*values, *earlier)
    return list(tied)


def lanes(index, size):
    return pl.ds(pl.multiple_of(index * size, size), size)


def norm_kernel(mark_ref, other_ref, where_ref, hidden_ref, gain_ref, *own_refs, tile):
    z = where_ref[0]
    rows, width = hidden_ref.shape
    depth = width // len(own_refs)

    @pl.loop(0, rows // tile)
    def _(i):
        at = pl.ds(pl.multiple_of(i * tile, tile), tile)
        total = jnp.zeros((tile, 1), f32)
        for k in range(len(own_refs)):
            part = hidden_ref[at, k * depth : (k + 1) * depth].astype(f32)
            total += jnp.sum(part * part, axis=-1, keepdims=True)
        scaling = lax.rsqrt(total * (1.0 / width) + norm_eps)
        for k, own_ref in enumerate(own_refs):
            cut = lanes(z ^ k, depth)
            own_ref[at, :] = (
                hidden_ref[at, cut].astype(f32) * scaling * gain_ref[:, cut]
            ).astype(bf16)


def grad_kernel(hidden_ref, gain_ref, d_ref, out_ref, *, tile):
    rows, width = hidden_ref.shape
    blocks = d_ref.shape[0]
    depth = width // blocks

    @pl.loop(0, rows // tile)
    def _(i):
        at = pl.ds(pl.multiple_of(i * tile, tile), tile)
        squares = jnp.zeros((tile, 1), f32)
        cross = jnp.zeros((tile, 1), f32)
        for k in range(blocks):
            cut = slice(k * depth, (k + 1) * depth)
            hidden = hidden_ref[at, cut].astype(f32)
            squares += jnp.sum(hidden * hidden, axis=-1, keepdims=True)
            upper = d_ref[k, at, :].astype(f32) * gain_ref[:, cut]
            cross += jnp.sum(upper * hidden, axis=-1, keepdims=True)
        scaling = lax.rsqrt(squares * (1.0 / width) + norm_eps)
        factor = scaling * scaling * scaling * (cross * (1.0 / width))
        for k in range(blocks):
            cut = slice(k * depth, (k + 1) * depth)
            upper = d_ref[k, at, :].astype(f32) * gain_ref[:, cut]
            hidden = hidden_ref[at, cut].astype(f32)
            out_ref[at, cut] = (scaling * upper - hidden * factor).astype(bf16)


def arrange_kernel(where_ref, *refs, dp, layout):
    cots, (send_ref, turned_ref) = refs[:dp], refs[dp:]
    t = where_ref[1]
    tensor = send_ref.shape[0]
    micro, rows, cols = cots[0].shape
    rows //= tensor
    piece = micro * rows
    for k in range(dp):
        for b in range(tensor):
            for m in range(micro):
                at = k * piece + m * rows
                send_ref[b, at : at + rows, :] = cots[k][m, b * rows : (b + 1) * rows, :]
    for p, (k, j) in enumerate(layout):
        at = pl.ds(pl.multiple_of((t ^ j) * rows, rows), rows)
        block = jnp.concatenate([cots[k][m, at, :] for m in range(micro)])
        turned_ref[:, p * piece : (p + 1) * piece] = block.astype(f32).T.astype(bf16)


def d_kernel(where_ref, cot_ref, *rest):
    w_refs, d_ref = rest[:8], rest[8]
    z, t = where_ref[0], where_ref[1]
    dp, rows = d_ref.shape[:2]
    half = w_refs[0].shape[0]
    tile = min(half, 512)
    cot = jnp.concatenate([cot_ref[t ^ j] for j in range(cot_ref.shape[0])], axis=1)
    for side in range(2):
        for i in range(half // tile):
            cut = slice(i * tile, (i + 1) * tile)
            whole = jnp.concatenate([w[cut, :] for w in w_refs[side::2]], axis=1)
            part = dot(cot, whole, ((1,), (1,))).astype(bf16)
            for k in range(dp):
                d_ref[z ^ k, :, side * half + i * tile : side * half + (i + 1) * tile] = part[
                    k * rows : (k + 1) * rows
                ]


def pack_kernel(*refs):
    pieces, packed_ref, sem = refs[:-2], refs[-2], refs[-1]
    rows = pieces[0].shape[0]
    copies = [
        pltpu.make_async_copy(x, packed_ref.at[pl.ds(p * rows, rows), :], sem.at[p])
        for p, x in enumerate(pieces)
    ]
    for copy in copies:
        copy.start()
    for copy in copies:
        copy.wait()


def token_copies(token_refs, tokens_ref, sems, cut, first):
    copies, row = [], 0
    for p, x in enumerate(token_refs):
        rows = x.shape[0]
        copies.append(
            pltpu.make_async_copy(
                x.at[:, cut], tokens_ref.at[pl.ds(row, rows), cut], sems.at[first + p]
            )
        )
        row += rows
    return copies


def update_kernel(turned_ref, master_hbm, m_hbm, v_hbm, *rest, count, tile, layout):
    token_refs = rest[:count]
    new_hbm, part_refs = rest[count], rest[count + 1 : -8]
    tokens, master, m, v, updated, new, sems, out_sems = rest[-8:]
    depth = master.shape[0]
    tiles = depth // tile
    each = count + 3
    groups = []
    for i in range(tiles):
        cut = pl.ds(i * tile, tile)
        group = token_copies(token_refs, tokens, sems, cut, i * each)
        for p, (source, target) in enumerate(((master_hbm, master), (m_hbm, m), (v_hbm, v))):
            group.append(
                pltpu.make_async_copy(
                    source.at[cut, :], target.at[cut, :], sems.at[i * each + count + p]
                )
            )
        for copy in group:
            copy.start()
        groups.append(group)
    outs = []
    for i in range(tiles):
        cut = slice(i * tile, (i + 1) * tile)
        for copy in groups[i]:
            copy.wait()
        grad = dot(turned_ref[...], tokens[:, cut], ((1,), (0,))).T
        m_new = beta_first * m[cut, :] + (1.0 - beta_first) * grad
        v_new = beta_second * v[cut, :] + (1.0 - beta_second) * grad * grad
        m_hat = m_new / (1.0 - beta_first**step_count)
        v_hat = v_new / (1.0 - beta_second**step_count)
        old = master[cut, :]
        master_new = old - learn_rate * (
            m_hat / (jnp.sqrt(v_hat) + adam_eps) + weight_decay * old
        )
        new[cut, :] = master_new
        out = pltpu.make_async_copy(
            new.at[pl.ds(i * tile, tile), :], new_hbm.at[pl.ds(i * tile, tile), :], out_sems.at[i]
        )
        out.start()
        outs.append(out)
        updated[cut, :] = master_new.astype(bf16)
    project(tokens, updated, part_refs, layout)
    for out in outs:
        out.wait()


def project(tokens, weights, part_refs, layout):
    piece = tokens.shape[0] // len(layout)
    slot = {0: 0, 2: 1, 1: 2, 3: 3}
    p = 0
    while p < len(layout):
        k, j = layout[p]
        span = 2 if layout[p + 1 : p + 2] == ((k, j + 2),) else 1
        part_refs[k][slot[j] * piece : (slot[j] + span) * piece, :] = dot(
            tokens[p * piece : (p + span) * piece, :], weights[...], ((1,), (0,))
        ).astype(bf16)
        p += span


def project_kernel(mark_ref, weights_ref, *rest, count, layout):
    token_refs = rest[:count]
    part_refs, (tokens, sems) = rest[count:-2], rest[-2:]
    copies = token_copies(token_refs, tokens, sems, slice(None), 0)
    for copy in copies:
        copy.start()
    for copy in copies:
        copy.wait()
    project(tokens, weights_ref, part_refs, layout)


def reorder(blocks, me):
    bit = 1
    while bit < len(blocks):
        flip = (me & bit) != 0
        blocks = [jnp.where(flip, blocks[i ^ bit], blocks[i]) for i in range(len(blocks))]
        bit *= 2
    return blocks


def scatter_sum(parts, *earlier):
    got1, got3 = swap(parts[1], "dp", 1), swap(parts[3], "dp", 1)
    if earlier:
        got1, got3 = after([got1, got3], *earlier)
    mine = parts[0].astype(f32) + got1.astype(f32)
    other = (parts[2].astype(f32) + got3.astype(f32)).astype(bf16)
    return mine + swap(other, "dp", 2).astype(f32)


def shards(hidden_in, norm_gain, kv_cot, master_kv, moment_m, moment_v):
    dp, tensor = lax.axis_size("dp"), lax.axis_size("tensor")
    assert dp == 4 and tensor == 4
    z, t = lax.axis_index("dp"), lax.axis_index("tensor")
    where = jnp.stack([z, t]).astype(jnp.int32)
    _, micro, rows, width = hidden_in.shape
    piece = micro * rows
    hidden = hidden_in.reshape(piece, width)
    own_depth, cols = master_kv.shape[1:]
    depth = width // dp
    tile = min(piece, 16)

    half = own_depth // 2
    w0 = [master_kv[0, :half].astype(bf16), master_kv[0, half:].astype(bf16)]
    w2 = [swap(w, "tensor", 2) for w in w0]
    w1 = [swap(w, "tensor", 1) for w in w0]
    cot0 = kv_cot[0]
    cot2 = swap(cot0, "dp", 2)
    cot1 = swap(cot0, "dp", 1)
    cot3 = swap(cot2, "dp", 1)
    own = call(
        functools.partial(norm_kernel, tile=tile),
        [like(piece, depth)] * dp,
        [anywhere, anywhere, smem, vmem, vmem],
        [vmem] * dp,
        8,
        "norm",
    )(cot2, cot1, where, hidden, norm_gain)
    n1, n3 = swap(own[1], "dp", 1), swap(own[3], "dp", 3)
    w3 = [swap(w, "tensor", 1) for w in w2]
    layout = tuple((k, j) for k in (0, 1, 3, 2) for j in (0, 2, 1, 3))
    send, turned = call(
        functools.partial(arrange_kernel, dp=dp, layout=layout),
        [like(tensor, dp * piece, cols), like(cols, dp * tensor * piece)],
        [smem] + [vmem] * dp,
        [vmem] * 2,
        8,
        "arrange",
    )(where, cot0, cot1, cot2, cot3)
    own2, n3 = after([own[2], n3])
    n2 = swap(own2, "dp", 2)
    (send,) = after([send], own2)
    mine_cot = lax.all_to_all(send, "tensor", 0, 0, tiled=True)
    def pack(*pieces):
        return call(
            pack_kernel,
            like(len(pieces) * piece, depth),
            [anywhere] * len(pieces),
            anywhere,
            0.25,
            "pack",
            scratch=[pltpu.SemaphoreType.DMA((len(pieces),))],
        )(*pieces)

    tokens = []
    for x in (own[0], n1, n3):
        near = pack(x, swap(x, "tensor", 2))
        tokens += [near, swap(near, "tensor", 1)]
    d = call(
        d_kernel,
        like(dp, piece, depth),
        [smem] + [vmem] * 9,
        vmem,
        20,
        "d_normed",
    )(where, mine_cot, *w0, *w1, *w2, *w3)
    n2, d = after([n2, d], tokens[1])
    d = lax.all_to_all(d, "dp", 0, 0, tiled=True)
    across = swap(n2, "tensor", 2)
    tokens += [n2, across, swap(n2, "tensor", 1), swap(across, "tensor", 1)]
    count = len(tokens)
    block = tensor * piece
    part_shape = [like(block, cols)] * dp
    step = min(own_depth, 512)
    tiles = own_depth // step
    whole = pltpu.VMEM((own_depth, cols), f32)
    all_tokens = pltpu.VMEM((dp * block, depth), bf16)
    master_new, *parts = call(
        functools.partial(update_kernel, count=count, tile=step, layout=layout),
        [like(own_depth, cols, dtype=f32)] + part_shape,
        [vmem] + [anywhere] * (3 + count),
        [anywhere] + [vmem] * dp,
        24,
        "update",
        scratch=[
            all_tokens,
            whole,
            whole,
            whole,
            pltpu.VMEM((own_depth, cols), bf16),
            whole,
            pltpu.SemaphoreType.DMA((tiles * (count + 3),)),
            pltpu.SemaphoreType.DMA((tiles,)),
        ],
    )(turned, master_kv[0], moment_m[0], moment_v[0], *tokens)

    def place(x):
        x = x.reshape(tensor, micro, rows, cols)
        return jnp.stack(reorder([x[j] for j in (0, 2, 1, 3)], t), 1).reshape(
            1, micro, tensor * rows, cols
        )

    mine = place(scatter_sum(parts).astype(bf16))
    kv_next = from_behind(mine, "segment", -1)
    own_parts = call(
        functools.partial(project_kernel, count=count, layout=layout),
        part_shape,
        [anywhere, vmem] + [anywhere] * count,
        [vmem] * dp,
        16,
        "project",
        scratch=[all_tokens, pltpu.SemaphoreType.DMA((count,))],
    )(parts[1], jnp.concatenate(w0), *tokens)
    kv_own = place(scatter_sum(own_parts).astype(bf16))
    (d,) = after([d], mine, kv_own)
    grad_in = call(
        functools.partial(grad_kernel, tile=tile),
        like(piece, width),
        [vmem] * 3,
        vmem,
        12,
        "grad_in",
    )(hidden, norm_gain, d)
    return (kv_own, grad_in.reshape(hidden_in.shape), master_new[None], kv_next)


def solution(mesh):
    in_specs = (
        P("segment", None, ("dp", "tensor"), None),
        P("segment", None),
        P("segment", None, "dp", "tensor"),
        P("segment", "dp", "tensor"),
        P("segment", "dp", "tensor"),
        P("segment", "dp", "tensor"),
    )
    out_specs = (
        P("segment", None, "dp", "tensor"),
        P("segment", None, ("dp", "tensor"), None),
        P("segment", "dp", "tensor"),
        P("segment", None, "dp", "tensor"),
    )
    return jax.shard_map(shards, mesh=mesh, in_specs=in_specs, out_specs=out_specs, check_vma=False)
```

```python
import functools

import jax
import jax.numpy as jnp
from jax import lax
from jax.experimental import pallas as pl
from jax.experimental.pallas import tpu as pltpu
from jax.sharding import PartitionSpec as P

beta_first = 0.9
beta_second = 0.95
learn_rate = 0.03
weight_decay = 0.1
adam_eps = 1e-08
norm_eps = 1e-05
step_count = 20.0

f32 = jnp.float32
bf16 = jnp.bfloat16

vmem = pl.BlockSpec(memory_space=pltpu.VMEM)
smem = pl.BlockSpec(memory_space=pltpu.SMEM)
anywhere = pl.BlockSpec(memory_space=pl.ANY)
light = pl.CostEstimate(flops=1000, bytes_accessed=1000, transcendentals=0)


def swap(x, axis, bits):
    peers = lax.axis_size(axis)
    return lax.ppermute(x, axis, [(i, i ^ bits) for i in range(peers)])


def from_behind(x, axis, by):
    peers = lax.axis_size(axis)
    return lax.ppermute(x, axis, [(i, (i + by) % peers) for i in range(peers)])


def dot(a, b, contract):
    return lax.dot_general(a, b, (contract, ((), ())), preferred_element_type=f32)


def like(*shape, dtype=bf16):
    return jax.ShapeDtypeStruct(shape, dtype)


def call(body, out_shape, in_specs, out_specs, mib, name, scratch=(), **more):
    return pl.pallas_call(
        body,
        out_shape=out_shape,
        in_specs=in_specs,
        out_specs=out_specs,
        scratch_shapes=list(scratch),
        compiler_params=pltpu.CompilerParams(vmem_limit_bytes=int(mib * 1024 * 1024)),
        cost_estimate=light,
        name=name,
        **more,
    )


def after(values, *earlier):
    tied = call(
        lambda *refs: None,
        [like(*x.shape, dtype=x.dtype) for x in values],
        [anywhere] * (len(values) + len(earlier)),
        [anywhere] * len(values),
        0.25,
        "after",
        input_output_aliases={i: i for i in range(len(values))},
    )(*values, *earlier)
    return list(tied)


def lanes(index, size):
    return pl.ds(pl.multiple_of(index * size, size), size)


def norm_kernel(hidden_ref, gain_ref, *own_refs, tile):
    blocks, rows = own_refs[0].shape[:2]
    width = hidden_ref.shape[1]
    depth = width // blocks
    for m, own_ref in enumerate(own_refs):

        @pl.loop(0, rows // tile)
        def _(i, m=m, own_ref=own_ref):
            row = pl.multiple_of(i * tile, tile)
            at, to = pl.ds(m * rows + row, tile), pl.ds(row, tile)
            total = jnp.zeros((tile, 1), f32)
            for k in range(blocks):
                part = hidden_ref[at, k * depth : (k + 1) * depth].astype(f32)
                total += jnp.sum(part * part, axis=-1, keepdims=True)
            scaling = lax.rsqrt(total * (1.0 / width) + norm_eps)
            for k in range(blocks):
                cut = slice(k * depth, (k + 1) * depth)
                own_ref[k, to, :] = (
                    hidden_ref[at, cut].astype(f32) * scaling * gain_ref[:, cut]
                ).astype(bf16)


def grad_kernel(hidden_ref, gain_ref, d_ref, out_ref, *, tile):
    rows, width = hidden_ref.shape
    blocks = d_ref.shape[0]
    depth = width // blocks

    @pl.loop(0, rows // tile)
    def _(i):
        at = pl.ds(pl.multiple_of(i * tile, tile), tile)
        squares = jnp.zeros((tile, 1), f32)
        cross = jnp.zeros((tile, 1), f32)
        for k in range(blocks):
            cut = slice(k * depth, (k + 1) * depth)
            hidden = hidden_ref[at, cut].astype(f32)
            squares += jnp.sum(hidden * hidden, axis=-1, keepdims=True)
            upper = d_ref[k, at, :].astype(f32) * gain_ref[:, cut]
            cross += jnp.sum(upper * hidden, axis=-1, keepdims=True)
        scaling = lax.rsqrt(squares * (1.0 / width) + norm_eps)
        factor = scaling * scaling * scaling * (cross * (1.0 / width))
        for k in range(blocks):
            cut = slice(k * depth, (k + 1) * depth)
            upper = d_ref[k, at, :].astype(f32) * gain_ref[:, cut]
            hidden = hidden_ref[at, cut].astype(f32)
            out_ref[at, cut] = (scaling * upper - hidden * factor).astype(bf16)


def arrange_kernel(mark_ref, where_ref, *refs, dp, layout):
    cots, send_refs, (turned_ref, held) = refs[:dp], refs[dp:-2], refs[-2:]
    z, t = where_ref[0], where_ref[1]
    micro, rows, cols = cots[0].shape
    rows //= len(send_refs)
    for k in range(dp):
        held[z ^ k] = cots[k][...]

    def block(k, m, j):
        return held[k, m, pl.ds(pl.multiple_of((t ^ j) * rows, rows), rows), :]

    for j, send_ref in enumerate(send_refs):
        for k in range(dp):
            for m in range(micro):
                at = (k * micro + m) * rows
                send_ref[at : at + rows, :] = block(k, m, j)
    for p, (m, j) in enumerate(layout):
        part = jnp.concatenate([block(k, m, j) for k in range(dp)])
        turned_ref[:, p * dp * rows : (p + 1) * dp * rows] = part.astype(f32).T.astype(bf16)


def d_kernel(*refs):
    cot_refs, w_refs, d_ref = refs[:4], refs[4:8], refs[8]
    dp, rows, depth = d_ref.shape
    tile = min(depth, 512)
    cot = jnp.concatenate([x[...] for x in cot_refs], axis=1)
    for i in range(depth // tile):
        cut = slice(i * tile, (i + 1) * tile)
        whole = jnp.concatenate([w[cut, :] for w in w_refs], axis=1)
        part = dot(cot, whole, ((1,), (1,))).astype(bf16)
        for k in range(dp):
            d_ref[k, :, cut] = part[k * rows : (k + 1) * rows]


def token_copies(token_refs, tokens, sems, cut, first):
    copies, row = [], 0
    for p, x in enumerate(token_refs):
        for k in range(x.shape[0]):
            copies.append(
                pltpu.make_async_copy(
                    x.at[k, :, cut],
                    tokens.at[pl.ds(row, x.shape[1]), cut],
                    sems.at[first + p * x.shape[0] + k],
                )
            )
            row += x.shape[1]
    return copies


def update_kernel(where_ref, turned_ref, master_hbm, m_hbm, v_hbm, *rest, count, tile):
    token_refs, (new_hbm, keep_ref, send_ref) = rest[:count], rest[count : count + 3]
    tokens, master, m, v, updated, new, product, sems, out_sems = rest[count + 3 :]
    tiles = master.shape[0] // tile
    each = count * token_refs[0].shape[0] + 3
    groups = []
    for i in range(tiles):
        cut = pl.ds(i * tile, tile)
        group = token_copies(token_refs, tokens, sems, cut, i * each)
        for p, (source, target) in enumerate(((master_hbm, master), (m_hbm, m), (v_hbm, v))):
            group.append(
                pltpu.make_async_copy(
                    source.at[cut, :], target.at[cut, :], sems.at[(i + 1) * each - 3 + p]
                )
            )
        for copy in group:
            copy.start()
        groups.append(group)
    outs = []
    for i in range(tiles):
        cut = slice(i * tile, (i + 1) * tile)
        for copy in groups[i]:
            copy.wait()
        grad = dot(turned_ref[...], tokens[:, cut], ((1,), (0,))).T
        m_new = beta_first * m[cut, :] + (1.0 - beta_first) * grad
        v_new = beta_second * v[cut, :] + (1.0 - beta_second) * grad * grad
        m_hat = m_new / (1.0 - beta_first**step_count)
        v_hat = v_new / (1.0 - beta_second**step_count)
        old = master[cut, :]
        master_new = old - learn_rate * (
            m_hat / (jnp.sqrt(v_hat) + adam_eps) + weight_decay * old
        )
        new[cut, :] = master_new
        out = pltpu.make_async_copy(
            new.at[pl.ds(i * tile, tile), :], new_hbm.at[pl.ds(i * tile, tile), :], out_sems.at[i]
        )
        out.start()
        outs.append(out)
        updated[cut, :] = master_new.astype(bf16)
    project(where_ref, tokens, updated, keep_ref, send_ref, product, count)
    for out in outs:
        out.wait()


def project(where_ref, tokens, weights, keep_ref, send_ref, product, count):
    z = where_ref[0]
    dp, rows = product.shape[1:3]
    size = dp * rows
    for p in range(count):
        part = dot(tokens[p * size : (p + 1) * size, :], weights[...], ((1,), (0,)))
        product[p] = part.astype(bf16).reshape(product.shape[1:])
    for k in range(dp):
        part_ref = send_ref if k % 2 else keep_ref
        for p in range(count):
            part_ref[k // 2, p * rows : (p + 1) * rows, :] = product[p, z ^ k]


def project_kernel(mark_ref, where_ref, weights_ref, *rest, count):
    token_refs = rest[:count]
    keep_ref, send_ref, tokens, product, sems = rest[count:]
    copies = token_copies(token_refs, tokens, sems, slice(None), 0)
    for copy in copies:
        copy.start()
    for copy in copies:
        copy.wait()
    project(where_ref, tokens, weights_ref, keep_ref, send_ref, product, count)


def reorder(blocks, me):
    bit = 1
    while bit < len(blocks):
        flip = (me & bit) != 0
        blocks = [jnp.where(flip, blocks[i ^ bit], blocks[i]) for i in range(len(blocks))]
        bit *= 2
    return blocks


def scatter_sum(keep, send, *earlier):
    got = swap(send, "dp", 1)
    if earlier:
        got = after([got], *earlier)[0]
    mine = keep[0].astype(f32) + got[0].astype(f32)
    other = (keep[1].astype(f32) + got[1].astype(f32)).astype(bf16)
    return mine + swap(other, "dp", 2).astype(f32)


def shards(hidden_in, norm_gain, kv_cot, master_kv, moment_m, moment_v):
    dp, tensor = lax.axis_size("dp"), lax.axis_size("tensor")
    assert dp == 4 and tensor == 4
    z, t = lax.axis_index("dp"), lax.axis_index("tensor")
    where = jnp.stack([z, t]).astype(jnp.int32)
    _, micro, rows, width = hidden_in.shape
    piece = micro * rows
    hidden = hidden_in.reshape(piece, width)
    own_depth, cols = master_kv.shape[1:]
    depth = width // dp
    tile = min(piece, 16)

    w0 = master_kv[0].astype(bf16)
    w2, w1 = swap(w0, "tensor", 2), swap(w0, "tensor", 1)
    cot0 = kv_cot[0]
    cot2, cot1 = swap(cot0, "dp", 2), swap(cot0, "dp", 1)
    cot3 = swap(cot2, "dp", 1)
    own = call(
        functools.partial(norm_kernel, tile=tile),
        [like(dp, rows, depth)] * micro,
        [vmem, vmem],
        [vmem] * micro,
        8,
        "norm",
    )(hidden, norm_gain)
    token0 = lax.all_to_all(own[0], "dp", 0, 0, tiled=True)
    layout = tuple((m, j) for m in range(micro) for j in (0, 1, 2, 3))
    *blocks, turned = call(
        functools.partial(arrange_kernel, dp=dp, layout=layout),
        [like(dp * piece, cols)] * tensor + [like(cols, dp * tensor * piece)],
        [anywhere, smem] + [vmem] * dp,
        [vmem] * (tensor + 1),
        8,
        "arrange",
        scratch=[pltpu.VMEM((dp,) + cot0.shape, bf16)],
    )(w2, where, cot0, cot1, cot2, cot3)
    own1, token0 = after([own[1], token0], blocks[0])
    token1 = lax.all_to_all(own1, "dp", 0, 0, tiled=True)
    across0 = swap(token0, "tensor", 2)
    mine_cot = [blocks[0]] + [swap(blocks[j], "tensor", j) for j in range(1, tensor)]
    w3 = swap(w2, "tensor", 1)
    d = call(
        d_kernel,
        like(dp, piece, depth),
        [vmem] * 8,
        vmem,
        20,
        "d_normed",
    )(*mine_cot, w0, w1, w2, w3)
    token1, d = after([token1, d], across0)
    d = lax.all_to_all(d, "dp", 0, 0, tiled=True)
    tokens = []
    for x, across in ((token0, across0), (token1, swap(token1, "tensor", 2))):
        tokens += [x, swap(x, "tensor", 1), across, swap(across, "tensor", 1)]
    count = len(tokens)
    block = tensor * piece
    part_shape = [like(dp // 2, block, cols)] * 2
    step = min(own_depth, 512)
    tiles = own_depth // step
    whole = pltpu.VMEM((own_depth, cols), f32)
    all_tokens = pltpu.VMEM((dp * block, depth), bf16)
    product = pltpu.VMEM((count, dp, rows, cols), bf16)
    master_new, keep, send = call(
        functools.partial(update_kernel, count=count, tile=step),
        [like(own_depth, cols, dtype=f32)] + part_shape,
        [smem, vmem] + [anywhere] * (3 + count),
        [anywhere] + [vmem] * 2,
        25,
        "update",
        scratch=[
            all_tokens,
            whole,
            whole,
            whole,
            pltpu.VMEM((own_depth, cols), bf16),
            whole,
            product,
            pltpu.SemaphoreType.DMA((tiles * (count * dp + 3),)),
            pltpu.SemaphoreType.DMA((tiles,)),
        ],
    )(where, turned, master_kv[0], moment_m[0], moment_v[0], *tokens)

    def place(x):
        x = x.reshape(micro, tensor, rows, cols)
        return jnp.stack(reorder([x[:, j] for j in range(tensor)], t), 1).reshape(
            1, micro, tensor * rows, cols
        )

    mine = place(scatter_sum(keep, send, d).astype(bf16))
    kv_next = from_behind(mine, "segment", -1)
    own_keep, own_send = call(
        functools.partial(project_kernel, count=count),
        part_shape,
        [anywhere, smem, vmem] + [anywhere] * count,
        [vmem] * 2,
        17,
        "project",
        scratch=[all_tokens, product, pltpu.SemaphoreType.DMA((count * dp,))],
    )(send, where, w0, *tokens)
    kv_own = place(scatter_sum(own_keep, own_send).astype(bf16))
    (d,) = after([d], mine, kv_own)
    grad_in = call(
        functools.partial(grad_kernel, tile=tile),
        like(piece, width),
        [vmem] * 3,
        vmem,
        12,
        "grad_in",
    )(hidden, norm_gain, d)
    return (kv_own, grad_in.reshape(hidden_in.shape), master_new[None], kv_next)


def solution(mesh):
    in_specs = (
        P("segment", None, ("dp", "tensor"), None),
        P("segment", None),
        P("segment", None, "dp", "tensor"),
        P("segment", "dp", "tensor"),
        P("segment", "dp", "tensor"),
        P("segment", "dp", "tensor"),
    )
    out_specs = (
        P("segment", None, "dp", "tensor"),
        P("segment", None, ("dp", "tensor"), None),
        P("segment", "dp", "tensor"),
        P("segment", None, "dp", "tensor"),
    )
    return jax.shard_map(shards, mesh=mesh, in_specs=in_specs, out_specs=out_specs, check_vma=False)
```

```python
import functools

import jax
import jax.numpy as jnp
from jax import lax
from jax.experimental import pallas as pl
from jax.experimental.pallas import tpu as pltpu
from jax.sharding import PartitionSpec as P

beta_first = 0.9
beta_second = 0.95
learn_rate = 0.03
weight_decay = 0.1
adam_eps = 1e-08
norm_eps = 1e-05
step_count = 20.0

f32 = jnp.float32
bf16 = jnp.bfloat16

vmem = pl.BlockSpec(memory_space=pltpu.VMEM)
smem = pl.BlockSpec(memory_space=pltpu.SMEM)
anywhere = pl.BlockSpec(memory_space=pl.ANY)
light = pl.CostEstimate(flops=1000, bytes_accessed=1000, transcendentals=0)


def swap(x, axis, bits):
    peers = lax.axis_size(axis)
    return lax.ppermute(x, axis, [(i, i ^ bits) for i in range(peers)])


def from_behind(x, axis, by):
    peers = lax.axis_size(axis)
    return lax.ppermute(x, axis, [(i, (i + by) % peers) for i in range(peers)])


def dot(a, b, contract):
    return lax.dot_general(a, b, (contract, ((), ())), preferred_element_type=f32)


def like(*shape, dtype=bf16):
    return jax.ShapeDtypeStruct(shape, dtype)


def call(body, out_shape, in_specs, out_specs, mib, name, scratch=(), **more):
    return pl.pallas_call(
        body,
        out_shape=out_shape,
        in_specs=in_specs,
        out_specs=out_specs,
        scratch_shapes=list(scratch),
        compiler_params=pltpu.CompilerParams(vmem_limit_bytes=int(mib * 1024 * 1024)),
        cost_estimate=light,
        name=name,
        **more,
    )


def after(values, *earlier):
    tied = call(
        lambda *refs: None,
        [like(*x.shape, dtype=x.dtype) for x in values],
        [anywhere] * (len(values) + len(earlier)),
        [anywhere] * len(values),
        0.25,
        "after",
        input_output_aliases={i: i for i in range(len(values))},
    )(*values, *earlier)
    return list(tied)


def lanes(index, size):
    return pl.ds(pl.multiple_of(index * size, size), size)


def norm_kernel(hidden_ref, gain_ref, *own_refs, tile):
    blocks = own_refs[0].shape[0]
    width = hidden_ref.shape[1]
    depth = width // blocks
    start = 0
    for own_ref in own_refs:

        @pl.loop(0, own_ref.shape[1] // tile)
        def _(i, start=start, own_ref=own_ref):
            row = pl.multiple_of(i * tile, tile)
            at, to = pl.ds(start + row, tile), pl.ds(row, tile)
            total = jnp.zeros((tile, 1), f32)
            for k in range(blocks):
                part = hidden_ref[at, k * depth : (k + 1) * depth].astype(f32)
                total += jnp.sum(part * part, axis=-1, keepdims=True)
            scaling = lax.rsqrt(total * (1.0 / width) + norm_eps)
            for k in range(blocks):
                cut = slice(k * depth, (k + 1) * depth)
                own_ref[k, to, :] = (
                    hidden_ref[at, cut].astype(f32) * scaling * gain_ref[:, cut]
                ).astype(bf16)

        start += own_ref.shape[1]


def grad_kernel(hidden_ref, gain_ref, d_ref, out_ref, *, tile):
    rows, width = hidden_ref.shape
    blocks = d_ref.shape[0]
    depth = width // blocks

    @pl.loop(0, rows // tile)
    def _(i):
        at = pl.ds(pl.multiple_of(i * tile, tile), tile)
        squares = jnp.zeros((tile, 1), f32)
        cross = jnp.zeros((tile, 1), f32)
        for k in range(blocks):
            cut = slice(k * depth, (k + 1) * depth)
            hidden = hidden_ref[at, cut].astype(f32)
            squares += jnp.sum(hidden * hidden, axis=-1, keepdims=True)
            upper = d_ref[k, at, :].astype(f32) * gain_ref[:, cut]
            cross += jnp.sum(upper * hidden, axis=-1, keepdims=True)
        scaling = lax.rsqrt(squares * (1.0 / width) + norm_eps)
        factor = scaling * scaling * scaling * (cross * (1.0 / width))
        for k in range(blocks):
            cut = slice(k * depth, (k + 1) * depth)
            upper = d_ref[k, at, :].astype(f32) * gain_ref[:, cut]
            hidden = hidden_ref[at, cut].astype(f32)
            out_ref[at, cut] = (scaling * upper - hidden * factor).astype(bf16)


def arrange_kernel(mark_ref, where_ref, *refs, dp, cuts):
    cots, send_refs, (turned_ref, held) = refs[:dp], refs[dp:-2], refs[-2:]
    z, t = where_ref[0], where_ref[1]
    tensor = len(send_refs)
    micro, rows, cols = cots[0].shape
    rows //= tensor
    piece = micro * rows
    for k in range(dp):
        held[z ^ k] = cots[k][...]
    for j, send_ref in enumerate(send_refs):
        at = pl.ds(pl.multiple_of((t ^ j) * rows, rows), rows)
        for k in range(dp):
            for m in range(micro):
                start = k * piece + m * rows
                send_ref[start : start + rows, :] = held[k, m, at, :]
    position = 0
    for low, high in zip(cuts[:-1], cuts[1:]):
        for send_ref in send_refs:
            part = jnp.concatenate(
                [send_ref[k * piece + low : k * piece + high, :] for k in range(dp)]
            )
            width = dp * (high - low)
            turned_ref[:, position : position + width] = part.astype(f32).T.astype(bf16)
            position += width


def d_kernel(*refs):
    cot_refs, w_refs, d_ref = refs[:4], refs[4:8], refs[8]
    dp, rows, depth = d_ref.shape
    tile = min(depth, 512)
    cot = jnp.concatenate([x[...] for x in cot_refs], axis=1)
    for i in range(depth // tile):
        cut = slice(i * tile, (i + 1) * tile)
        whole = jnp.concatenate([w[cut, :] for w in w_refs], axis=1)
        part = dot(cot, whole, ((1,), (1,))).astype(bf16)
        for k in range(dp):
            d_ref[k, :, cut] = part[k * rows : (k + 1) * rows]


def token_copies(token_refs, tokens, sems, cut, first):
    copies, row = [], 0
    for p, x in enumerate(token_refs):
        for k in range(x.shape[0]):
            copies.append(
                pltpu.make_async_copy(
                    x.at[k, :, cut],
                    tokens.at[pl.ds(row, x.shape[1]), cut],
                    sems.at[first + p * x.shape[0] + k],
                )
            )
            row += x.shape[1]
    return copies


def update_kernel(mark_ref, where_ref, turned_ref, weights_ref, master_hbm, m_hbm, v_hbm, *rest, cuts):
    tensor = (len(rest) - 13) // (len(cuts) - 1)
    count = tensor * (len(cuts) - 1)
    token_refs, new_hbm, part_refs = rest[:count], rest[count], rest[count + 1 : count + 5]
    tokens, master, m, v, updated, new, sems, out_sems = rest[count + 5 :]
    tile = new.shape[0] // out_sems.shape[0]
    each = count * token_refs[0].shape[0] + 3
    groups = []
    for i in range(out_sems.shape[0]):
        cut = pl.ds(i * tile, tile)
        group = token_copies(token_refs, tokens, sems, cut, i * each)
        for p, (source, target) in enumerate(((master_hbm, master), (m_hbm, m), (v_hbm, v))):
            group.append(
                pltpu.make_async_copy(
                    source.at[cut, :], target.at[cut, :], sems.at[(i + 1) * each - 3 + p]
                )
            )
        for copy in group:
            copy.start()
        groups.append(group)
    outs = []
    for i in range(out_sems.shape[0]):
        cut = slice(i * tile, (i + 1) * tile)
        for copy in groups[i]:
            copy.wait()
        grad = dot(turned_ref[...], tokens[:, cut], ((1,), (0,))).T
        m_new = beta_first * m[cut, :] + (1.0 - beta_first) * grad
        v_new = beta_second * v[cut, :] + (1.0 - beta_second) * grad * grad
        m_hat = m_new / (1.0 - beta_first**step_count)
        v_hat = v_new / (1.0 - beta_second**step_count)
        old = master[cut, :]
        master_new = old - learn_rate * (
            m_hat / (jnp.sqrt(v_hat) + adam_eps) + weight_decay * old
        )
        new[cut, :] = master_new
        out = pltpu.make_async_copy(
            new.at[pl.ds(i * tile, tile), :], new_hbm.at[pl.ds(i * tile, tile), :], out_sems.at[i]
        )
        out.start()
        outs.append(out)
        updated[cut, :] = master_new.astype(bf16)
    project(where_ref, tokens, updated, *part_refs[:2], cuts, 0)
    project(where_ref, tokens, weights_ref, *part_refs[2:], cuts, len(cuts) - 2)
    for out in outs:
        out.wait()


def project(where_ref, tokens, weights, keep_ref, send_ref, cuts, first):
    z = where_ref[0]
    dp = 4
    tensor = tokens.shape[0] // (dp * cuts[-1])
    stored = keep_ref.shape[1] // tensor
    for c in range(first, len(cuts) - 1):
        rows = cuts[c + 1] - cuts[c]
        for j in range(tensor):
            at = dp * (tensor * cuts[c] + j * rows)
            part = dot(tokens[at : at + dp * rows, :], weights[...], ((1,), (0,))).astype(bf16)
            to = j * stored + cuts[c] - cuts[first]
            for k in range(dp):
                piece = part[k * rows : (k + 1) * rows]
                if k % 2 == 0:
                    even = piece
                else:
                    odd = z % 2 == 1
                    slot = (k // 2) ^ (z // 2)
                    keep_ref[slot, to : to + rows, :] = jnp.where(odd, piece, even)
                    send_ref[slot, to : to + rows, :] = jnp.where(odd, even, piece)


def project_kernel(where_ref, weights_ref, *rest, cuts):
    token_refs, (keep_ref, send_ref, tokens, sems) = rest[:-4], rest[-4:]
    copies = token_copies(token_refs, tokens, sems, slice(None), 0)
    for copy in copies:
        copy.start()
    for copy in copies:
        copy.wait()
    project(where_ref, tokens, weights_ref, keep_ref, send_ref, cuts, 0)


def reorder(blocks, me):
    bit = 1
    while bit < len(blocks):
        flip = (me & bit) != 0
        blocks = [jnp.where(flip, blocks[i ^ bit], blocks[i]) for i in range(len(blocks))]
        bit *= 2
    return blocks


def scatter_sum(keep, send, *earlier):
    got = swap(send, "dp", 1)
    if earlier:
        got = after([got], *earlier)[0]
    mine = keep[0].astype(f32) + got[0].astype(f32)
    other = (keep[1].astype(f32) + got[1].astype(f32)).astype(bf16)
    return mine + swap(other, "dp", 2).astype(f32), got


def shards(hidden_in, norm_gain, kv_cot, master_kv, moment_m, moment_v):
    dp, tensor = lax.axis_size("dp"), lax.axis_size("tensor")
    assert dp == 4 and tensor == 4
    z, t = lax.axis_index("dp"), lax.axis_index("tensor")
    where = jnp.stack([z, t]).astype(jnp.int32)
    _, micro, rows, width = hidden_in.shape
    piece = micro * rows
    hidden = hidden_in.reshape(piece, width)
    own_depth, cols = master_kv.shape[1:]
    depth = width // dp
    tile = min(piece, 16)

    w0 = master_kv[0].astype(bf16)
    w2, w1 = swap(w0, "tensor", 2), swap(w0, "tensor", 1)
    cot0 = kv_cot[0]
    cot2, cot1 = swap(cot0, "dp", 2), swap(cot0, "dp", 1)
    cot3 = swap(cot0, "dp", 3)
    cuts = (0, 3 * piece // 8, 3 * piece // 4, piece)
    own = call(
        functools.partial(norm_kernel, tile=tile),
        [like(dp, high - low, depth) for low, high in zip(cuts[:-1], cuts[1:])],
        [vmem, vmem],
        [vmem] * (len(cuts) - 1),
        60,
        "norm",
    )(hidden, norm_gain)
    *blocks, turned = call(
        functools.partial(arrange_kernel, dp=dp, cuts=cuts),
        [like(dp * piece, cols)] * tensor + [like(cols, dp * tensor * piece)],
        [anywhere, smem] + [vmem] * dp,
        [vmem] * (tensor + 1),
        60,
        "arrange",
        scratch=[pltpu.VMEM((dp,) + cot0.shape, bf16)],
    )(w2, where, cot0, cot1, cot2, cot3)
    (own0,) = after([own[0]], blocks[0])
    token0 = lax.all_to_all(own0, "dp", 0, 0, tiled=True)
    mine_cot = [blocks[0]] + [swap(blocks[j], "tensor", j) for j in range(1, tensor)]
    w3 = swap(w2, "tensor", 1)
    own1, token0 = after([own[1], token0], mine_cot[2], mine_cot[3])
    token1 = lax.all_to_all(own1, "dp", 0, 0, tiled=True)
    across0 = swap(token0, "tensor", 2)
    d = call(
        d_kernel,
        like(dp, piece, depth),
        [vmem] * 8,
        vmem,
        60,
        "d_normed",
    )(*mine_cot, w0, w1, w2, w3)
    own2, token1 = after([own[2], token1], across0)
    token2 = lax.all_to_all(own2, "dp", 0, 0, tiled=True)
    across1 = swap(token1, "tensor", 2)
    token2, d = after([token2, d], across1)
    d = lax.all_to_all(d, "dp", 0, 0, tiled=True)
    across2 = swap(token2, "tensor", 2)
    tokens = []
    for x, across in ((token0, across0), (token1, across1), (token2, across2)):
        tokens += [x, swap(x, "tensor", 1), across, swap(across, "tensor", 1)]
    count = len(tokens)
    block = tensor * piece
    first = cuts[-2]
    part_shape = [like(dp // 2, block, cols)] * 2
    step = min(own_depth, 512)
    tiles = own_depth // step
    whole = pltpu.VMEM((own_depth, cols), f32)
    keep0, send0 = call(
        functools.partial(project_kernel, cuts=cuts[:-1]),
        [like(dp // 2, tensor * first, cols)] * 2,
        [smem, vmem] + [anywhere] * (count - tensor),
        [vmem] * 2,
        60,
        "project",
        scratch=[
            pltpu.VMEM((dp * tensor * first, depth), bf16),
            pltpu.SemaphoreType.DMA(((count - tensor) * dp,)),
        ],
    )(where, w0, *tokens[:-tensor])
    master_new, keep, send, keep1, send1 = call(
        functools.partial(update_kernel, cuts=cuts),
        [like(own_depth, cols, dtype=f32)] + part_shape
        + [like(dp // 2, tensor * (piece - first), cols)] * 2,
        [anywhere, smem, vmem, vmem] + [anywhere] * (3 + count),
        [anywhere] + [vmem] * 4,
        60,
        "update",
        scratch=[
            pltpu.VMEM((dp * block, depth), bf16),
            whole,
            whole,
            whole,
            pltpu.VMEM((own_depth, cols), bf16),
            whole,
            pltpu.SemaphoreType.DMA((tiles * (count * dp + 3),)),
            pltpu.SemaphoreType.DMA((tiles,)),
        ],
    )(send0, where, turned, w0, master_kv[0], moment_m[0], moment_v[0], *tokens)

    def place(x):
        x = x.reshape(tensor, micro, rows, cols)
        return jnp.stack(reorder([x[j] for j in range(tensor)], t), 1).reshape(
            1, micro, tensor * rows, cols
        )

    mine, got = scatter_sum(keep, send, d)
    mine = place(mine.astype(bf16))
    kv_next = from_behind(mine, "segment", -1)
    (send1,) = after([send1], got)
    early, _ = scatter_sum(keep0, send0)
    late, _ = scatter_sum(keep1, send1)
    kv_own = place(
        jnp.concatenate(
            [x.reshape(tensor, -1, cols) for x in (early.astype(bf16), late.astype(bf16))], 1
        )
    )
    (d,) = after([d], mine, kv_own)
    grad_in = call(
        functools.partial(grad_kernel, tile=tile),
        like(piece, width),
        [vmem] * 3,
        vmem,
        60,
        "grad_in",
    )(hidden, norm_gain, d)
    return (kv_own, grad_in.reshape(hidden_in.shape), master_new[None], kv_next)


def solution(mesh):
    in_specs = (
        P("segment", None, ("dp", "tensor"), None),
        P("segment", None),
        P("segment", None, "dp", "tensor"),
        P("segment", "dp", "tensor"),
        P("segment", "dp", "tensor"),
        P("segment", "dp", "tensor"),
    )
    out_specs = (
        P("segment", None, "dp", "tensor"),
        P("segment", None, ("dp", "tensor"), None),
        P("segment", "dp", "tensor"),
        P("segment", None, "dp", "tensor"),
    )
    return jax.shard_map(shards, mesh=mesh, in_specs=in_specs, out_specs=out_specs, check_vma=False)
```

```python
import functools

import jax
import jax.numpy as jnp
from jax import lax
from jax.experimental import pallas as pl
from jax.experimental.pallas import tpu as pltpu
from jax.sharding import PartitionSpec as P

beta_first = 0.9
beta_second = 0.95
learn_rate = 0.03
weight_decay = 0.1
adam_eps = 1e-08
norm_eps = 1e-05
step_count = 20.0

f32 = jnp.float32
bf16 = jnp.bfloat16

vmem = pl.BlockSpec(memory_space=pltpu.VMEM)
smem = pl.BlockSpec(memory_space=pltpu.SMEM)
anywhere = pl.BlockSpec(memory_space=pl.ANY)
light = pl.CostEstimate(flops=1000, bytes_accessed=1000, transcendentals=0)


def swap(x, axis, bits):
    peers = lax.axis_size(axis)
    return lax.ppermute(x, axis, [(i, i ^ bits) for i in range(peers)])


def from_behind(x, axis, by):
    peers = lax.axis_size(axis)
    return lax.ppermute(x, axis, [(i, (i + by) % peers) for i in range(peers)])


def dot(a, b, contract):
    return lax.dot_general(a, b, (contract, ((), ())), preferred_element_type=f32)


def like(*shape, dtype=bf16):
    return jax.ShapeDtypeStruct(shape, dtype)


def call(body, out_shape, in_specs, out_specs, mib, name, scratch=(), **more):
    return pl.pallas_call(
        body,
        out_shape=out_shape,
        in_specs=in_specs,
        out_specs=out_specs,
        scratch_shapes=list(scratch),
        compiler_params=pltpu.CompilerParams(vmem_limit_bytes=int(mib * 1024 * 1024)),
        cost_estimate=light,
        name=name,
        **more,
    )


def after(values, *earlier):
    tied = call(
        lambda *refs: None,
        [like(*x.shape, dtype=x.dtype) for x in values],
        [anywhere] * (len(values) + len(earlier)),
        [anywhere] * len(values),
        0.25,
        "after",
        input_output_aliases={i: i for i in range(len(values))},
    )(*values, *earlier)
    return list(tied)


def lanes(index, size):
    return pl.ds(pl.multiple_of(index * size, size), size)


def norm_kernel(mark_ref, other_ref, where_ref, hidden_ref, gain_ref, *own_refs, tile):
    z = where_ref[0]
    rows, width = hidden_ref.shape
    depth = width // len(own_refs)

    @pl.loop(0, rows // tile)
    def _(i):
        at = pl.ds(pl.multiple_of(i * tile, tile), tile)
        total = jnp.zeros((tile, 1), f32)
        for k in range(len(own_refs)):
            part = hidden_ref[at, k * depth : (k + 1) * depth].astype(f32)
            total += jnp.sum(part * part, axis=-1, keepdims=True)
        scaling = lax.rsqrt(total * (1.0 / width) + norm_eps)
        for k, own_ref in enumerate(own_refs):
            cut = lanes(z ^ k, depth)
            own_ref[at, :] = (
                hidden_ref[at, cut].astype(f32) * scaling * gain_ref[:, cut]
            ).astype(bf16)


def grad_kernel(hidden_ref, gain_ref, d_ref, out_ref, *, tile):
    rows, width = hidden_ref.shape
    blocks = d_ref.shape[0]
    depth = width // blocks

    @pl.loop(0, rows // tile)
    def _(i):
        at = pl.ds(pl.multiple_of(i * tile, tile), tile)
        squares = jnp.zeros((tile, 1), f32)
        cross = jnp.zeros((tile, 1), f32)
        for k in range(blocks):
            cut = slice(k * depth, (k + 1) * depth)
            hidden = hidden_ref[at, cut].astype(f32)
            squares += jnp.sum(hidden * hidden, axis=-1, keepdims=True)
            upper = d_ref[k, at, :].astype(f32) * gain_ref[:, cut]
            cross += jnp.sum(upper * hidden, axis=-1, keepdims=True)
        scaling = lax.rsqrt(squares * (1.0 / width) + norm_eps)
        factor = scaling * scaling * scaling * (cross * (1.0 / width))
        for k in range(blocks):
            cut = slice(k * depth, (k + 1) * depth)
            upper = d_ref[k, at, :].astype(f32) * gain_ref[:, cut]
            hidden = hidden_ref[at, cut].astype(f32)
            out_ref[at, cut] = (scaling * upper - hidden * factor).astype(bf16)


def arrange_kernel(mark_ref, where_ref, *refs, dp, layout):
    cots, send_refs, turned_ref = refs[:dp], refs[dp:-1], refs[-1]
    t = where_ref[1]
    tensor = len(send_refs)
    micro, rows, cols = cots[0].shape
    rows //= tensor
    piece = micro * rows
    for j, send_ref in enumerate(send_refs):
        at = pl.ds(pl.multiple_of((t ^ j) * rows, rows), rows)
        for k in range(dp):
            for m in range(micro):
                start = k * piece + m * rows
                send_ref[start : start + rows, :] = cots[k][m, at, :]
    for p, (k, j) in enumerate(layout):
        block = send_refs[j][k * piece : (k + 1) * piece, :]
        turned_ref[:, p * piece : (p + 1) * piece] = block.astype(f32).T.astype(bf16)


def d_kernel(where_ref, c0_ref, c1_ref, c2_ref, c3_ref, w_ref, d_ref):
    z, t = where_ref[0], where_ref[1]
    dp, rows, depth = d_ref.shape
    tile = min(depth, 512)
    cot = jnp.concatenate([x[...] for x in (c0_ref, c1_ref, c2_ref, c3_ref)], axis=1)
    for i in range(depth // tile):
        cut = slice(i * tile, (i + 1) * tile)
        whole = jnp.concatenate([w_ref[t ^ j, cut, :] for j in range(w_ref.shape[0])], axis=1)
        part = dot(cot, whole, ((1,), (1,))).astype(bf16)
        for k in range(dp):
            d_ref[z ^ k, :, cut] = part[k * rows : (k + 1) * rows]


def token_copies(token_refs, tokens_ref, sems, cut, first):
    copies, row = [], 0
    for p, x in enumerate(token_refs):
        rows = x.shape[0]
        copies.append(
            pltpu.make_async_copy(
                x.at[:, cut], tokens_ref.at[pl.ds(row, rows), cut], sems.at[first + p]
            )
        )
        row += rows
    return copies


def update_kernel(mark_ref, turned_ref, weights_ref, master_hbm, m_hbm, v_hbm, *rest, count, tile, layout):
    token_refs = rest[:count]
    new_hbm, part_refs, last_ref = rest[count], rest[count + 1 : -9], rest[-9]
    tokens, master, m, v, updated, new, sems, out_sems = rest[-8:]
    depth = master.shape[0]
    tiles = depth // tile
    each = count + 3
    groups = []
    for i in range(tiles):
        cut = pl.ds(i * tile, tile)
        group = token_copies(token_refs, tokens, sems, cut, i * each)
        for p, (source, target) in enumerate(((master_hbm, master), (m_hbm, m), (v_hbm, v))):
            group.append(
                pltpu.make_async_copy(
                    source.at[cut, :], target.at[cut, :], sems.at[i * each + count + p]
                )
            )
        for copy in group:
            copy.start()
        groups.append(group)
    outs = []
    for i in range(tiles):
        cut = slice(i * tile, (i + 1) * tile)
        for copy in groups[i]:
            copy.wait()
        grad = dot(turned_ref[...], tokens[:, cut], ((1,), (0,))).T
        m_new = beta_first * m[cut, :] + (1.0 - beta_first) * grad
        v_new = beta_second * v[cut, :] + (1.0 - beta_second) * grad * grad
        m_hat = m_new / (1.0 - beta_first**step_count)
        v_hat = v_new / (1.0 - beta_second**step_count)
        old = master[cut, :]
        master_new = old - learn_rate * (
            m_hat / (jnp.sqrt(v_hat) + adam_eps) + weight_decay * old
        )
        new[cut, :] = master_new
        out = pltpu.make_async_copy(
            new.at[pl.ds(i * tile, tile), :], new_hbm.at[pl.ds(i * tile, tile), :], out_sems.at[i]
        )
        out.start()
        outs.append(out)
        updated[cut, :] = master_new.astype(bf16)
    project(tokens, updated, part_refs, layout)
    late = [p for p, (k, _) in enumerate(layout) if k == 3]
    rows = tokens.shape[0] // len(layout)
    project(
        tokens.at[pl.ds(late[0] * rows, len(late) * rows), :],
        weights_ref,
        {3: last_ref},
        [layout[p] for p in late],
    )
    for out in outs:
        out.wait()


def project(tokens, weights, part_refs, layout):
    piece = tokens.shape[0] // len(layout)
    slot = {0: 0, 2: 1, 1: 2, 3: 3}
    p = 0
    while p < len(layout):
        k, j = layout[p]
        span = 2 if layout[p + 1 : p + 2] == ((k, j + 2),) else 1
        part_refs[k][slot[j] * piece : (slot[j] + span) * piece, :] = dot(
            tokens[p * piece : (p + span) * piece, :], weights[...], ((1,), (0,))
        ).astype(bf16)
        p += span


def project_kernel(weights_ref, *rest, count, layout):
    token_refs = rest[:count]
    part_refs, (tokens, sems) = rest[count:-2], rest[-2:]
    copies = token_copies(token_refs, tokens, sems, slice(None), 0)
    for copy in copies:
        copy.start()
    for copy in copies:
        copy.wait()
    project(tokens, weights_ref, part_refs, layout)


def reorder(blocks, me):
    bit = 1
    while bit < len(blocks):
        flip = (me & bit) != 0
        blocks = [jnp.where(flip, blocks[i ^ bit], blocks[i]) for i in range(len(blocks))]
        bit *= 2
    return blocks


def scatter_sum(parts, *earlier):
    got1, got3 = swap(parts[1], "dp", 1), swap(parts[3], "dp", 1)
    if earlier:
        got1, got3 = after([got1, got3], *earlier)
    mine = parts[0].astype(f32) + got1.astype(f32)
    other = (parts[2].astype(f32) + got3.astype(f32)).astype(bf16)
    return mine + swap(other, "dp", 2).astype(f32)


def shards(hidden_in, norm_gain, kv_cot, master_kv, moment_m, moment_v):
    dp, tensor = lax.axis_size("dp"), lax.axis_size("tensor")
    assert dp == 4 and tensor == 4
    z, t = lax.axis_index("dp"), lax.axis_index("tensor")
    where = jnp.stack([z, t]).astype(jnp.int32)
    _, micro, rows, width = hidden_in.shape
    piece = micro * rows
    hidden = hidden_in.reshape(piece, width)
    own_depth, cols = master_kv.shape[1:]
    depth = width // dp
    tile = min(piece, 16)

    w0 = master_kv[0].astype(bf16)
    whole_w = lax.all_to_all(
        jnp.broadcast_to(w0, (tensor, own_depth, cols)), "tensor", 0, 0, tiled=True
    )
    cot0 = kv_cot[0]
    cot2 = swap(cot0, "dp", 2)
    cot1 = swap(cot0, "dp", 1)
    cot3 = swap(cot2, "dp", 1)
    own = call(
        functools.partial(norm_kernel, tile=tile),
        [like(piece, depth)] * dp,
        [anywhere, anywhere, smem, vmem, vmem],
        [vmem] * dp,
        8,
        "norm",
    )(cot2, cot1, where, hidden, norm_gain)
    n1, n3 = swap(own[1], "dp", 1), swap(own[3], "dp", 3)
    n2 = swap(own[2], "dp", 2)
    layout = tuple((k, j) for k in range(dp) for j in (0, 2, 1, 3))
    *blocks, turned = call(
        functools.partial(arrange_kernel, dp=dp, layout=layout),
        [like(dp * piece, cols)] * tensor + [like(cols, dp * tensor * piece)],
        [anywhere, smem] + [vmem] * dp,
        [vmem] * (tensor + 1),
        8,
        "arrange",
    )(own[1], where, cot0, cot1, cot2, cot3)
    got1 = swap(blocks[1], "tensor", 1)
    got1, blocks[2], blocks[3] = after([got1, blocks[2], blocks[3]])
    mine_cot = [blocks[0], got1] + [swap(blocks[j], "tensor", j) for j in (2, 3)]
    d = call(
        d_kernel,
        like(dp, piece, depth),
        [smem] + [vmem] * 5,
        vmem,
        20,
        "d_normed",
    )(where, *mine_cot, whole_w)
    n1, n2, n3, d = after([n1, n2, n3, d])
    d = lax.all_to_all(d, "dp", 0, 0, tiled=True)
    tokens = []
    for x in (own[0], n1, n2, n3):
        across = swap(x, "tensor", 2)
        tokens += [x, across, swap(x, "tensor", 1), swap(across, "tensor", 1)]
    count = len(tokens)
    block = tensor * piece
    part_shape = [like(block, cols)] * dp
    step = min(own_depth, 512)
    tiles = own_depth // step
    whole = pltpu.VMEM((own_depth, cols), f32)
    all_tokens = pltpu.VMEM((dp * block, depth), bf16)
    early = count * 3 // 4
    own_parts = call(
        functools.partial(project_kernel, count=early, layout=layout[: 3 * tensor]),
        part_shape[:3],
        [vmem] + [anywhere] * early,
        [vmem] * 3,
        16,
        "project",
        scratch=[
            pltpu.VMEM((3 * block, depth), bf16),
            pltpu.SemaphoreType.DMA((early,)),
        ],
    )(w0, *tokens[:early])
    master_new, *parts, last = call(
        functools.partial(update_kernel, count=count, tile=step, layout=layout),
        [like(own_depth, cols, dtype=f32)] + part_shape + part_shape[:1],
        [anywhere, vmem, vmem] + [anywhere] * (3 + count),
        [anywhere] + [vmem] * (dp + 1),
        24,
        "update",
        scratch=[
            all_tokens,
            whole,
            whole,
            whole,
            pltpu.VMEM((own_depth, cols), bf16),
            whole,
            pltpu.SemaphoreType.DMA((tiles * (count + 3),)),
            pltpu.SemaphoreType.DMA((tiles,)),
        ],
    )(own_parts[0], turned, w0, master_kv[0], moment_m[0], moment_v[0], *tokens)

    def place(x):
        x = x.reshape(tensor, micro, rows, cols)
        return jnp.stack(reorder([x[j] for j in (0, 2, 1, 3)], t), 1).reshape(
            1, micro, tensor * rows, cols
        )

    mine = place(scatter_sum(parts).astype(bf16))
    kv_next = from_behind(mine, "segment", -1)
    kv_own = place(scatter_sum([*own_parts, last]).astype(bf16))
    (d,) = after([d], mine, kv_own)
    grad_in = call(
        functools.partial(grad_kernel, tile=tile),
        like(piece, width),
        [vmem] * 3,
        vmem,
        12,
        "grad_in",
    )(hidden, norm_gain, d)
    return (kv_own, grad_in.reshape(hidden_in.shape), master_new[None], kv_next)


def solution(mesh):
    in_specs = (
        P("segment", None, ("dp", "tensor"), None),
        P("segment", None),
        P("segment", None, "dp", "tensor"),
        P("segment", "dp", "tensor"),
        P("segment", "dp", "tensor"),
        P("segment", "dp", "tensor"),
    )
    out_specs = (
        P("segment", None, "dp", "tensor"),
        P("segment", None, ("dp", "tensor"), None),
        P("segment", "dp", "tensor"),
        P("segment", None, "dp", "tensor"),
    )
    return jax.shard_map(shards, mesh=mesh, in_specs=in_specs, out_specs=out_specs, check_vma=False)
```

```python
import functools

import jax
import jax.numpy as jnp
from jax import lax
from jax.experimental import pallas as pl
from jax.experimental.pallas import tpu as pltpu
from jax.sharding import PartitionSpec as P

beta_first = 0.9
beta_second = 0.95
learn_rate = 0.03
weight_decay = 0.1
adam_eps = 1e-08
norm_eps = 1e-05
step_count = 20.0

f32 = jnp.float32
bf16 = jnp.bfloat16

vmem = pl.BlockSpec(memory_space=pltpu.VMEM)
smem = pl.BlockSpec(memory_space=pltpu.SMEM)
anywhere = pl.BlockSpec(memory_space=pl.ANY)
light = pl.CostEstimate(flops=1000, bytes_accessed=1000, transcendentals=0)


def swap(x, axis, bits):
    peers = lax.axis_size(axis)
    return lax.ppermute(x, axis, [(i, i ^ bits) for i in range(peers)])


def from_behind(x, axis, by):
    peers = lax.axis_size(axis)
    return lax.ppermute(x, axis, [(i, (i + by) % peers) for i in range(peers)])


def dot(a, b, contract):
    return lax.dot_general(a, b, (contract, ((), ())), preferred_element_type=f32)


def like(*shape, dtype=bf16):
    return jax.ShapeDtypeStruct(shape, dtype)


def call(body, out_shape, in_specs, out_specs, mib, name, scratch=(), **more):
    return pl.pallas_call(
        body,
        out_shape=out_shape,
        in_specs=in_specs,
        out_specs=out_specs,
        scratch_shapes=list(scratch),
        compiler_params=pltpu.CompilerParams(vmem_limit_bytes=int(mib * 1024 * 1024)),
        cost_estimate=light,
        name=name,
        **more,
    )


def after(values, *earlier):
    tied = call(
        lambda *refs: None,
        [like(*x.shape, dtype=x.dtype) for x in values],
        [anywhere] * (len(values) + len(earlier)),
        [anywhere] * len(values),
        0.25,
        "after",
        input_output_aliases={i: i for i in range(len(values))},
    )(*values, *earlier)
    return list(tied)


def lanes(index, size):
    return pl.ds(pl.multiple_of(index * size, size), size)


def norm_kernel(where_ref, hidden_ref, gain_ref, *own_refs, tile):
    z = where_ref[0]
    rows, width = hidden_ref.shape
    depth = width // len(own_refs)

    @pl.loop(0, rows // tile)
    def _(i):
        at = pl.ds(pl.multiple_of(i * tile, tile), tile)
        total = jnp.zeros((tile, 1), f32)
        for k in range(len(own_refs)):
            part = hidden_ref[at, k * depth : (k + 1) * depth].astype(f32)
            total += jnp.sum(part * part, axis=-1, keepdims=True)
        scaling = lax.rsqrt(total * (1.0 / width) + norm_eps)
        for k, own_ref in enumerate(own_refs):
            cut = lanes(z ^ k, depth)
            own_ref[at, :] = (
                hidden_ref[at, cut].astype(f32) * scaling * gain_ref[:, cut]
            ).astype(bf16)


def grad_kernel(hidden_ref, gain_ref, d_ref, out_ref, *, tile):
    rows, width = hidden_ref.shape
    blocks = d_ref.shape[0]
    depth = width // blocks

    @pl.loop(0, rows // tile)
    def _(i):
        at = pl.ds(pl.multiple_of(i * tile, tile), tile)
        squares = jnp.zeros((tile, 1), f32)
        cross = jnp.zeros((tile, 1), f32)
        for k in range(blocks):
            cut = slice(k * depth, (k + 1) * depth)
            hidden = hidden_ref[at, cut].astype(f32)
            squares += jnp.sum(hidden * hidden, axis=-1, keepdims=True)
            upper = d_ref[k, at, :].astype(f32) * gain_ref[:, cut]
            cross += jnp.sum(upper * hidden, axis=-1, keepdims=True)
        scaling = lax.rsqrt(squares * (1.0 / width) + norm_eps)
        factor = scaling * scaling * scaling * (cross * (1.0 / width))
        for k in range(blocks):
            cut = slice(k * depth, (k + 1) * depth)
            upper = d_ref[k, at, :].astype(f32) * gain_ref[:, cut]
            hidden = hidden_ref[at, cut].astype(f32)
            out_ref[at, cut] = (scaling * upper - hidden * factor).astype(bf16)


def arrange_kernel(mark_ref, where_ref, *refs, dp, layout):
    cots, send_refs, turned_ref = refs[:dp], refs[dp:-1], refs[-1]
    t = where_ref[1]
    tensor = len(send_refs)
    micro, rows, cols = cots[0].shape
    rows //= tensor
    piece = micro * rows
    for j, send_ref in enumerate(send_refs):
        at = pl.ds(pl.multiple_of((t ^ j) * rows, rows), rows)
        for k in range(dp):
            for m in range(micro):
                start = k * piece + m * rows
                send_ref[start : start + rows, :] = cots[k][m, at, :]
    for p, (k, j) in enumerate(layout):
        block = send_refs[j][k * piece : (k + 1) * piece, :]
        turned_ref[:, p * piece : (p + 1) * piece] = block.astype(f32).T.astype(bf16)


def d_kernel(where_ref, c0_ref, c1_ref, c2_ref, c3_ref, w_ref, d_ref):
    z, t = where_ref[0], where_ref[1]
    dp, rows, depth = d_ref.shape
    tile = min(depth, 512)
    cot = jnp.concatenate([x[...] for x in (c0_ref, c1_ref, c2_ref, c3_ref)], axis=1)
    for i in range(depth // tile):
        cut = slice(i * tile, (i + 1) * tile)
        whole = jnp.concatenate([w_ref[t ^ j, cut, :] for j in range(w_ref.shape[0])], axis=1)
        part = dot(cot, whole, ((1,), (1,))).astype(bf16)
        for k in range(dp):
            d_ref[z ^ k, :, cut] = part[k * rows : (k + 1) * rows]


def pack_kernel(*refs):
    pieces, packed_ref, sem = refs[:-2], refs[-2], refs[-1]
    rows = pieces[0].shape[0]
    copies = [
        pltpu.make_async_copy(x, packed_ref.at[pl.ds(p * rows, rows), :], sem.at[p])
        for p, x in enumerate(pieces)
    ]
    for copy in copies:
        copy.start()
    for copy in copies:
        copy.wait()


def token_copies(token_refs, tokens_ref, sems, cut, first):
    copies, row = [], 0
    for p, x in enumerate(token_refs):
        rows = x.shape[0]
        copies.append(
            pltpu.make_async_copy(
                x.at[:, cut], tokens_ref.at[pl.ds(row, rows), cut], sems.at[first + p]
            )
        )
        row += rows
    return copies


def update_kernel(turned_ref, master_hbm, m_hbm, v_hbm, *rest, count, tile, layout):
    token_refs = rest[:count]
    new_hbm, part_refs = rest[count], rest[count + 1 : -8]
    tokens, master, m, v, updated, new, sems, out_sems = rest[-8:]
    depth = master.shape[0]
    tiles = depth // tile
    each = count + 3
    groups = []
    for i in range(tiles):
        cut = pl.ds(i * tile, tile)
        group = token_copies(token_refs, tokens, sems, cut, i * each)
        for p, (source, target) in enumerate(((master_hbm, master), (m_hbm, m), (v_hbm, v))):
            group.append(
                pltpu.make_async_copy(
                    source.at[cut, :], target.at[cut, :], sems.at[i * each + count + p]
                )
            )
        for copy in group:
            copy.start()
        groups.append(group)
    outs = []
    for i in range(tiles):
        cut = slice(i * tile, (i + 1) * tile)
        for copy in groups[i]:
            copy.wait()
        grad = dot(turned_ref[...], tokens[:, cut], ((1,), (0,))).T
        m_new = beta_first * m[cut, :] + (1.0 - beta_first) * grad
        v_new = beta_second * v[cut, :] + (1.0 - beta_second) * grad * grad
        m_hat = m_new / (1.0 - beta_first**step_count)
        v_hat = v_new / (1.0 - beta_second**step_count)
        old = master[cut, :]
        master_new = old - learn_rate * (
            m_hat / (jnp.sqrt(v_hat) + adam_eps) + weight_decay * old
        )
        new[cut, :] = master_new
        out = pltpu.make_async_copy(
            new.at[pl.ds(i * tile, tile), :], new_hbm.at[pl.ds(i * tile, tile), :], out_sems.at[i]
        )
        out.start()
        outs.append(out)
        updated[cut, :] = master_new.astype(bf16)
    project(tokens, updated, part_refs, layout)
    for out in outs:
        out.wait()


def project(tokens, weights, part_refs, layout):
    piece = tokens.shape[0] // len(layout)
    slot = {0: 0, 2: 1, 1: 2, 3: 3}
    p = 0
    while p < len(layout):
        k, j = layout[p]
        span = 2 if layout[p + 1 : p + 2] == ((k, j + 2),) else 1
        part_refs[k][slot[j] * piece : (slot[j] + span) * piece, :] = dot(
            tokens[p * piece : (p + span) * piece, :], weights[...], ((1,), (0,))
        ).astype(bf16)
        p += span


def project_kernel(mark_ref, weights_ref, *rest, count, layout):
    token_refs = rest[:count]
    part_refs, (tokens, sems) = rest[count:-2], rest[-2:]
    copies = token_copies(token_refs, tokens, sems, slice(None), 0)
    for copy in copies:
        copy.start()
    for copy in copies:
        copy.wait()
    project(tokens, weights_ref, part_refs, layout)


def reorder(blocks, me):
    bit = 1
    while bit < len(blocks):
        flip = (me & bit) != 0
        blocks = [jnp.where(flip, blocks[i ^ bit], blocks[i]) for i in range(len(blocks))]
        bit *= 2
    return blocks


def scatter_sum(parts, got1, got3):
    mine = parts[0].astype(f32) + got1.astype(f32)
    other = (parts[2].astype(f32) + got3.astype(f32)).astype(bf16)
    return mine + swap(other, "dp", 2).astype(f32)


def shards(hidden_in, norm_gain, kv_cot, master_kv, moment_m, moment_v):
    dp, tensor = lax.axis_size("dp"), lax.axis_size("tensor")
    assert dp == 4 and tensor == 4
    z, t = lax.axis_index("dp"), lax.axis_index("tensor")
    where = jnp.stack([z, t]).astype(jnp.int32)
    _, micro, rows, width = hidden_in.shape
    piece = micro * rows
    hidden = hidden_in.reshape(piece, width)
    own_depth, cols = master_kv.shape[1:]
    depth = width // dp
    tile = min(piece, 16)

    w0 = master_kv[0].astype(bf16)
    whole_w = lax.all_to_all(
        jnp.broadcast_to(w0, (tensor, own_depth, cols)), "tensor", 0, 0, tiled=True
    )
    cot0 = kv_cot[0]
    cot2 = swap(cot0, "dp", 2)
    cot1 = swap(cot0, "dp", 1)
    cot3 = swap(cot2, "dp", 1)
    own = call(
        functools.partial(norm_kernel, tile=tile),
        [like(piece, depth)] * dp,
        [smem, vmem, vmem],
        [vmem] * dp,
        8,
        "norm",
    )(where, hidden, norm_gain)
    n1, n3 = swap(own[1], "dp", 1), swap(own[3], "dp", 3)
    n2 = swap(own[2], "dp", 2)
    layout = tuple(
        (k, j) for group in ((0,), (1, 2), (3,)) for j in (0, 2, 1, 3) for k in group
    )
    across0 = swap(own[0], "tensor", 2)
    *blocks, turned = call(
        functools.partial(arrange_kernel, dp=dp, layout=layout),
        [like(dp * piece, cols)] * tensor + [like(cols, dp * tensor * piece)],
        [anywhere, smem] + [vmem] * dp,
        [vmem] * (tensor + 1),
        8,
        "arrange",
    )(across0, where, cot0, cot1, cot2, cot3)
    mine_cot = [blocks[0]] + [swap(blocks[j], "tensor", j) for j in range(1, tensor)]
    n1, n2, n3, mine_cot[0] = after([n1, n2, n3, mine_cot[0]], *mine_cot[2:])
    d = call(
        d_kernel,
        like(dp, piece, depth),
        [smem] + [vmem] * 5,
        vmem,
        20,
        "d_normed",
    )(where, *mine_cot, whole_w)
    d = lax.all_to_all(d, "dp", 0, 0, tiled=True)

    def pack(*pieces):
        return call(
            pack_kernel,
            like(len(pieces) * piece, depth),
            [anywhere] * len(pieces),
            anywhere,
            0.25,
            "pack",
            scratch=[pltpu.SemaphoreType.DMA((len(pieces),))],
        )(*pieces)

    tokens = []
    for x in (own[0], pack(n1, n2), n3):
        across = swap(x, "tensor", 2) if tokens else across0
        tokens += [x, across, swap(x, "tensor", 1), swap(across, "tensor", 1)]
    count = len(tokens)
    block = tensor * piece
    part_shape = [like(block, cols)] * dp
    step = min(own_depth, 512)
    tiles = own_depth // step
    whole = pltpu.VMEM((own_depth, cols), f32)
    all_tokens = pltpu.VMEM((dp * block, depth), bf16)
    master_new, *parts = call(
        functools.partial(update_kernel, count=count, tile=step, layout=layout),
        [like(own_depth, cols, dtype=f32)] + part_shape,
        [vmem] + [anywhere] * (3 + count),
        [anywhere] + [vmem] * dp,
        24,
        "update",
        scratch=[
            all_tokens,
            whole,
            whole,
            whole,
            pltpu.VMEM((own_depth, cols), bf16),
            whole,
            pltpu.SemaphoreType.DMA((tiles * (count + 3),)),
            pltpu.SemaphoreType.DMA((tiles,)),
        ],
    )(turned, master_kv[0], moment_m[0], moment_v[0], *tokens)

    def place(x):
        x = x.reshape(tensor, micro, rows, cols)
        return jnp.stack(reorder([x[j] for j in (0, 2, 1, 3)], t), 1).reshape(
            1, micro, tensor * rows, cols
        )

    got1, got3 = swap(parts[1], "dp", 1), swap(parts[3], "dp", 1)
    mine = place(scatter_sum(parts, got1, got3).astype(bf16))
    kv_next = from_behind(mine, "segment", -1)
    own_parts = call(
        functools.partial(project_kernel, count=count, layout=layout),
        part_shape,
        [anywhere, vmem] + [anywhere] * count,
        [vmem] * dp,
        16,
        "project",
        scratch=[all_tokens, pltpu.SemaphoreType.DMA((count,))],
    )(got1, w0, *tokens)
    own_got1, own_got3 = swap(own_parts[1], "dp", 1), swap(own_parts[3], "dp", 1)
    kv_own = place(scatter_sum(own_parts, own_got1, own_got3).astype(bf16))
    (d,) = after([d], mine, kv_own)
    grad_in = call(
        functools.partial(grad_kernel, tile=tile),
        like(piece, width),
        [vmem] * 3,
        vmem,
        12,
        "grad_in",
    )(hidden, norm_gain, d)
    return (kv_own, grad_in.reshape(hidden_in.shape), master_new[None], kv_next)


def solution(mesh):
    in_specs = (
        P("segment", None, ("dp", "tensor"), None),
        P("segment", None),
        P("segment", None, "dp", "tensor"),
        P("segment", "dp", "tensor"),
        P("segment", "dp", "tensor"),
        P("segment", "dp", "tensor"),
    )
    out_specs = (
        P("segment", None, "dp", "tensor"),
        P("segment", None, ("dp", "tensor"), None),
        P("segment", "dp", "tensor"),
        P("segment", None, "dp", "tensor"),
    )
    return jax.shard_map(shards, mesh=mesh, in_specs=in_specs, out_specs=out_specs, check_vma=False)
```

```python
import functools

import jax
import jax.numpy as jnp
from jax import lax
from jax.experimental import pallas as pl
from jax.experimental.pallas import tpu as pltpu
from jax.sharding import PartitionSpec as P

beta_first = 0.9
beta_second = 0.95
learn_rate = 0.03
weight_decay = 0.1
adam_eps = 1e-08
norm_eps = 1e-05
step_count = 20.0

f32 = jnp.float32
bf16 = jnp.bfloat16

vmem = pl.BlockSpec(memory_space=pltpu.VMEM)
smem = pl.BlockSpec(memory_space=pltpu.SMEM)
anywhere = pl.BlockSpec(memory_space=pl.ANY)
light = pl.CostEstimate(flops=1000, bytes_accessed=1000, transcendentals=0)


def swap(x, axis, bits):
    peers = lax.axis_size(axis)
    return lax.ppermute(x, axis, [(i, i ^ bits) for i in range(peers)])


def from_behind(x, axis, by):
    peers = lax.axis_size(axis)
    return lax.ppermute(x, axis, [(i, (i + by) % peers) for i in range(peers)])


def dot(a, b, contract):
    return lax.dot_general(a, b, (contract, ((), ())), preferred_element_type=f32)


def like(*shape, dtype=bf16):
    return jax.ShapeDtypeStruct(shape, dtype)


def call(body, out_shape, in_specs, out_specs, mib, name, scratch=(), cost=light, **more):
    return pl.pallas_call(
        body,
        out_shape=out_shape,
        in_specs=in_specs,
        out_specs=out_specs,
        scratch_shapes=list(scratch),
        compiler_params=pltpu.CompilerParams(vmem_limit_bytes=int(mib * 1024 * 1024)),
        cost_estimate=cost,
        name=name,
        **more,
    )


def after(values, *earlier):
    tied = call(
        lambda *refs: None,
        [like(*x.shape, dtype=x.dtype) for x in values],
        [anywhere] * (len(values) + len(earlier)),
        [anywhere] * len(values),
        0.25,
        "after",
        input_output_aliases={i: i for i in range(len(values))},
    )(*values, *earlier)
    return list(tied)


def lanes(index, size):
    return pl.ds(pl.multiple_of(index * size, size), size)


def norm_kernel(where_ref, hidden_ref, gain_ref, *own_refs, tile):
    z = where_ref[0]
    rows, width = hidden_ref.shape
    depth = width // len(own_refs)

    @pl.loop(0, rows // tile)
    def _(i):
        at = pl.ds(pl.multiple_of(i * tile, tile), tile)
        total = jnp.zeros((tile, 1), f32)
        for k in range(len(own_refs)):
            part = hidden_ref[at, k * depth : (k + 1) * depth].astype(f32)
            total += jnp.sum(part * part, axis=-1, keepdims=True)
        scaling = lax.rsqrt(total * (1.0 / width) + norm_eps)
        for k, own_ref in enumerate(own_refs):
            cut = lanes(z ^ k, depth)
            own_ref[at, :] = (
                hidden_ref[at, cut].astype(f32) * scaling * gain_ref[:, cut]
            ).astype(bf16)


def grad_kernel(hidden_ref, gain_ref, d_ref, out_ref, *, tile):
    rows, width = hidden_ref.shape
    blocks = d_ref.shape[0]
    depth = width // blocks

    @pl.loop(0, rows // tile)
    def _(i):
        at = pl.ds(pl.multiple_of(i * tile, tile), tile)
        squares = jnp.zeros((tile, 1), f32)
        cross = jnp.zeros((tile, 1), f32)
        for k in range(blocks):
            cut = slice(k * depth, (k + 1) * depth)
            hidden = hidden_ref[at, cut].astype(f32)
            squares += jnp.sum(hidden * hidden, axis=-1, keepdims=True)
            upper = d_ref[k, at, :].astype(f32) * gain_ref[:, cut]
            cross += jnp.sum(upper * hidden, axis=-1, keepdims=True)
        scaling = lax.rsqrt(squares * (1.0 / width) + norm_eps)
        factor = scaling * scaling * scaling * (cross * (1.0 / width))
        for k in range(blocks):
            cut = slice(k * depth, (k + 1) * depth)
            upper = d_ref[k, at, :].astype(f32) * gain_ref[:, cut]
            hidden = hidden_ref[at, cut].astype(f32)
            out_ref[at, cut] = (scaling * upper - hidden * factor).astype(bf16)


def arrange_kernel(mark_ref, where_ref, *refs, dp, layout):
    cots, send_refs, turned_ref = refs[:dp], refs[dp:-1], refs[-1]
    t = where_ref[1]
    tensor = len(send_refs)
    micro, rows, cols = cots[0].shape
    rows //= tensor
    piece = micro * rows
    for j, send_ref in enumerate(send_refs):
        at = pl.ds(pl.multiple_of((t ^ j) * rows, rows), rows)
        for k in range(dp):
            for m in range(micro):
                start = k * piece + m * rows
                send_ref[start : start + rows, :] = cots[k][m, at, :]
    for p, (k, j) in enumerate(layout):
        block = send_refs[j][k * piece : (k + 1) * piece, :]
        turned_ref[:, p * piece : (p + 1) * piece] = block.astype(f32).T.astype(bf16)


def d_kernel(where_ref, c0_ref, c1_ref, c2_ref, c3_ref, w_ref, d_ref):
    z, t = where_ref[0], where_ref[1]
    dp, rows, depth = d_ref.shape
    tile = min(depth, 512)
    cot = jnp.concatenate([x[...] for x in (c0_ref, c1_ref, c2_ref, c3_ref)], axis=1)
    for i in range(depth // tile):
        cut = slice(i * tile, (i + 1) * tile)
        whole = jnp.concatenate([w_ref[t ^ j, cut, :] for j in range(w_ref.shape[0])], axis=1)
        part = dot(cot, whole, ((1,), (1,))).astype(bf16)
        for k in range(dp):
            d_ref[z ^ k, :, cut] = part[k * rows : (k + 1) * rows]


def pack_kernel(*refs):
    pieces, packed_ref, sem = refs[:-2], refs[-2], refs[-1]
    rows = pieces[0].shape[0]
    copies = [
        pltpu.make_async_copy(x, packed_ref.at[pl.ds(p * rows, rows), :], sem.at[p])
        for p, x in enumerate(pieces)
    ]
    for copy in copies:
        copy.start()
    for copy in copies:
        copy.wait()


def token_copies(token_refs, tokens_ref, sems, cut, first):
    copies, row = [], 0
    for p, x in enumerate(token_refs):
        rows = x.shape[0]
        copies.append(
            pltpu.make_async_copy(
                x.at[:, cut], tokens_ref.at[pl.ds(row, rows), cut], sems.at[first + p]
            )
        )
        row += rows
    return copies


def update_kernel(turned_ref, weights_ref, master_hbm, m_hbm, v_hbm, *rest, count, tile, layout):
    token_refs = rest[:count]
    new_hbm, part_refs = rest[count], rest[count + 1 : -8]
    part_refs, own_refs = part_refs[:4], part_refs[4:]
    tokens, master, m, v, updated, new, sems, out_sems = rest[-8:]
    depth = master.shape[0]
    tiles = depth // tile
    each = count + 3
    groups = []
    for i in range(tiles):
        cut = pl.ds(i * tile, tile)
        group = token_copies(token_refs, tokens, sems, cut, i * each)
        for p, (source, target) in enumerate(((master_hbm, master), (m_hbm, m), (v_hbm, v))):
            group.append(
                pltpu.make_async_copy(
                    source.at[cut, :], target.at[cut, :], sems.at[i * each + count + p]
                )
            )
        for copy in group:
            copy.start()
        groups.append(group)
    outs = []
    for i in range(tiles):
        cut = slice(i * tile, (i + 1) * tile)
        for copy in groups[i]:
            copy.wait()
        grad = dot(turned_ref[...], tokens[:, cut], ((1,), (0,))).T
        m_new = beta_first * m[cut, :] + (1.0 - beta_first) * grad
        v_new = beta_second * v[cut, :] + (1.0 - beta_second) * grad * grad
        m_hat = m_new / (1.0 - beta_first**step_count)
        v_hat = v_new / (1.0 - beta_second**step_count)
        old = master[cut, :]
        master_new = old - learn_rate * (
            m_hat / (jnp.sqrt(v_hat) + adam_eps) + weight_decay * old
        )
        new[cut, :] = master_new
        out = pltpu.make_async_copy(
            new.at[pl.ds(i * tile, tile), :], new_hbm.at[pl.ds(i * tile, tile), :], out_sems.at[i]
        )
        out.start()
        outs.append(out)
        updated[cut, :] = master_new.astype(bf16)
    project(tokens, updated, part_refs, layout)
    project(tokens, weights_ref, own_refs, layout)
    for out in outs:
        out.wait()


def project(tokens, weights, part_refs, layout):
    piece = tokens.shape[0] // len(layout)
    slot = {0: 0, 2: 1, 1: 2, 3: 3}
    p = 0
    while p < len(layout):
        k, j = layout[p]
        span = 2 if layout[p + 1 : p + 2] == ((k, j + 2),) else 1
        part_refs[k][slot[j] * piece : (slot[j] + span) * piece, :] = dot(
            tokens[p * piece : (p + span) * piece, :], weights[...], ((1,), (0,))
        ).astype(bf16)
        p += span


def reorder(blocks, me):
    bit = 1
    while bit < len(blocks):
        flip = (me & bit) != 0
        blocks = [jnp.where(flip, blocks[i ^ bit], blocks[i]) for i in range(len(blocks))]
        bit *= 2
    return blocks


def scatter_sum(parts, got1, got3):
    mine = parts[0].astype(f32) + got1.astype(f32)
    other = (parts[2].astype(f32) + got3.astype(f32)).astype(bf16)
    return mine + swap(other, "dp", 2).astype(f32)


def shards(hidden_in, norm_gain, kv_cot, master_kv, moment_m, moment_v):
    dp, tensor = lax.axis_size("dp"), lax.axis_size("tensor")
    assert dp == 4 and tensor == 4
    z, t = lax.axis_index("dp"), lax.axis_index("tensor")
    where = jnp.stack([z, t]).astype(jnp.int32)
    _, micro, rows, width = hidden_in.shape
    piece = micro * rows
    hidden = hidden_in.reshape(piece, width)
    own_depth, cols = master_kv.shape[1:]
    depth = width // dp
    tile = min(piece, 16)

    w0 = master_kv[0].astype(bf16)
    whole_w = lax.all_to_all(
        jnp.broadcast_to(w0, (tensor, own_depth, cols)), "tensor", 0, 0, tiled=True
    )
    cot0 = kv_cot[0]
    cot2 = swap(cot0, "dp", 2)
    cot1 = swap(cot0, "dp", 1)
    cot3 = swap(cot0, "dp", 3)
    own = call(
        functools.partial(norm_kernel, tile=tile),
        [like(piece, depth)] * dp,
        [smem, vmem, vmem],
        [vmem] * dp,
        8,
        "norm",
    )(where, hidden, norm_gain)
    own = list(own)
    own[2], own[3] = after([own[2], own[3]], cot1)
    n1, n3 = swap(own[1], "dp", 1), swap(own[3], "dp", 3)
    n2 = swap(own[2], "dp", 2)
    layout = tuple(
        (k, j) for group in ((0,), (1, 2), (3,)) for j in (0, 2, 1, 3) for k in group
    )
    across0 = swap(own[0], "tensor", 2)
    *blocks, turned = call(
        functools.partial(arrange_kernel, dp=dp, layout=layout),
        [like(dp * piece, cols)] * tensor + [like(cols, dp * tensor * piece)],
        [anywhere, smem] + [vmem] * dp,
        [vmem] * (tensor + 1),
        8,
        "arrange",
    )(across0, where, cot0, cot1, cot2, cot3)
    mine_cot = [blocks[0]] + [swap(blocks[j], "tensor", j) for j in range(1, tensor)]
    n1, n2, n3, mine_cot[0] = after([n1, n2, n3, mine_cot[0]], *mine_cot[2:])
    d = call(
        d_kernel,
        like(dp, piece, depth),
        [smem] + [vmem] * 5,
        vmem,
        60,
        "d_normed",
    )(where, *mine_cot, whole_w)
    d = lax.all_to_all(d, "dp", 0, 0, tiled=True)

    def pack(*pieces):
        return call(
            pack_kernel,
            like(len(pieces) * piece, depth),
            [anywhere] * len(pieces),
            anywhere,
            0.25,
            "pack",
            scratch=[pltpu.SemaphoreType.DMA((len(pieces),))],
        )(*pieces)

    tokens = []
    for x in (own[0], pack(n1, n2), n3):
        across = swap(x, "tensor", 2) if tokens else across0
        tokens += [x, across, swap(x, "tensor", 1), swap(across, "tensor", 1)]
    count = len(tokens)
    block = tensor * piece
    part_shape = [like(block, cols)] * dp
    step = min(own_depth, 512)
    tiles = own_depth // step
    whole = pltpu.VMEM((own_depth, cols), f32)
    all_tokens = pltpu.VMEM((dp * block, depth), bf16)
    master_new, *parts = call(
        functools.partial(update_kernel, count=count, tile=step, layout=layout),
        [like(own_depth, cols, dtype=f32)] + part_shape * 2,
        [vmem] * 2 + [anywhere] * (3 + count),
        [anywhere] + [vmem] * (2 * dp),
        60,
        "update",
        scratch=[
            all_tokens,
            whole,
            whole,
            whole,
            pltpu.VMEM((own_depth, cols), bf16),
            whole,
            pltpu.SemaphoreType.DMA((tiles * (count + 3),)),
            pltpu.SemaphoreType.DMA((tiles,)),
        ],
    )(turned, w0, master_kv[0], moment_m[0], moment_v[0], *tokens)

    def place(x):
        x = x.reshape(tensor, micro, rows, cols)
        return jnp.stack(reorder([x[j] for j in (0, 2, 1, 3)], t), 1).reshape(
            1, micro, tensor * rows, cols
        )

    got1, got3 = swap(parts[1], "dp", 1), swap(parts[3], "dp", 1)
    mine = place(scatter_sum(parts, got1, got3).astype(bf16))
    kv_next = from_behind(mine, "segment", -1)
    parts, own_parts = parts[:dp], parts[dp:]
    own_parts[1], own_parts[3] = after([own_parts[1], own_parts[3]], got1, got3)
    own_got1, own_got3 = swap(own_parts[1], "dp", 1), swap(own_parts[3], "dp", 1)
    kv_own = place(scatter_sum(own_parts, own_got1, own_got3).astype(bf16))
    (d,) = after([d], mine)
    grad_in = call(
        functools.partial(grad_kernel, tile=tile),
        like(piece, width),
        [vmem] * 3,
        vmem,
        60,
        "grad_in",
        cost=pl.CostEstimate(
            flops=20 * piece * width, bytes_accessed=6 * piece * width, transcendentals=0
        ),
    )(hidden, norm_gain, d)
    (kv_next,) = after([kv_next], grad_in[:16, :128])
    return (kv_own, grad_in.reshape(hidden_in.shape), master_new[None], kv_next)


def solution(mesh):
    in_specs = (
        P("segment", None, ("dp", "tensor"), None),
        P("segment", None),
        P("segment", None, "dp", "tensor"),
        P("segment", "dp", "tensor"),
        P("segment", "dp", "tensor"),
        P("segment", "dp", "tensor"),
    )
    out_specs = (
        P("segment", None, "dp", "tensor"),
        P("segment", None, ("dp", "tensor"), None),
        P("segment", "dp", "tensor"),
        P("segment", None, "dp", "tensor"),
    )
    return jax.shard_map(shards, mesh=mesh, in_specs=in_specs, out_specs=out_specs, check_vma=False)
```

```python
import functools

import jax
import jax.numpy as jnp
from jax import lax
from jax.experimental import pallas as pl
from jax.experimental.pallas import tpu as pltpu
from jax.sharding import PartitionSpec as P

beta_first = 0.9
beta_second = 0.95
learn_rate = 0.03
weight_decay = 0.1
adam_eps = 1e-08
norm_eps = 1e-05
step_count = 20.0

f32 = jnp.float32
bf16 = jnp.bfloat16

vmem = pl.BlockSpec(memory_space=pltpu.VMEM)
smem = pl.BlockSpec(memory_space=pltpu.SMEM)
anywhere = pl.BlockSpec(memory_space=pl.ANY)
light = pl.CostEstimate(flops=1000, bytes_accessed=1000, transcendentals=0)


def swap(x, axis, bits):
    peers = lax.axis_size(axis)
    return lax.ppermute(x, axis, [(i, i ^ bits) for i in range(peers)])


def from_behind(x, axis, by):
    peers = lax.axis_size(axis)
    return lax.ppermute(x, axis, [(i, (i + by) % peers) for i in range(peers)])


def dot(a, b, contract):
    return lax.dot_general(a, b, (contract, ((), ())), preferred_element_type=f32)


def like(*shape, dtype=bf16):
    return jax.ShapeDtypeStruct(shape, dtype)


def call(body, out_shape, in_specs, out_specs, mib, name, scratch=(), **more):
    return pl.pallas_call(
        body,
        out_shape=out_shape,
        in_specs=in_specs,
        out_specs=out_specs,
        scratch_shapes=list(scratch),
        compiler_params=pltpu.CompilerParams(vmem_limit_bytes=int(mib * 1024 * 1024)),
        cost_estimate=light,
        name=name,
        **more,
    )


def after(values, *earlier):
    tied = call(
        lambda *refs: None,
        [like(*x.shape, dtype=x.dtype) for x in values],
        [anywhere] * (len(values) + len(earlier)),
        [anywhere] * len(values),
        0.25,
        "after",
        input_output_aliases={i: i for i in range(len(values))},
    )(*values, *earlier)
    return list(tied)


def lanes(index, size):
    return pl.ds(pl.multiple_of(index * size, size), size)


def norm_kernel(mark_ref, other_ref, where_ref, hidden_ref, gain_ref, *own_refs, tile):
    z = where_ref[0]
    rows, width = hidden_ref.shape
    depth = width // len(own_refs)

    @pl.loop(0, rows // tile)
    def _(i):
        at = pl.ds(pl.multiple_of(i * tile, tile), tile)
        total = jnp.zeros((tile, 1), f32)
        for k in range(len(own_refs)):
            part = hidden_ref[at, k * depth : (k + 1) * depth].astype(f32)
            total += jnp.sum(part * part, axis=-1, keepdims=True)
        scaling = lax.rsqrt(total * (1.0 / width) + norm_eps)
        for k, own_ref in enumerate(own_refs):
            cut = lanes(z ^ k, depth)
            own_ref[at, :] = (
                hidden_ref[at, cut].astype(f32) * scaling * gain_ref[:, cut]
            ).astype(bf16)


def grad_kernel(hidden_ref, gain_ref, d_ref, out_ref, *, tile):
    rows, width = hidden_ref.shape
    blocks = d_ref.shape[0]
    depth = width // blocks

    @pl.loop(0, rows // tile)
    def _(i):
        at = pl.ds(pl.multiple_of(i * tile, tile), tile)
        squares = jnp.zeros((tile, 1), f32)
        cross = jnp.zeros((tile, 1), f32)
        for k in range(blocks):
            cut = slice(k * depth, (k + 1) * depth)
            hidden = hidden_ref[at, cut].astype(f32)
            squares += jnp.sum(hidden * hidden, axis=-1, keepdims=True)
            upper = d_ref[k, at, :].astype(f32) * gain_ref[:, cut]
            cross += jnp.sum(upper * hidden, axis=-1, keepdims=True)
        scaling = lax.rsqrt(squares * (1.0 / width) + norm_eps)
        factor = scaling * scaling * scaling * (cross * (1.0 / width))
        for k in range(blocks):
            cut = slice(k * depth, (k + 1) * depth)
            upper = d_ref[k, at, :].astype(f32) * gain_ref[:, cut]
            hidden = hidden_ref[at, cut].astype(f32)
            out_ref[at, cut] = (scaling * upper - hidden * factor).astype(bf16)


def arrange_kernel(where_ref, *refs, dp, layout):
    cots, (send_ref, turned_ref) = refs[:dp], refs[dp:]
    t = where_ref[1]
    tensor = send_ref.shape[0]
    micro, rows, cols = cots[0].shape
    rows //= tensor
    piece = micro * rows
    for k in range(dp):
        for b in range(tensor):
            for m in range(micro):
                at = k * piece + m * rows
                send_ref[b, at : at + rows, :] = cots[k][m, b * rows : (b + 1) * rows, :]
    for p, (k, j) in enumerate(layout):
        at = pl.ds(pl.multiple_of((t ^ j) * rows, rows), rows)
        block = jnp.concatenate([cots[k][m, at, :] for m in range(micro)])
        turned_ref[:, p * piece : (p + 1) * piece] = block.astype(f32).T.astype(bf16)


def d_kernel(where_ref, cot_ref, *rest):
    w_refs, d_ref = rest[:4], rest[4]
    z, t = where_ref[0], where_ref[1]
    dp, rows = d_ref.shape[:2]
    half = w_refs[0].shape[0]
    tile = min(half, 512)
    cot = jnp.concatenate([cot_ref[t ^ j] for j in range(cot_ref.shape[0])], axis=1)
    for side in range(1):
        for i in range(half // tile):
            cut = slice(i * tile, (i + 1) * tile)
            whole = jnp.concatenate([w[cut, :] for w in w_refs], axis=1)
            part = dot(cot, whole, ((1,), (1,))).astype(bf16)
            for k in range(dp):
                d_ref[z ^ k, :, side * half + i * tile : side * half + (i + 1) * tile] = part[
                    k * rows : (k + 1) * rows
                ]


def pack_kernel(*refs):
    pieces, packed_ref, sem = refs[:-2], refs[-2], refs[-1]
    rows = pieces[0].shape[0]
    copies = [
        pltpu.make_async_copy(x, packed_ref.at[pl.ds(p * rows, rows), :], sem.at[p])
        for p, x in enumerate(pieces)
    ]
    for copy in copies:
        copy.start()
    for copy in copies:
        copy.wait()


def token_copies(token_refs, tokens_ref, sems, cut, first):
    copies, row = [], 0
    for p, x in enumerate(token_refs):
        rows = x.shape[0]
        copies.append(
            pltpu.make_async_copy(
                x.at[:, cut], tokens_ref.at[pl.ds(row, rows), cut], sems.at[first + p]
            )
        )
        row += rows
    return copies


def update_kernel(turned_ref, master_hbm, m_hbm, v_hbm, *rest, count, tile, layout):
    token_refs = rest[:count]
    new_hbm, part_refs = rest[count], rest[count + 1 : -8]
    tokens, master, m, v, updated, new, sems, out_sems = rest[-8:]
    depth = master.shape[0]
    tiles = depth // tile
    each = count + 3
    groups = []
    for i in range(tiles):
        cut = pl.ds(i * tile, tile)
        group = token_copies(token_refs, tokens, sems, cut, i * each)
        for p, (source, target) in enumerate(((master_hbm, master), (m_hbm, m), (v_hbm, v))):
            group.append(
                pltpu.make_async_copy(
                    source.at[cut, :], target.at[cut, :], sems.at[i * each + count + p]
                )
            )
        for copy in group:
            copy.start()
        groups.append(group)
    outs = []
    for i in range(tiles):
        cut = slice(i * tile, (i + 1) * tile)
        for copy in groups[i]:
            copy.wait()
        grad = dot(turned_ref[...], tokens[:, cut], ((1,), (0,))).T
        m_new = beta_first * m[cut, :] + (1.0 - beta_first) * grad
        v_new = beta_second * v[cut, :] + (1.0 - beta_second) * grad * grad
        m_hat = m_new / (1.0 - beta_first**step_count)
        v_hat = v_new / (1.0 - beta_second**step_count)
        old = master[cut, :]
        master_new = old - learn_rate * (
            m_hat / (jnp.sqrt(v_hat) + adam_eps) + weight_decay * old
        )
        new[cut, :] = master_new
        out = pltpu.make_async_copy(
            new.at[pl.ds(i * tile, tile), :], new_hbm.at[pl.ds(i * tile, tile), :], out_sems.at[i]
        )
        out.start()
        outs.append(out)
        updated[cut, :] = master_new.astype(bf16)
    project(tokens, updated, part_refs, layout)
    for out in outs:
        out.wait()


def project(tokens, weights, part_refs, layout):
    piece = tokens.shape[0] // len(layout)
    slot = {0: 0, 2: 1, 1: 2, 3: 3}
    p = 0
    while p < len(layout):
        k, j = layout[p]
        span = 2 if layout[p + 1 : p + 2] == ((k, j + 2),) else 1
        part_refs[k][slot[j] * piece : (slot[j] + span) * piece, :] = dot(
            tokens[p * piece : (p + span) * piece, :], weights[...], ((1,), (0,))
        ).astype(bf16)
        p += span


def project_kernel(mark_ref, weights_ref, *rest, count, layout):
    token_refs = rest[:count]
    part_refs, (tokens, sems) = rest[count:-2], rest[-2:]
    copies = token_copies(token_refs, tokens, sems, slice(None), 0)
    for copy in copies:
        copy.start()
    for copy in copies:
        copy.wait()
    project(tokens, weights_ref, part_refs, layout)


def reorder(blocks, me):
    bit = 1
    while bit < len(blocks):
        flip = (me & bit) != 0
        blocks = [jnp.where(flip, blocks[i ^ bit], blocks[i]) for i in range(len(blocks))]
        bit *= 2
    return blocks


def scatter_sum(parts, got=None):
    got1, got3 = got or (swap(parts[1], "dp", 1), swap(parts[3], "dp", 1))
    mine = parts[0].astype(f32) + got1.astype(f32)
    other = (parts[2].astype(f32) + got3.astype(f32)).astype(bf16)
    return mine + swap(other, "dp", 2).astype(f32)


def shards(hidden_in, norm_gain, kv_cot, master_kv, moment_m, moment_v):
    dp, tensor = lax.axis_size("dp"), lax.axis_size("tensor")
    assert dp == 4 and tensor == 4
    z, t = lax.axis_index("dp"), lax.axis_index("tensor")
    where = jnp.stack([z, t]).astype(jnp.int32)
    _, micro, rows, width = hidden_in.shape
    piece = micro * rows
    hidden = hidden_in.reshape(piece, width)
    own_depth, cols = master_kv.shape[1:]
    depth = width // dp
    tile = min(piece, 16)

    w0 = [master_kv[0].astype(bf16)]
    w2 = [swap(w, "tensor", 2) for w in w0]
    w1 = [swap(w, "tensor", 1) for w in w0]
    cot0 = kv_cot[0]
    cot2 = swap(cot0, "dp", 2)
    cot1 = swap(cot0, "dp", 1)
    cot3 = swap(cot2, "dp", 1)
    own = call(
        functools.partial(norm_kernel, tile=tile),
        [like(piece, depth)] * dp,
        [anywhere, anywhere, smem, vmem, vmem],
        [vmem] * dp,
        8,
        "norm",
    )(cot2, cot1, where, hidden, norm_gain)
    n1, n3 = swap(own[1], "dp", 1), swap(own[3], "dp", 3)
    w3 = [swap(w, "tensor", 1) for w in w2]
    layout = tuple((k, j) for k in (0, 1, 3, 2) for j in (0, 2, 1, 3))
    send, turned = call(
        functools.partial(arrange_kernel, dp=dp, layout=layout),
        [like(tensor, dp * piece, cols), like(cols, dp * tensor * piece)],
        [smem] + [vmem] * dp,
        [vmem] * 2,
        8,
        "arrange",
    )(where, cot0, cot1, cot2, cot3)
    own2, n3 = after([own[2], n3])
    n2 = swap(own2, "dp", 2)
    (send,) = after([send], own2)
    mine_cot = lax.all_to_all(send, "tensor", 0, 0, tiled=True)
    def pack(*pieces):
        return call(
            pack_kernel,
            like(len(pieces) * piece, depth),
            [anywhere] * len(pieces),
            anywhere,
            0.25,
            "pack",
            scratch=[pltpu.SemaphoreType.DMA((len(pieces),))],
        )(*pieces)

    tokens = []
    for x in (own[0], n1, n3):
        near = pack(x, swap(x, "tensor", 2))
        tokens += [near, swap(near, "tensor", 1)]
    d = call(
        d_kernel,
        like(dp, piece, depth),
        [smem] + [vmem] * 5,
        vmem,
        20,
        "d_normed",
    )(where, mine_cot, *w0, *w1, *w2, *w3)
    n2, d = after([n2, d], tokens[1])
    d = lax.all_to_all(d, "dp", 0, 0, tiled=True)
    across = swap(n2, "tensor", 2)
    tokens += [n2, across, swap(n2, "tensor", 1), swap(across, "tensor", 1)]
    count = len(tokens)
    block = tensor * piece
    part_shape = [like(block, cols)] * dp
    step = min(own_depth, 512)
    tiles = own_depth // step
    whole = pltpu.VMEM((own_depth, cols), f32)
    all_tokens = pltpu.VMEM((dp * block, depth), bf16)
    master_new, *parts = call(
        functools.partial(update_kernel, count=count, tile=step, layout=layout),
        [like(own_depth, cols, dtype=f32)] + part_shape,
        [vmem] + [anywhere] * (3 + count),
        [anywhere] + [vmem] * dp,
        24,
        "update",
        scratch=[
            all_tokens,
            whole,
            whole,
            whole,
            pltpu.VMEM((own_depth, cols), bf16),
            whole,
            pltpu.SemaphoreType.DMA((tiles * (count + 3),)),
            pltpu.SemaphoreType.DMA((tiles,)),
        ],
    )(turned, master_kv[0], moment_m[0], moment_v[0], *tokens)

    def place(x):
        x = x.reshape(tensor, micro, rows, cols)
        return jnp.stack(reorder([x[j] for j in (0, 2, 1, 3)], t), 1).reshape(
            1, micro, tensor * rows, cols
        )

    got1, got3 = swap(parts[1], "dp", 1), swap(parts[3], "dp", 1)
    mine = place(scatter_sum(parts, (got1, got3)).astype(bf16))
    kv_next = from_behind(mine, "segment", -1)
    own_parts = call(
        functools.partial(project_kernel, count=count, layout=layout),
        part_shape,
        [anywhere, vmem] + [anywhere] * count,
        [vmem] * dp,
        16,
        "project",
        scratch=[all_tokens, pltpu.SemaphoreType.DMA((count,))],
    )(got1, w0[0], *tokens)
    kv_own = place(scatter_sum(own_parts).astype(bf16))
    (d,) = after([d], mine, kv_own)
    grad_in = call(
        functools.partial(grad_kernel, tile=tile),
        like(piece, width),
        [vmem] * 3,
        vmem,
        12,
        "grad_in",
    )(hidden, norm_gain, d)
    return (kv_own, grad_in.reshape(hidden_in.shape), master_new[None], kv_next)


def solution(mesh):
    in_specs = (
        P("segment", None, ("dp", "tensor"), None),
        P("segment", None),
        P("segment", None, "dp", "tensor"),
        P("segment", "dp", "tensor"),
        P("segment", "dp", "tensor"),
        P("segment", "dp", "tensor"),
    )
    out_specs = (
        P("segment", None, "dp", "tensor"),
        P("segment", None, ("dp", "tensor"), None),
        P("segment", "dp", "tensor"),
        P("segment", None, "dp", "tensor"),
    )
    return jax.shard_map(shards, mesh=mesh, in_specs=in_specs, out_specs=out_specs, check_vma=False)
```

```python
import functools

import jax
import jax.numpy as jnp
from jax import lax
from jax.experimental import pallas as pl
from jax.experimental.pallas import tpu as pltpu
from jax.sharding import PartitionSpec as P

beta_first = 0.9
beta_second = 0.95
learn_rate = 0.03
weight_decay = 0.1
adam_eps = 1e-08
norm_eps = 1e-05
step_count = 20.0

f32 = jnp.float32
bf16 = jnp.bfloat16

vmem = pl.BlockSpec(memory_space=pltpu.VMEM)
smem = pl.BlockSpec(memory_space=pltpu.SMEM)
anywhere = pl.BlockSpec(memory_space=pl.ANY)
light = pl.CostEstimate(flops=1000, bytes_accessed=1000, transcendentals=0)


def swap(x, axis, bits):
    peers = lax.axis_size(axis)
    return lax.ppermute(x, axis, [(i, i ^ bits) for i in range(peers)])


def from_behind(x, axis, by):
    peers = lax.axis_size(axis)
    return lax.ppermute(x, axis, [(i, (i + by) % peers) for i in range(peers)])


def dot(a, b, contract):
    return lax.dot_general(a, b, (contract, ((), ())), preferred_element_type=f32)


def like(*shape, dtype=bf16):
    return jax.ShapeDtypeStruct(shape, dtype)


def call(body, out_shape, in_specs, out_specs, mib, name, scratch=(), **more):
    return pl.pallas_call(
        body,
        out_shape=out_shape,
        in_specs=in_specs,
        out_specs=out_specs,
        scratch_shapes=list(scratch),
        compiler_params=pltpu.CompilerParams(vmem_limit_bytes=int(mib * 1024 * 1024)),
        cost_estimate=light,
        name=name,
        **more,
    )


def after(values, *earlier):
    tied = call(
        lambda *refs: None,
        [like(*x.shape, dtype=x.dtype) for x in values],
        [anywhere] * (len(values) + len(earlier)),
        [anywhere] * len(values),
        0.25,
        "after",
        input_output_aliases={i: i for i in range(len(values))},
    )(*values, *earlier)
    return list(tied)


def lanes(index, size):
    return pl.ds(pl.multiple_of(index * size, size), size)


def norm_kernel(mark_ref, other_ref, third_ref, where_ref, hidden_ref, gain_ref, *own_refs, tile):
    z = where_ref[0]
    rows, width = hidden_ref.shape
    depth = width // len(own_refs)

    @pl.loop(0, rows // tile)
    def _(i):
        at = pl.ds(pl.multiple_of(i * tile, tile), tile)
        total = jnp.zeros((tile, 1), f32)
        for k in range(len(own_refs)):
            part = hidden_ref[at, k * depth : (k + 1) * depth].astype(f32)
            total += jnp.sum(part * part, axis=-1, keepdims=True)
        scaling = lax.rsqrt(total * (1.0 / width) + norm_eps)
        for k, own_ref in enumerate(own_refs):
            cut = lanes(z ^ k, depth)
            own_ref[at, :] = (
                hidden_ref[at, cut].astype(f32) * scaling * gain_ref[:, cut]
            ).astype(bf16)


def grad_kernel(hidden_ref, gain_ref, d_ref, out_ref, *, tile):
    rows, width = hidden_ref.shape
    blocks = d_ref.shape[0]
    depth = width // blocks

    @pl.loop(0, rows // tile)
    def _(i):
        at = pl.ds(pl.multiple_of(i * tile, tile), tile)
        squares = jnp.zeros((tile, 1), f32)
        cross = jnp.zeros((tile, 1), f32)
        for k in range(blocks):
            cut = slice(k * depth, (k + 1) * depth)
            hidden = hidden_ref[at, cut].astype(f32)
            squares += jnp.sum(hidden * hidden, axis=-1, keepdims=True)
            upper = d_ref[k, at, :].astype(f32) * gain_ref[:, cut]
            cross += jnp.sum(upper * hidden, axis=-1, keepdims=True)
        scaling = lax.rsqrt(squares * (1.0 / width) + norm_eps)
        factor = scaling * scaling * scaling * (cross * (1.0 / width))
        for k in range(blocks):
            cut = slice(k * depth, (k + 1) * depth)
            upper = d_ref[k, at, :].astype(f32) * gain_ref[:, cut]
            hidden = hidden_ref[at, cut].astype(f32)
            out_ref[at, cut] = (scaling * upper - hidden * factor).astype(bf16)


def arrange_kernel(where_ref, *refs, dp, layout):
    cots, (send_ref, turned_ref) = refs[:dp], refs[dp:]
    t = where_ref[1]
    tensor = send_ref.shape[0]
    micro, rows, cols = cots[0].shape
    rows //= tensor
    piece = micro * rows
    for k in range(dp):
        for b in range(tensor):
            for m in range(micro):
                at = k * piece + m * rows
                send_ref[b, at : at + rows, :] = cots[k][m, b * rows : (b + 1) * rows, :]
    for p, (k, j) in enumerate(layout):
        at = pl.ds(pl.multiple_of((t ^ j) * rows, rows), rows)
        block = jnp.concatenate([cots[k][m, at, :] for m in range(micro)])
        turned_ref[:, p * piece : (p + 1) * piece] = block.astype(f32).T.astype(bf16)


def d_kernel(where_ref, cot_ref, *rest):
    w_refs, d_ref = rest[:4], rest[4]
    z, t = where_ref[0], where_ref[1]
    dp, rows = d_ref.shape[:2]
    half = w_refs[0].shape[0]
    tile = min(half, 512)
    cot = jnp.concatenate([cot_ref[t ^ j] for j in range(cot_ref.shape[0])], axis=1)
    for side in range(1):
        for i in range(half // tile):
            cut = slice(i * tile, (i + 1) * tile)
            whole = jnp.concatenate([w[cut, :] for w in w_refs], axis=1)
            part = dot(cot, whole, ((1,), (1,))).astype(bf16)
            for k in range(dp):
                d_ref[z ^ k, :, side * half + i * tile : side * half + (i + 1) * tile] = part[
                    k * rows : (k + 1) * rows
                ]


def pack_kernel(*refs):
    pieces, packed_ref, sem = refs[:-2], refs[-2], refs[-1]
    rows = pieces[0].shape[0]
    copies = [
        pltpu.make_async_copy(x, packed_ref.at[pl.ds(p * rows, rows), :], sem.at[p])
        for p, x in enumerate(pieces)
    ]
    for copy in copies:
        copy.start()
    for copy in copies:
        copy.wait()


def token_copies(token_refs, tokens_ref, sems, cut, first):
    copies, row = [], 0
    for p, x in enumerate(token_refs):
        rows = x.shape[0]
        copies.append(
            pltpu.make_async_copy(
                x.at[:, cut], tokens_ref.at[pl.ds(row, rows), cut], sems.at[first + p]
            )
        )
        row += rows
    return copies


def update_kernel(turned_ref, master_hbm, m_hbm, v_hbm, *rest, count, tile, layout):
    token_refs = rest[:count]
    new_hbm, part_refs = rest[count], rest[count + 1 : -8]
    tokens, master, m, v, updated, new, sems, out_sems = rest[-8:]
    depth = master.shape[0]
    tiles = depth // tile
    each = count + 3
    groups = []
    for i in range(tiles):
        cut = pl.ds(i * tile, tile)
        group = token_copies(token_refs, tokens, sems, cut, i * each)
        for p, (source, target) in enumerate(((master_hbm, master), (m_hbm, m), (v_hbm, v))):
            group.append(
                pltpu.make_async_copy(
                    source.at[cut, :], target.at[cut, :], sems.at[i * each + count + p]
                )
            )
        for copy in group:
            copy.start()
        groups.append(group)
    outs = []
    for i in range(tiles):
        cut = slice(i * tile, (i + 1) * tile)
        for copy in groups[i]:
            copy.wait()
        grad = dot(turned_ref[...], tokens[:, cut], ((1,), (0,))).T
        m_new = beta_first * m[cut, :] + (1.0 - beta_first) * grad
        v_new = beta_second * v[cut, :] + (1.0 - beta_second) * grad * grad
        m_hat = m_new / (1.0 - beta_first**step_count)
        v_hat = v_new / (1.0 - beta_second**step_count)
        old = master[cut, :]
        master_new = old - learn_rate * (
            m_hat / (jnp.sqrt(v_hat) + adam_eps) + weight_decay * old
        )
        new[cut, :] = master_new
        out = pltpu.make_async_copy(
            new.at[pl.ds(i * tile, tile), :], new_hbm.at[pl.ds(i * tile, tile), :], out_sems.at[i]
        )
        out.start()
        outs.append(out)
        updated[cut, :] = master_new.astype(bf16)
    project(tokens, updated, part_refs, layout)
    for out in outs:
        out.wait()


def project(tokens, weights, part_refs, layout):
    piece = tokens.shape[0] // len(layout)
    slot = {0: 0, 2: 1, 1: 2, 3: 3}
    p = 0
    while p < len(layout):
        k, j = layout[p]
        span = 2 if layout[p + 1 : p + 2] == ((k, j + 2),) else 1
        part_refs[k][slot[j] * piece : (slot[j] + span) * piece, :] = dot(
            tokens[p * piece : (p + span) * piece, :], weights[...], ((1,), (0,))
        ).astype(bf16)
        p += span


def project_kernel(mark_ref, weights_ref, *rest, count, layout):
    token_refs = rest[:count]
    part_refs, (tokens, sems) = rest[count:-2], rest[-2:]
    copies = token_copies(token_refs, tokens, sems, slice(None), 0)
    for copy in copies:
        copy.start()
    for copy in copies:
        copy.wait()
    project(tokens, weights_ref, part_refs, layout)


def reorder(blocks, me):
    bit = 1
    while bit < len(blocks):
        flip = (me & bit) != 0
        blocks = [jnp.where(flip, blocks[i ^ bit], blocks[i]) for i in range(len(blocks))]
        bit *= 2
    return blocks


def scatter_sum(parts, got1, got3, *earlier):
    mine = parts[0].astype(f32) + got1.astype(f32)
    other = (parts[2].astype(f32) + got3.astype(f32)).astype(bf16)
    got = swap(other, "dp", 2)
    if earlier:
        got = after([got], *earlier)[0]
    return mine + got.astype(f32), other


def shards(hidden_in, norm_gain, kv_cot, master_kv, moment_m, moment_v):
    dp, tensor = lax.axis_size("dp"), lax.axis_size("tensor")
    assert dp == 4 and tensor == 4
    z, t = lax.axis_index("dp"), lax.axis_index("tensor")
    where = jnp.stack([z, t]).astype(jnp.int32)
    _, micro, rows, width = hidden_in.shape
    piece = micro * rows
    hidden = hidden_in.reshape(piece, width)
    own_depth, cols = master_kv.shape[1:]
    depth = width // dp
    tile = min(piece, 16)

    w0 = [master_kv[0].astype(bf16)]
    w2 = [swap(w, "tensor", 2) for w in w0]
    w1 = [swap(w, "tensor", 1) for w in w0]
    cot0 = kv_cot[0]
    cot2 = swap(cot0, "dp", 2)
    cot1 = swap(cot0, "dp", 1)
    cot3 = swap(cot2, "dp", 1)
    own = call(
        functools.partial(norm_kernel, tile=tile),
        [like(piece, depth)] * dp,
        [anywhere] * 3 + [smem, vmem, vmem],
        [vmem] * dp,
        8,
        "norm",
    )(cot2, cot1, w1[0], where, hidden, norm_gain)
    n1, n3 = swap(own[1], "dp", 1), swap(own[3], "dp", 3)
    w3 = [swap(w, "tensor", 1) for w in w2]
    layout = tuple((k, j) for k in (0, 1, 3, 2) for j in (0, 2, 1, 3))
    send, turned = call(
        functools.partial(arrange_kernel, dp=dp, layout=layout),
        [like(tensor, dp * piece, cols), like(cols, dp * tensor * piece)],
        [smem] + [vmem] * dp,
        [vmem] * 2,
        8,
        "arrange",
    )(where, cot0, cot1, cot2, cot3)
    own2, n3 = after([own[2], n3])
    n2 = swap(own2, "dp", 2)
    (send,) = after([send], own2)
    mine_cot = lax.all_to_all(send, "tensor", 0, 0, tiled=True)
    def pack(*pieces):
        return call(
            pack_kernel,
            like(len(pieces) * piece, depth),
            [anywhere] * len(pieces),
            anywhere,
            0.25,
            "pack",
            scratch=[pltpu.SemaphoreType.DMA((len(pieces),))],
        )(*pieces)

    tokens = []
    for x in (own[0], n1, n3):
        near = pack(x, swap(x, "tensor", 2))
        tokens += [near, swap(near, "tensor", 1)]
    d = call(
        d_kernel,
        like(dp, piece, depth),
        [smem] + [vmem] * 5,
        vmem,
        20,
        "d_normed",
    )(where, mine_cot, *w0, *w1, *w2, *w3)
    n2, d = after([n2, d], tokens[1])
    d = lax.all_to_all(d, "dp", 0, 0, tiled=True)
    across = swap(n2, "tensor", 2)
    tokens += [n2, across, swap(n2, "tensor", 1), swap(across, "tensor", 1)]
    count = len(tokens)
    block = tensor * piece
    part_shape = [like(block, cols)] * dp
    step = min(own_depth, 512)
    tiles = own_depth // step
    whole = pltpu.VMEM((own_depth, cols), f32)
    all_tokens = pltpu.VMEM((dp * block, depth), bf16)
    master_new, *parts = call(
        functools.partial(update_kernel, count=count, tile=step, layout=layout),
        [like(own_depth, cols, dtype=f32)] + part_shape,
        [vmem] + [anywhere] * (3 + count),
        [anywhere] + [vmem] * dp,
        24,
        "update",
        scratch=[
            all_tokens,
            whole,
            whole,
            whole,
            pltpu.VMEM((own_depth, cols), bf16),
            whole,
            pltpu.SemaphoreType.DMA((tiles * (count + 3),)),
            pltpu.SemaphoreType.DMA((tiles,)),
        ],
    )(turned, master_kv[0], moment_m[0], moment_v[0], *tokens)

    def place(x):
        x = x.reshape(tensor, micro, rows, cols)
        return jnp.stack(reorder([x[j] for j in (0, 2, 1, 3)], t), 1).reshape(
            1, micro, tensor * rows, cols
        )

    got1, got3 = swap(parts[1], "dp", 1), swap(parts[3], "dp", 1)
    got1, got3 = after([got1, got3])
    mine, _ = scatter_sum(parts, got1, got3)
    mine = place(mine.astype(bf16))
    kv_next = from_behind(mine, "segment", -1)
    own_parts = call(
        functools.partial(project_kernel, count=count, layout=layout),
        part_shape,
        [anywhere, vmem] + [anywhere] * count,
        [vmem] * dp,
        16,
        "project",
        scratch=[all_tokens, pltpu.SemaphoreType.DMA((count,))],
    )(parts[1], w0[0], *tokens)
    (d,) = after([d], mine)
    grad_in = call(
        functools.partial(grad_kernel, tile=tile),
        like(piece, width),
        [vmem] * 3,
        vmem,
        12,
        "grad_in",
    )(hidden, norm_gain, d)
    own_got = after([swap(own_parts[1], "dp", 1), swap(own_parts[3], "dp", 1)])
    kv_own, _ = scatter_sum(own_parts, *own_got, grad_in[:16, :128])
    kv_own = place(kv_own.astype(bf16))
    return (kv_own, grad_in.reshape(hidden_in.shape), master_new[None], kv_next)


def solution(mesh):
    in_specs = (
        P("segment", None, ("dp", "tensor"), None),
        P("segment", None),
        P("segment", None, "dp", "tensor"),
        P("segment", "dp", "tensor"),
        P("segment", "dp", "tensor"),
        P("segment", "dp", "tensor"),
    )
    out_specs = (
        P("segment", None, "dp", "tensor"),
        P("segment", None, ("dp", "tensor"), None),
        P("segment", "dp", "tensor"),
        P("segment", None, "dp", "tensor"),
    )
    return jax.shard_map(shards, mesh=mesh, in_specs=in_specs, out_specs=out_specs, check_vma=False)
```

```python
import functools

import jax
import jax.numpy as jnp
from jax import lax
from jax.experimental import pallas as pl
from jax.experimental.pallas import tpu as pltpu
from jax.sharding import PartitionSpec as P

beta_first = 0.9
beta_second = 0.95
learn_rate = 0.03
weight_decay = 0.1
adam_eps = 1e-08
norm_eps = 1e-05
step_count = 20.0

f32 = jnp.float32
bf16 = jnp.bfloat16

vmem = pl.BlockSpec(memory_space=pltpu.VMEM)
smem = pl.BlockSpec(memory_space=pltpu.SMEM)
anywhere = pl.BlockSpec(memory_space=pl.ANY)
light = pl.CostEstimate(flops=1000, bytes_accessed=1000, transcendentals=0)


def swap(x, axis, bits):
    peers = lax.axis_size(axis)
    return lax.ppermute(x, axis, [(i, i ^ bits) for i in range(peers)])


def from_behind(x, axis, by):
    peers = lax.axis_size(axis)
    return lax.ppermute(x, axis, [(i, (i + by) % peers) for i in range(peers)])


def dot(a, b, contract):
    return lax.dot_general(a, b, (contract, ((), ())), preferred_element_type=f32)


def like(*shape, dtype=bf16):
    return jax.ShapeDtypeStruct(shape, dtype)


def call(body, out_shape, in_specs, out_specs, mib, name, scratch=(), **more):
    return pl.pallas_call(
        body,
        out_shape=out_shape,
        in_specs=in_specs,
        out_specs=out_specs,
        scratch_shapes=list(scratch),
        compiler_params=pltpu.CompilerParams(vmem_limit_bytes=int(mib * 1024 * 1024)),
        cost_estimate=light,
        name=name,
        **more,
    )


def after(values, *earlier):
    tied = call(
        lambda *refs: None,
        [like(*x.shape, dtype=x.dtype) for x in values],
        [anywhere] * (len(values) + len(earlier)),
        [anywhere] * len(values),
        0.25,
        "after",
        input_output_aliases={i: i for i in range(len(values))},
    )(*values, *earlier)
    return list(tied)


def lanes(index, size):
    return pl.ds(pl.multiple_of(index * size, size), size)


def norm_kernel(mark_ref, other_ref, third_ref, where_ref, hidden_ref, gain_ref, *own_refs, tile):
    z = where_ref[0]
    rows, width = hidden_ref.shape
    depth = width // len(own_refs)

    @pl.loop(0, rows // tile)
    def _(i):
        at = pl.ds(pl.multiple_of(i * tile, tile), tile)
        total = jnp.zeros((tile, 1), f32)
        for k in range(len(own_refs)):
            part = hidden_ref[at, k * depth : (k + 1) * depth].astype(f32)
            total += jnp.sum(part * part, axis=-1, keepdims=True)
        scaling = lax.rsqrt(total * (1.0 / width) + norm_eps)
        for k, own_ref in enumerate(own_refs):
            cut = lanes(z ^ k, depth)
            own_ref[at, :] = (
                hidden_ref[at, cut].astype(f32) * scaling * gain_ref[:, cut]
            ).astype(bf16)


def grad_kernel(hidden_ref, gain_ref, d_ref, out_ref, *, tile):
    rows, width = hidden_ref.shape
    blocks = d_ref.shape[0]
    depth = width // blocks

    @pl.loop(0, rows // tile)
    def _(i):
        at = pl.ds(pl.multiple_of(i * tile, tile), tile)
        squares = jnp.zeros((tile, 1), f32)
        cross = jnp.zeros((tile, 1), f32)
        for k in range(blocks):
            cut = slice(k * depth, (k + 1) * depth)
            hidden = hidden_ref[at, cut].astype(f32)
            squares += jnp.sum(hidden * hidden, axis=-1, keepdims=True)
            upper = d_ref[k, at, :].astype(f32) * gain_ref[:, cut]
            cross += jnp.sum(upper * hidden, axis=-1, keepdims=True)
        scaling = lax.rsqrt(squares * (1.0 / width) + norm_eps)
        factor = scaling * scaling * scaling * (cross * (1.0 / width))
        for k in range(blocks):
            cut = slice(k * depth, (k + 1) * depth)
            upper = d_ref[k, at, :].astype(f32) * gain_ref[:, cut]
            hidden = hidden_ref[at, cut].astype(f32)
            out_ref[at, cut] = (scaling * upper - hidden * factor).astype(bf16)


def arrange_kernel(where_ref, *refs, dp, layout):
    cots, (send_ref, turned_ref) = refs[:dp], refs[dp:]
    t = where_ref[1]
    tensor = send_ref.shape[0]
    micro, rows, cols = cots[0].shape
    rows //= tensor
    piece = micro * rows
    for k in range(dp):
        for b in range(tensor):
            for m in range(micro):
                at = k * piece + m * rows
                send_ref[b, at : at + rows, :] = cots[k][m, b * rows : (b + 1) * rows, :]
    for p, (k, j) in enumerate(layout):
        at = pl.ds(pl.multiple_of((t ^ j) * rows, rows), rows)
        block = jnp.concatenate([cots[k][m, at, :] for m in range(micro)])
        turned_ref[:, p * piece : (p + 1) * piece] = block.astype(f32).T.astype(bf16)


def d_kernel(where_ref, cot_ref, *rest):
    w_refs, d_ref = rest[:4], rest[4]
    z, t = where_ref[0], where_ref[1]
    dp, rows = d_ref.shape[:2]
    half = w_refs[0].shape[0]
    tile = min(half, 512)
    cot = jnp.concatenate([cot_ref[t ^ j] for j in range(cot_ref.shape[0])], axis=1)
    for side in range(1):
        for i in range(half // tile):
            cut = slice(i * tile, (i + 1) * tile)
            whole = jnp.concatenate([w[cut, :] for w in w_refs], axis=1)
            part = dot(cot, whole, ((1,), (1,))).astype(bf16)
            for k in range(dp):
                d_ref[z ^ k, :, side * half + i * tile : side * half + (i + 1) * tile] = part[
                    k * rows : (k + 1) * rows
                ]


def pack_kernel(*refs):
    pieces, packed_ref, sem = refs[:-2], refs[-2], refs[-1]
    rows = pieces[0].shape[0]
    copies = [
        pltpu.make_async_copy(x, packed_ref.at[pl.ds(p * rows, rows), :], sem.at[p])
        for p, x in enumerate(pieces)
    ]
    for copy in copies:
        copy.start()
    for copy in copies:
        copy.wait()


def token_copies(token_refs, tokens_ref, sems, cut, first):
    copies, row = [], 0
    for p, x in enumerate(token_refs):
        rows = x.shape[0]
        copies.append(
            pltpu.make_async_copy(
                x.at[:, cut], tokens_ref.at[pl.ds(row, rows), cut], sems.at[first + p]
            )
        )
        row += rows
    return copies


def update_kernel(turned_ref, master_hbm, m_hbm, v_hbm, *rest, count, tile, layout):
    token_refs = rest[:count]
    new_hbm, part_refs = rest[count], rest[count + 1 : -8]
    tokens, master, m, v, updated, new, sems, out_sems = rest[-8:]
    depth = master.shape[0]
    tiles = depth // tile
    each = count + 3
    groups = []
    for i in range(tiles):
        cut = pl.ds(i * tile, tile)
        group = token_copies(token_refs, tokens, sems, cut, i * each)
        for p, (source, target) in enumerate(((master_hbm, master), (m_hbm, m), (v_hbm, v))):
            group.append(
                pltpu.make_async_copy(
                    source.at[cut, :], target.at[cut, :], sems.at[i * each + count + p]
                )
            )
        for copy in group:
            copy.start()
        groups.append(group)
    outs = []
    for i in range(tiles):
        cut = slice(i * tile, (i + 1) * tile)
        for copy in groups[i]:
            copy.wait()
        grad = dot(turned_ref[...], tokens[:, cut], ((1,), (0,))).T
        m_new = beta_first * m[cut, :] + (1.0 - beta_first) * grad
        v_new = beta_second * v[cut, :] + (1.0 - beta_second) * grad * grad
        m_hat = m_new / (1.0 - beta_first**step_count)
        v_hat = v_new / (1.0 - beta_second**step_count)
        old = master[cut, :]
        master_new = old - learn_rate * (
            m_hat / (jnp.sqrt(v_hat) + adam_eps) + weight_decay * old
        )
        new[cut, :] = master_new
        out = pltpu.make_async_copy(
            new.at[pl.ds(i * tile, tile), :], new_hbm.at[pl.ds(i * tile, tile), :], out_sems.at[i]
        )
        out.start()
        outs.append(out)
        updated[cut, :] = master_new.astype(bf16)
    project(tokens, updated, part_refs, layout)
    for out in outs:
        out.wait()


def project(tokens, weights, part_refs, layout):
    piece = tokens.shape[0] // len(layout)
    slot = {0: 0, 2: 1, 1: 2, 3: 3}
    p = 0
    while p < len(layout):
        k, j = layout[p]
        span = 2 if layout[p + 1 : p + 2] == ((k, j + 2),) else 1
        part_refs[k][slot[j] * piece : (slot[j] + span) * piece, :] = dot(
            tokens[p * piece : (p + span) * piece, :], weights[...], ((1,), (0,))
        ).astype(bf16)
        p += span


def project_kernel(mark_ref, weights_ref, *rest, count, layout):
    token_refs = rest[:count]
    part_refs, (tokens, sems) = rest[count:-2], rest[-2:]
    copies = token_copies(token_refs, tokens, sems, slice(None), 0)
    for copy in copies:
        copy.start()
    for copy in copies:
        copy.wait()
    project(tokens, weights_ref, part_refs, layout)


def reorder(blocks, me):
    bit = 1
    while bit < len(blocks):
        flip = (me & bit) != 0
        blocks = [jnp.where(flip, blocks[i ^ bit], blocks[i]) for i in range(len(blocks))]
        bit *= 2
    return blocks


def scatter_sum(parts, got1, got3, *earlier):
    mine = parts[0].astype(f32) + got1.astype(f32)
    other = (parts[2].astype(f32) + got3.astype(f32)).astype(bf16)
    got = swap(other, "dp", 2)
    if earlier:
        got = after([got], *earlier)[0]
    return mine + got.astype(f32)


def shards(hidden_in, norm_gain, kv_cot, master_kv, moment_m, moment_v):
    dp, tensor = lax.axis_size("dp"), lax.axis_size("tensor")
    assert dp == 4 and tensor == 4
    z, t = lax.axis_index("dp"), lax.axis_index("tensor")
    where = jnp.stack([z, t]).astype(jnp.int32)
    _, micro, rows, width = hidden_in.shape
    piece = micro * rows
    hidden = hidden_in.reshape(piece, width)
    own_depth, cols = master_kv.shape[1:]
    depth = width // dp
    tile = min(piece, 16)

    w0 = [master_kv[0].astype(bf16)]
    w2 = [swap(w, "tensor", 2) for w in w0]
    w1 = [swap(w, "tensor", 1) for w in w0]
    cot0 = kv_cot[0]
    cot2 = swap(cot0, "dp", 2)
    cot1 = swap(cot0, "dp", 1)
    cot3 = swap(cot2, "dp", 1)
    own = call(
        functools.partial(norm_kernel, tile=tile),
        [like(piece, depth)] * dp,
        [anywhere] * 3 + [smem, vmem, vmem],
        [vmem] * dp,
        8,
        "norm",
    )(cot2, cot1, w1[0], where, hidden, norm_gain)
    n1, n3 = swap(own[1], "dp", 1), swap(own[3], "dp", 3)
    w3 = [swap(w, "tensor", 1) for w in w2]
    layout = tuple((k, j) for k in (0, 1, 3, 2) for j in (0, 2, 1, 3))
    send, turned = call(
        functools.partial(arrange_kernel, dp=dp, layout=layout),
        [like(tensor, dp * piece, cols), like(cols, dp * tensor * piece)],
        [smem] + [vmem] * dp,
        [vmem] * 2,
        8,
        "arrange",
    )(where, cot0, cot1, cot2, cot3)
    own2, n3 = after([own[2], n3])
    n2 = swap(own2, "dp", 2)
    (send,) = after([send], own2)
    mine_cot = lax.all_to_all(send, "tensor", 0, 0, tiled=True)
    def pack(*pieces):
        return call(
            pack_kernel,
            like(len(pieces) * piece, depth),
            [anywhere] * len(pieces),
            anywhere,
            0.25,
            "pack",
            scratch=[pltpu.SemaphoreType.DMA((len(pieces),))],
        )(*pieces)

    tokens = []
    for x in (own[0], n1, n3):
        near = pack(x, swap(x, "tensor", 2))
        tokens += [near, swap(near, "tensor", 1)]
    d = call(
        d_kernel,
        like(dp, piece, depth),
        [smem] + [vmem] * 5,
        vmem,
        20,
        "d_normed",
    )(where, mine_cot, *w0, *w1, *w2, *w3)
    n2, d = after([n2, d], tokens[1])
    d = lax.all_to_all(d, "dp", 0, 0, tiled=True)
    across = swap(n2, "tensor", 2)
    tokens += [n2, across, swap(n2, "tensor", 1), swap(across, "tensor", 1)]
    count = len(tokens)
    block = tensor * piece
    part_shape = [like(block, cols)] * dp
    step = min(own_depth, 512)
    tiles = own_depth // step
    whole = pltpu.VMEM((own_depth, cols), f32)
    all_tokens = pltpu.VMEM((dp * block, depth), bf16)
    master_new, *parts = call(
        functools.partial(update_kernel, count=count, tile=step, layout=layout),
        [like(own_depth, cols, dtype=f32)] + part_shape,
        [vmem] + [anywhere] * (3 + count),
        [anywhere] + [vmem] * dp,
        24,
        "update",
        scratch=[
            all_tokens,
            whole,
            whole,
            whole,
            pltpu.VMEM((own_depth, cols), bf16),
            whole,
            pltpu.SemaphoreType.DMA((tiles * (count + 3),)),
            pltpu.SemaphoreType.DMA((tiles,)),
        ],
    )(turned, master_kv[0], moment_m[0], moment_v[0], *tokens)

    def place(x):
        x = x.reshape(tensor, micro, rows, cols)
        return jnp.stack(reorder([x[j] for j in (0, 2, 1, 3)], t), 1).reshape(
            1, micro, tensor * rows, cols
        )

    got1, got3 = swap(parts[1], "dp", 1), swap(parts[3], "dp", 1)
    mine = place(scatter_sum(parts, got1, got3).astype(bf16))
    kv_next = from_behind(mine, "segment", -1)
    own_parts = call(
        functools.partial(project_kernel, count=count, layout=layout),
        part_shape,
        [anywhere, vmem] + [anywhere] * count,
        [vmem] * dp,
        16,
        "project",
        scratch=[all_tokens, pltpu.SemaphoreType.DMA((count,))],
    )(got1, w0[0], *tokens)
    (d,) = after([d], mine)
    grad_in = call(
        functools.partial(grad_kernel, tile=tile),
        like(piece, width),
        [vmem] * 3,
        vmem,
        12,
        "grad_in",
    )(hidden, norm_gain, d)
    own_got = after([swap(own_parts[1], "dp", 1), swap(own_parts[3], "dp", 1)])
    kv_own = place(scatter_sum(own_parts, *own_got, grad_in[:16, :128]).astype(bf16))
    return (kv_own, grad_in.reshape(hidden_in.shape), master_new[None], kv_next)


def solution(mesh):
    in_specs = (
        P("segment", None, ("dp", "tensor"), None),
        P("segment", None),
        P("segment", None, "dp", "tensor"),
        P("segment", "dp", "tensor"),
        P("segment", "dp", "tensor"),
        P("segment", "dp", "tensor"),
    )
    out_specs = (
        P("segment", None, "dp", "tensor"),
        P("segment", None, ("dp", "tensor"), None),
        P("segment", "dp", "tensor"),
        P("segment", None, "dp", "tensor"),
    )
    return jax.shard_map(shards, mesh=mesh, in_specs=in_specs, out_specs=out_specs, check_vma=False)
```
